128 devices in a mesh: dp: 16 (over x, y_lo, core), tensor: 8 (over y_hi, z).
Axes of the slice: x: 4, y: 4 (y_hi: 2, y_lo: 2; y = y_hi * 2 + y_lo), z: 4, core: 2. Of those that a mesh axis runs over, the one named last changes fastest.
Arguments:
- layer_input: bfloat16 [16384, 1024], P(('dp', 'tensor')), may hold values from -6 to 6
- seq_lengths: int32 [16, 4], P('dp'), may hold values from 1 to 1021, as said below
- attn_gain: bfloat16 [1024], P('dp'), may hold values from 0.099609375 to 1.8984375
- w_query: bfloat16 [1024, 2048], P('dp', 'tensor'), may hold values from -0.1875 to 0.1875
- key_projection: bfloat16 [1024, 1024], P('dp', 'tensor'), may hold values from -0.1875 to 0.1875
- value_projection: bfloat16 [1024, 1024], P('dp', 'tensor'), may hold values from -0.1875 to 0.1875
- query_gain: bfloat16 [128], replicated, may hold values from 0.25 to 1.75
- key_gain: bfloat16 [128], replicated, may hold values from 0.25 to 1.75
- w_out: bfloat16 [2048, 1024], P('tensor', 'dp'), may hold values from -1 to 1
- mlp_gain: bfloat16 [1024], P('dp'), may hold values from 0.099609375 to 1.8984375
- w_gate: bfloat16 [1024, 3072], P('dp', 'tensor'), may hold values from -0.1875 to 0.1875
- w_up: bfloat16 [1024, 3072], P('dp', 'tensor'), may hold values from -0.1875 to 0.1875
- w_down: bfloat16 [3072, 1024], P('tensor', 'dp'), may hold values from -0.109375 to 0.109375
- out_grad: bfloat16 [16384, 1024], P(('dp', 'tensor')), may hold values from -6 to 6
Outputs:
- layer_output: bfloat16 [16384, 1024], P(('dp', 'tensor'))
- input_grad: bfloat16 [16384, 1024], P(('dp', 'tensor'))
- grad_attn_gain: float32 [1024], P('dp')
- grad_query_w: float32 [1024, 2048], P('dp', 'tensor')
- grad_key_w: float32 [1024, 1024], P('dp', 'tensor')
- grad_value_w: float32 [1024, 1024], P('dp', 'tensor')
- grad_query_gain: float32 [128], replicated
- grad_key_gain: float32 [128], replicated
- grad_out_w: float32 [2048, 1024], P('tensor', 'dp')
- grad_mlp_gain: float32 [1024], P('dp')
- grad_gate_w: float32 [1024, 3072], P('dp', 'tensor')
- grad_up_w: float32 [1024, 3072], P('dp', 'tensor')
- grad_down_w: float32 [3072, 1024], P('tensor', 'dp')
The draws below stay inside these ranges and needn't reach their ends.
Inputs may be any that keep to these rules, and one draw needn't show every extreme that they name: `seq_lengths`: row r lists the lengths of the 4 documents packed in order into the 1024 tokens of dp index r and sums to 1024. In every row one document, which one drawn, begins among the first 128 of those tokens and ends among the last 128; every other one has at most (127) // 3 tokens.
All inputs are finite; a program needn't handle non-finite values.
Results may differ from the reference program's by a relative error of at most 0.025.
Values may be sent and summed in bfloat16 or wider, within the bound.
A program may use at most 128 MiB of HBM per device.

```python
import jax
import jax.numpy as jnp
from jax import lax

MODEL_WIDTH = 1024
QUERY_HEADS = 16
KEY_VALUE_HEADS = 8
HEAD_SIZE = 128
FF = 3072
TOK_DEV = 128
SEQS = 4
GROUP_TOKENS = 1024
TOKEN_TOTAL = 16384
QBLK = 512
N_DP = 16
N_TENSOR = 8


def draw_seq_lengths(key, part):
    key = jax.random.fold_in(key, 7)
    first, second = jax.random.split(key)
    longest_other = (TOK_DEV - 1) // (SEQS - 1)
    others = jax.random.randint(first, (N_DP, SEQS), 1, longest_other + 1)
    chosen = jax.random.randint(second, (N_DP, 1), 0, SEQS)
    columns = jnp.arange(SEQS)[None, :]
    others = jnp.where(columns == chosen, 0, others)
    longest = TOK_DEV * N_TENSOR - jnp.sum(others, axis=1, keepdims=True)
    return jnp.where(columns == chosen, longest, others).astype(jnp.int32)


def block_scale(own_key, dims, cuts, low, high):
    def one(dim, shards_of):
        heights = jax.random.uniform(jax.random.fold_in(jax.random.fold_in(own_key, 6), dim), (shards_of,), jnp.float32, low / len(cuts), high / len(cuts))
        return jnp.repeat(jnp.exp(heights), dims[dim] // shards_of).reshape((-1,) + (1,) * (len(dims) - dim - 1))

    level = one(*cuts[0])
    for cut in cuts[1:]:
        level = level * one(*cut)
    return level


def normal_values(own_key, dims, deviation, most, pieces=(), kind=jnp.bfloat16):
    factor_of = block_scale(own_key, dims, pieces, -0.22, 0.18) if pieces else 1.0
    array = jax.random.normal(own_key, dims, jnp.float32) * deviation * factor_of
    return jnp.minimum(jnp.maximum(array, -most), most).astype(kind)


def setup_inputs(seed: int = 0) -> dict:
    key_list = jax.random.split(jax.random.key(seed), 15)
    layer_input = normal_values(key_list[0], (TOKEN_TOTAL, MODEL_WIDTH), 1.0, 6.0, ((0, 128),))
    seq_lengths = draw_seq_lengths(jax.random.fold_in(key_list[14], 71), 0)
    attn_gain = jnp.clip(1.0 + 0.18 * jax.random.normal(key_list[2], (MODEL_WIDTH,), jnp.float32), 0.099609375, 1.8984375).astype(jnp.bfloat16)
    w_query = normal_values(key_list[3], (MODEL_WIDTH, QUERY_HEADS * HEAD_SIZE), MODEL_WIDTH ** -0.5, 0.1875, ((0, 16), (1, 8)))
    key_projection = normal_values(key_list[4], (MODEL_WIDTH, KEY_VALUE_HEADS * HEAD_SIZE), MODEL_WIDTH ** -0.5, 0.1875, ((0, 16), (1, 8)))
    value_projection = normal_values(key_list[5], (MODEL_WIDTH, KEY_VALUE_HEADS * HEAD_SIZE), MODEL_WIDTH ** -0.5, 0.1875, ((0, 16), (1, 8)))
    query_gain = jnp.clip(1.0 + 0.15 * jax.random.normal(key_list[6], (HEAD_SIZE,), jnp.float32), 0.25, 1.75).astype(jnp.bfloat16)
    key_gain = jnp.clip(1.0 + 0.15 * jax.random.normal(key_list[7], (HEAD_SIZE,), jnp.float32), 0.25, 1.75).astype(jnp.bfloat16)
    w_out = normal_values(key_list[8], (QUERY_HEADS * HEAD_SIZE, MODEL_WIDTH), (QUERY_HEADS * HEAD_SIZE // 64) ** -0.5, 1.0, ((0, 8), (1, 16)))
    mlp_gain = jnp.clip(1.0 + 0.18 * jax.random.normal(key_list[9], (MODEL_WIDTH,), jnp.float32), 0.099609375, 1.8984375).astype(jnp.bfloat16)
    w_gate = normal_values(key_list[10], (MODEL_WIDTH, FF), MODEL_WIDTH ** -0.5, 0.1875, ((0, 16), (1, 8)))
    w_up = normal_values(key_list[11], (MODEL_WIDTH, FF), MODEL_WIDTH ** -0.5, 0.1875, ((0, 16), (1, 8)))
    w_down = normal_values(key_list[12], (FF, MODEL_WIDTH), FF ** -0.5, 0.109375, ((0, 8), (1, 16)))
    out_grad = normal_values(key_list[13], (TOKEN_TOTAL, MODEL_WIDTH), 1.0, 6.0, ((0, 128),))
    return dict(layer_input=layer_input, seq_lengths=seq_lengths, attn_gain=attn_gain, w_query=w_query, key_projection=key_projection, value_projection=value_projection, query_gain=query_gain, key_gain=key_gain, w_out=w_out, mlp_gain=mlp_gain, w_gate=w_gate, w_up=w_up, w_down=w_down, out_grad=out_grad)


eps_norm = 1e-06
rope_base = 1000000.0
masked_score = -1e+30

@jax.custom_vjp
def lowered_value(v):
    return lax.optimization_barrier(v.astype(jnp.bfloat16)).astype(jnp.float32)

@jax.custom_vjp
def lowered_backward(v):
    return v

def low_keep(v):
    return (lowered_value(v), None)

def low_pass(kept, grad):
    return (grad,)

def back_keep(v):
    return (v, None)

def back_low(kept, grad):
    return (lowered_value(grad),)
lowered_value.defvjp(low_keep, low_pass)
lowered_backward.defvjp(back_keep, back_low)

def rms_scale(values, gain_in):
    return values * lax.rsqrt(lax.optimization_barrier(jnp.mean(values * values, axis=-1, keepdims=True)) + eps_norm) * gain_in

def rotate(values, cosine, sine_table):
    half_width = values.shape[-1] // 2
    turned = jnp.concatenate([-values[..., half_width:], values[..., :half_width]], axis=-1)
    return values * cosine + turned * sine_table

def tables(positions, head_width):
    frequency = rope_base ** (-(jnp.arange(head_width // 2).astype(jnp.float32) * 2.0 / head_width))
    angles = positions.astype(jnp.float32)[:, None] * frequency[None, :]
    cosine = jnp.concatenate([jnp.cos(angles), jnp.cos(angles)], axis=-1)
    sine_table = jnp.concatenate([jnp.sin(angles), jnp.sin(angles)], axis=-1)
    return (cosine[:, None, :], sine_table[:, None, :])

def layout(lengths, row_count):
    lengths = lengths.astype(jnp.int32)
    doc_ends = jnp.cumsum(lengths).astype(jnp.int32)
    doc_starts = (doc_ends - lengths).astype(jnp.int32)
    row_position = jnp.arange(row_count, dtype=jnp.int32)
    document_labels = lax.optimization_barrier(jnp.sum((row_position[:, None] >= doc_ends[None, :]).astype(jnp.int32), axis=1)).astype(jnp.int32)
    chosen = document_labels[:, None] == jnp.arange(lengths.shape[0], dtype=jnp.int32)[None, :]
    offsets = lax.optimization_barrier(jnp.sum(jnp.where(chosen, doc_starts[None, :], 0), axis=1)).astype(jnp.int32)
    return (document_labels, (row_position - offsets).astype(jnp.int32), row_position)

def attend_block(query_tile_rows, doc_block, index_block, key_rotated, value_row_matrix, doc_keys, index_keys):
    reshaped_rows = query_tile_rows.reshape(query_tile_rows.shape[0], KEY_VALUE_HEADS, QUERY_HEADS // KEY_VALUE_HEADS, HEAD_SIZE)
    scores = jnp.einsum('qgrd,kgd->grqk', reshaped_rows, key_rotated, precision=lax.Precision.HIGHEST) * HEAD_SIZE ** (-0.5)
    scores = lowered_backward(scores)
    allowed = (doc_block[:, None] == doc_keys[None, :]) & (index_keys[None, :] <= index_block[:, None])
    scores = jnp.where(allowed[None, None], scores, masked_score)
    weights = lowered_value(jax.nn.softmax(scores, axis=-1))
    mixed_heads = jnp.einsum('grqk,kgd->qgrd', weights, value_row_matrix, precision=lax.Precision.HIGHEST)
    return mixed_heads.reshape(query_tile_rows.shape[0], QUERY_HEADS * HEAD_SIZE)

def reference(layer_input, seq_lengths, attn_gain, w_query, key_projection, value_projection, query_gain, key_gain, w_out, mlp_gain, w_gate, w_up, w_down, out_grad):
    document_labels, positions, row_position = jax.vmap(lambda lengths: layout(lengths, GROUP_TOKENS))(seq_lengths)
    cosine, sine_table = tables(positions.reshape(TOKEN_TOTAL), HEAD_SIZE)
    highest_precision = lax.Precision.HIGHEST
    count_blocks = GROUP_TOKENS // QBLK

    def attend_token_group(group_item):
        queries, key_rotated, value_row_matrix, group_docs, group_index = group_item

        def one_block(block_item):
            return attend_block(block_item[0], block_item[1], block_item[2], key_rotated, value_row_matrix, group_docs, group_index)
        mixed_heads = lax.map(jax.checkpoint(one_block), (queries.reshape(count_blocks, QBLK, QUERY_HEADS, HEAD_SIZE), group_docs.reshape(count_blocks, QBLK), group_index.reshape(count_blocks, QBLK)))
        return mixed_heads.reshape(GROUP_TOKENS, QUERY_HEADS * HEAD_SIZE)

    def forward(input_full, gain_one, query_w, key_matrix, value_matrix, query_g, key_g, out_w, gain_two, gate_w, up_w, down_w):
        first_normalized = lowered_value(rms_scale(input_full, gain_one))
        query_pre = lowered_backward(jnp.dot(first_normalized, query_w, precision=highest_precision)).reshape(TOKEN_TOTAL, QUERY_HEADS, HEAD_SIZE)
        key_before_rotary = lowered_backward(jnp.dot(first_normalized, key_matrix, precision=highest_precision)).reshape(TOKEN_TOTAL, KEY_VALUE_HEADS, HEAD_SIZE)
        value_row_matrix = lowered_value(lowered_backward(jnp.dot(first_normalized, value_matrix, precision=highest_precision))).reshape(TOKEN_TOTAL, KEY_VALUE_HEADS, HEAD_SIZE)
        query_rotated = lowered_value(lowered_backward(rotate(rms_scale(query_pre, query_g), cosine, sine_table)))
        key_rotated = lowered_value(lowered_backward(rotate(rms_scale(key_before_rotary, key_g), cosine, sine_table)))
        mixed_heads = lax.map(attend_token_group, (query_rotated.reshape(N_DP, GROUP_TOKENS, QUERY_HEADS, HEAD_SIZE), key_rotated.reshape(N_DP, GROUP_TOKENS, KEY_VALUE_HEADS, HEAD_SIZE), value_row_matrix.reshape(N_DP, GROUP_TOKENS, KEY_VALUE_HEADS, HEAD_SIZE), document_labels, row_position))
        mixed_heads = lowered_value(lowered_backward(mixed_heads.reshape(TOKEN_TOTAL, QUERY_HEADS * HEAD_SIZE)))
        middle = input_full + lowered_backward(jnp.dot(mixed_heads, out_w, precision=highest_precision))
        normed_two = lowered_value(rms_scale(middle, gain_two))
        gate_pre = lowered_backward(jnp.dot(normed_two, gate_w, precision=highest_precision))
        up_pre = lowered_backward(jnp.dot(normed_two, up_w, precision=highest_precision))
        activated = lowered_value(jax.nn.silu(gate_pre) * up_pre)
        return middle + lowered_backward(jnp.dot(activated, down_w, precision=highest_precision))
    inputs = (layer_input, attn_gain, w_query, key_projection, value_projection, query_gain, key_gain, w_out, mlp_gain, w_gate, w_up, w_down)
    inputs = tuple((item.astype(jnp.float32) for item in inputs))
    output, pullback = jax.vjp(forward, *inputs)
    grads = pullback(out_grad.astype(jnp.float32))
    return (output.astype(jnp.bfloat16), grads[0].astype(jnp.bfloat16), grads[1], grads[2], grads[3], grads[4], grads[5], grads[6], grads[7], grads[8], grads[9], grads[10], grads[11])
```

```python
import functools

import jax
import jax.numpy as jnp
from jax import lax
from jax.experimental import pallas as pl
from jax.experimental.pallas import tpu as pltpu
from jax.sharding import PartitionSpec as P

MESH = pl.DeviceIdType.MESH
BF = jnp.bfloat16
F32 = jnp.float32
HEAD = 128
EPS = 1e-06
ROPE_BASE = 1000000.0
MASKED = -1e30
SCALE = HEAD ** (-0.5)
TOK = 128
GROUP = 1024
WIDTH = 1024
NA = 768
NM = 1152
CH = 256
N_SEMS = 220


def dot(a, b):
    return jnp.dot(a, b, preferred_element_type=F32)


def dot_nt(a, b):
    return lax.dot_general(a, b, (((1,), (1,)), ((), ())), preferred_element_type=F32)


def dot_tn(a, b):
    return lax.dot_general(a, b, (((0,), (0,)), ((), ())), preferred_element_type=F32)


class Links:
    def __init__(self, send_sems, recv_sems):
        self.send_sems, self.recv_sems = send_sems, recv_sems
        self.sends, self.recvs = 0, 0
        self.pending = []

    def send_ids(self, count=1):
        first = self.sends
        self.sends += count
        assert self.sends <= N_SEMS
        return first

    def recv_ids(self, count=1):
        first = self.recvs
        self.recvs += count
        assert self.recvs <= N_SEMS
        return first

    def copy(self, src, dst, device, send_id, recv_id):
        return pltpu.make_async_remote_copy(
            src_ref=src,
            dst_ref=dst,
            send_sem=self.send_sems.at[send_id],
            recv_sem=self.recv_sems.at[recv_id],
            device_id=device,
            device_id_type=MESH,
        )

    def send(self, src, dst, device, recv_id):
        copy = self.copy(src, dst, device, self.send_ids(), recv_id)
        copy.start()
        self.pending.append(copy)

    def wait(self, dst, device, recv_id):
        self.copy(dst, dst, device, 0, recv_id).wait_recv()

    def drain(self):
        for copy in self.pending:
            copy.wait_send()


class Place:
    def __init__(self):
        self.d = lax.axis_index("dp")
        self.t = lax.axis_index("tensor")
        self.x = self.d // 4
        self.y = (self.d // 2) % 2
        self.c = self.d % 2

    def dp_index(self, dx, dy, dc):
        return ((self.x + dx) % 4) * 4 + ((self.y + dy) % 2) * 2 + (self.c + dc) % 2

    def dp_peer(self, dx, dy, dc):
        return (self.dp_index(dx, dy, dc), self.t)

    def tensor_peer(self, t):
        return (self.d, t)


class WeightGather:
    def __init__(self, links, place, buf):
        self.links, self.place, self.buf = links, place, buf
        names = ["y", "xm0", "xp0", "xm1", "xp1", "l0", "r0", "l1", "r1"]
        names += ["c%d%d" % (dx, dy) for dx in range(4) for dy in range(2)]
        self.ids = {name: links.recv_ids() for name in names}

    def rows(self, dx, dy, dc, half=None):
        first = self.place.dp_index(dx, dy, dc) * 64
        if half is None:
            return self.buf.at[pl.ds(pl.multiple_of(first, 64), 64)]
        return self.buf.at[pl.ds(pl.multiple_of(first + 32 * half, 32), 32)]

    def push(self, src, dst, device, name):
        self.links.send(src, dst, device, self.ids[name])

    def core(self, dx, dy):
        ref = self.rows(dx, dy, 0)
        self.push(ref, ref, self.place.dp_peer(0, 0, 1), "c%d%d" % (dx, dy))

    def got(self, ref, device, name):
        self.links.wait(ref, device, self.ids[name])

    def begin(self):
        place, own = self.place, self.rows(0, 0, 0)
        self.push(own, own, place.dp_peer(0, 1, 0), "y")
        self.push(own, own, place.dp_peer(1, 0, 0), "xm0")
        self.push(own, own, place.dp_peer(3, 0, 0), "xp0")
        self.core(0, 0)

    def second(self):
        place, ref = self.place, self.rows(0, 1, 0)
        self.got(ref, place.dp_peer(0, 1, 0), "y")
        self.push(ref, ref, place.dp_peer(1, 0, 0), "xm1")
        self.push(ref, ref, place.dp_peer(3, 0, 0), "xp1")
        self.core(0, 1)

    def third(self, dy):
        place = self.place
        left, right = place.dp_peer(3, 0, 0), place.dp_peer(1, 0, 0)
        self.got(self.rows(3, dy, 0), left, "xm%d" % dy)
        half = self.rows(3, dy, 0, 0)
        self.push(half, half, right, "l%d" % dy)
        self.got(self.rows(1, dy, 0), right, "xp%d" % dy)
        half = self.rows(1, dy, 0, 1)
        self.push(half, half, left, "r%d" % dy)
        self.core(3, dy)
        self.core(1, dy)

    def fourth(self, dy):
        place = self.place
        self.got(self.rows(2, dy, 0, 0), place.dp_peer(3, 0, 0), "l%d" % dy)
        self.got(self.rows(2, dy, 0, 1), place.dp_peer(1, 0, 0), "r%d" % dy)
        self.core(2, dy)

    def finish(self):
        for dx in range(4):
            for dy in range(2):
                self.got(self.rows(dx, dy, 1), self.place.dp_peer(0, 0, 1), "c%d%d" % (dx, dy))


class WeightSum:
    def __init__(self, links, place, full, core_in, total, side, last, wide):
        self.links, self.place, self.full = links, place, full
        self.core_in, self.total, self.side, self.last, self.wide = core_in, total, side, last, wide
        self.ids = {n: links.recv_ids() for n in ("core", "la", "lr", "ra", "rr", "lc", "rc", "y")}

    def begin(self):
        place = self.place
        self.links.send(self.full.at[:, (place.c + 1) % 2], self.core_in, place.dp_peer(0, 0, 1), self.ids["core"])

    def cross(self):
        place, links, side = self.place, self.links, self.side
        links.wait(self.core_in, place.dp_peer(0, 0, 1), self.ids["core"])

        def add(i, carry):
            self.total[i] = (
                self.full[i, place.c].astype(F32) + self.core_in[i].astype(F32)
            ).astype(BF)
            return carry

        lax.fori_loop(0, 8, add, 0)
        left, right = place.dp_peer(3, 0, 0), place.dp_peer(1, 0, 0)
        x = place.x
        links.send(self.total.at[((x + 2) % 4) * 2], side.at[0], right, self.ids["la"])
        links.send(self.total.at[((x + 2) % 4) * 2 + 1], side.at[2], left, self.ids["ra"])
        links.send(self.total.at[((x + 1) % 4) * 2 + 1], side.at[1], right, self.ids["lr"])
        links.send(self.total.at[((x + 3) % 4) * 2], side.at[3], left, self.ids["rr"])

    def relay(self):
        place, links, side = self.place, self.links, self.side
        left, right = place.dp_peer(3, 0, 0), place.dp_peer(1, 0, 0)
        x = place.x
        links.wait(side.at[0], left, self.ids["la"])
        side[7] = (self.total[((x + 1) % 4) * 2].astype(F32) + side[0].astype(F32)).astype(BF)
        links.send(side.at[7], side.at[4], right, self.ids["lc"])
        links.wait(side.at[2], right, self.ids["ra"])
        side[8] = (self.total[((x + 3) % 4) * 2 + 1].astype(F32) + side[2].astype(F32)).astype(BF)
        links.send(side.at[8], side.at[5], left, self.ids["rc"])

    def pair(self):
        place, links, side = self.place, self.links, self.side
        left, right = place.dp_peer(3, 0, 0), place.dp_peer(1, 0, 0)
        links.wait(side.at[1], left, self.ids["lr"])
        links.wait(side.at[3], right, self.ids["rr"])
        links.wait(side.at[4], left, self.ids["lc"])
        links.wait(side.at[5], right, self.ids["rc"])
        x = place.x
        self.wide[0] = self.total[x * 2].astype(F32) + side[4].astype(F32) + side[3].astype(F32)
        self.wide[1] = self.total[x * 2 + 1].astype(F32) + side[5].astype(F32) + side[1].astype(F32)
        side[9] = self.wide[(place.y + 1) % 2].astype(BF)
        links.send(side.at[9], side.at[6], place.dp_peer(0, 1, 0), self.ids["y"])

    def finish(self):
        place = self.place
        self.links.wait(self.side.at[6], place.dp_peer(0, 1, 0), self.ids["y"])
        self.last[...] = self.wide[place.y] + self.side[6].astype(F32)


class TokenSum:
    def __init__(self, links, place, partial, landed):
        self.links, self.place, self.partial, self.landed = links, place, partial, landed
        self.send_id, self.recv_id = links.send_ids(8), links.recv_ids(8)

    def copy_to(self, t):
        rows = pl.ds(pl.multiple_of(t * TOK, TOK), TOK)
        me = self.place.t
        return self.links.copy(
            self.partial.at[rows], self.landed.at[me], self.place.tensor_peer(t), self.send_id + t, self.recv_id + me
        )

    def send_block(self, t):
        @pl.when(t != self.place.t)
        def _():
            self.copy_to(t).start()

    def total(self):
        place, links = self.place, self.links
        own = pl.ds(pl.multiple_of(place.t * TOK, TOK), TOK)
        acc = self.partial[own].astype(F32)
        for k in range(1, 8):
            src = (place.t + k) % 8
            links.wait(self.landed.at[src], place.tensor_peer(src), self.recv_id + src)
        for k in range(1, 8):
            acc = acc + self.landed[(place.t + k) % 8].astype(F32)
        return acc

    def drain(self):
        for k in range(1, 8):
            self.copy_to((self.place.t + k) % 8).wait_send()


class TokenGather:
    def __init__(self, links, place, buf):
        self.links, self.place, self.buf = links, place, buf
        self.recv_id = links.recv_ids(8)

    def rows(self, t):
        return self.buf.at[pl.ds(pl.multiple_of(t * TOK, TOK), TOK)]

    def begin(self):
        t = self.place.t
        order = [t + 1 - 2 * (t % 2)]
        for k in range(1, 4):
            first = ((t // 2 + 4 - k) % 4) * 2
            order += [first + t % 2, first + 1 - t % 2]
        own = self.rows(t)
        for peer in order:
            self.links.send(own, own, self.place.tensor_peer(peer), self.recv_id + t)

    def wait(self, t):
        self.links.wait(self.rows(t), self.place.tensor_peer(t), self.recv_id + t)

    def wait_all(self):
        for k in range(1, 8):
            self.wait((self.place.t + k) % 8)


def layer_kernel(
    wa_own,
    wm_own,
    gain_own,
    x_own,
    og_own,
    query_gain,
    key_gain,
    cosine,
    sine,
    starts,
    out_ref,
    in_grad_ref,
    ga_ref,
    gm_ref,
    gains_ref,
    wa,
    wm,
    gain_in,
    gain_one,
    gain_two,
    xs,
    ogs,
    h1,
    r1,
    qk_pre,
    q_rot,
    k_rot,
    vals,
    mixed,
    lse,
    p1,
    l1,
    middle,
    h2,
    grad_act,
    act,
    dgu,
    p2,
    l2,
    po,
    lo,
    gb,
    grad_mid,
    dk,
    dv,
    dqkv,
    p3,
    l3,
    gm_full,
    gm_core,
    gm_total,
    gm_side,
    gm_wide,
    ga_full,
    ga_core,
    ga_total,
    ga_side,
    ga_wide,
    gg,
    gg_sum,
    gg_t,
    gg_d,
    send_sems,
    recv_sems,
):
    links = Links(send_sems, recv_sems)
    place = Place()
    d, t = place.d, place.t
    own = pl.ds(pl.multiple_of(t * TOK, TOK), TOK)
    own_w = pl.ds(pl.multiple_of(d * 64, 64), 64)
    dp_peers = [(k // 4, (k // 2) % 2, k % 2) for k in range(1, 16)]

    barrier = pltpu.get_barrier_semaphore()
    for k in range(1, 8):
        pl.semaphore_signal(
            barrier, inc=1, device_id=place.tensor_peer((t + k) % 8), device_id_type=MESH
        )
    for k in dp_peers:
        pl.semaphore_signal(barrier, inc=1, device_id=place.dp_peer(*k), device_id_type=MESH)

    xs[own] = x_own[...]
    ogs[own] = og_own[...]
    wa[own_w] = wa_own[...]
    wm[own_w] = wm_own[...]
    gain_in[d] = gain_own[...]

    pl.semaphore_wait(barrier, 22)

    gather_a = WeightGather(links, place, wa)
    gather_m = WeightGather(links, place, wm)
    gather_x = TokenGather(links, place, xs)
    gather_og = TokenGather(links, place, ogs)
    gather_h2 = TokenGather(links, place, h2)
    gather_gb = TokenGather(links, place, gb)
    sum_1 = TokenSum(links, place, p1, l1)
    sum_2 = TokenSum(links, place, p2, l2)
    sum_o = TokenSum(links, place, po, lo)
    sum_3 = TokenSum(links, place, p3, l3)
    weight_m = WeightSum(links, place, gm_full, gm_core, gm_total, gm_side, gm_ref, gm_wide)
    weight_a = WeightSum(links, place, ga_full, ga_core, ga_total, ga_side, ga_ref, ga_wide)

    gather_a.begin()
    gain_id = links.recv_ids(16)
    for k in dp_peers:
        links.send(gain_in.at[d], gain_in.at[d], place.dp_peer(*k), gain_id + d)
    gather_x.begin()
    gather_a.second()
    gather_a.third(0)
    gather_a.third(1)
    gather_m.begin()

    for k in dp_peers:
        src = place.dp_index(*k)
        links.wait(gain_in.at[src], place.dp_peer(*k), gain_id + src)
    low = lax.broadcasted_iota(jnp.int32, (1, 128), 1) < 64
    for k in range(8):
        even, odd = gain_in[2 * k][0:1], gain_in[2 * k + 1][0:1]
        cols = slice(128 * k, 128 * k + 128)
        gain_one[0:1, cols] = jnp.where(low, even, pltpu.roll(odd, 64, 1))
        gain_two[0:1, cols] = jnp.where(low, pltpu.roll(even, 64, 1), odd)

    gather_a.fourth(0)
    gather_a.fourth(1)
    gather_x.wait_all()

    def norm_chunk(i, carry):
        rows = pl.ds(pl.multiple_of(i * 128, 128), 128)
        wide = xs[rows].astype(F32)
        r = lax.rsqrt(jnp.mean(wide * wide, axis=-1, keepdims=True) + EPS)
        r1[rows] = r
        h1[rows] = (wide * r * gain_one[0:1]).astype(BF)
        return carry

    lax.fori_loop(0, 8, norm_chunk, 0)
    gather_a.finish()
    gather_og.begin()
    gather_m.second()

    def qkv_chunk(i, carry):
        rows = pl.ds(pl.multiple_of(i * CH, CH), CH)
        pre = dot(h1[rows], wa[:, 0:512])
        qk_pre[rows] = pre[:, 0:384]
        vals[rows] = pre[:, 384:512].astype(BF)
        cos, sin = cosine[rows], sine[rows]
        for h in range(3):
            part = pre[:, 128 * h : 128 * h + 128]
            r = lax.rsqrt(jnp.mean(part * part, axis=-1, keepdims=True) + EPS)
            scaled = part * r * (query_gain if h < 2 else key_gain)[0:1]
            turned = (scaled * cos + pltpu.roll(scaled, 64, 1) * sin).astype(BF)
            if h < 2:
                q_rot[h, rows] = turned
            else:
                k_rot[rows] = turned
        return carry

    lax.fori_loop(0, 4, qkv_chunk, 0)
    gather_m.third(0)
    gather_m.third(1)

    def allowed(qb, keys):
        key_at = lax.broadcasted_iota(jnp.int32, (CH, keys), 1)
        query_at = lax.broadcasted_iota(jnp.int32, (CH, keys), 0) + qb * CH
        return (key_at >= starts[qb * CH : qb * CH + CH]) & (key_at <= query_at)

    for qb in range(4):
        rows = slice(qb * CH, qb * CH + CH)
        keys = CH * (qb + 1)
        ok = allowed(qb, keys)
        for h in range(2):
            scores = jnp.where(ok, dot_nt(q_rot[h, rows], k_rot[0:keys]) * SCALE, MASKED)
            top = jnp.max(scores, axis=-1, keepdims=True)
            terms = jnp.exp(scores - top)
            total = jnp.sum(terms, axis=-1, keepdims=True)
            lse[h, rows] = top + jnp.log(total)
            weights = (terms * (1.0 / total)).astype(BF)
            mixed[rows, 128 * h : 128 * h + 128] = dot(weights, vals[0:keys]).astype(BF)
        p1[rows] = dot_nt(mixed[rows], wa[:, 512:768]).astype(BF)
        sum_1.send_block(2 * qb)
        sum_1.send_block(2 * qb + 1)

    gather_m.fourth(0)
    gather_m.fourth(1)
    gather_og.wait_all()
    gather_m.finish()

    def grad_act_chunk(i, carry):
        rows = pl.ds(pl.multiple_of(i * CH, CH), CH)
        grad_act[rows] = dot(ogs[rows], wm[:, 768:1152])
        return carry

    lax.fori_loop(0, 4, grad_act_chunk, 0)

    mid = x_own[...].astype(F32) + sum_1.total()
    middle[...] = mid
    r_two = lax.rsqrt(jnp.mean(mid * mid, axis=-1, keepdims=True) + EPS)
    h2[own] = (mid * r_two * gain_two[0:1]).astype(BF)
    gather_h2.begin()

    def mlp_chunk(j):
        rows = pl.ds(pl.multiple_of(j * CH, CH), CH)
        pre = dot(h2[rows], wm[:, 0:768])
        gate, up = pre[:, 0:384], pre[:, 384:768]
        sig = 1.0 / (1.0 + jnp.exp(-gate))
        silu = gate * sig
        acted = (silu * up).astype(BF)
        act[rows] = acted
        grad = grad_act[rows]
        dgu[rows, 0:384] = (grad * up * (sig * (1.0 + gate * (1.0 - sig)))).astype(BF)
        dgu[rows, 384:768] = (grad * silu).astype(BF)
        p2[rows] = dot_nt(dgu[rows], wm[:, 0:768]).astype(BF)
        sum_2.send_block(2 * j)
        sum_2.send_block(2 * j + 1)
        po[rows] = dot_nt(acted, wm[:, 768:1152]).astype(BF)

    gather_h2.wait(t + 1 - 2 * (t % 2))
    mlp_chunk(t // 2)

    def mlp_step(k, carry):
        j = (t // 2 + k) % 4
        gather_h2.wait(2 * j)
        gather_h2.wait(2 * j + 1)
        mlp_chunk(j)
        return carry

    lax.fori_loop(1, 4, mlp_step, 0)
    for k in range(1, 8):
        sum_o.send_block((t + k) % 8)

    def mlp_weight_chunk(i, carry):
        cols = pl.ds(pl.multiple_of(i * CH, CH), CH)
        pair = pl.ds(i * 2, 2)
        gm_full[pair, :, :, 0:768] = dot_tn(h2[:, cols], dgu[...]).astype(BF).reshape(2, 2, 64, 768)
        gm_full[pair, :, :, 768:1152] = dot_tn(ogs[:, cols], act[...]).astype(BF).reshape(2, 2, 64, 384)
        return carry

    lax.fori_loop(0, 4, mlp_weight_chunk, 0)
    weight_m.begin()

    err = sum_2.total()
    mid = middle[...]
    r_two = lax.rsqrt(jnp.mean(mid * mid, axis=-1, keepdims=True) + EPS)
    normed = mid * r_two
    part = jnp.sum(err * normed, axis=0, keepdims=True)
    gg[...] = jnp.zeros_like(gg)
    for k in range(8):
        gg[8 + k : 9 + k] = part[:, 128 * k : 128 * k + 128]
    scaled = err * gain_two[0:1]
    grad = og_own[...].astype(F32) + r_two * (
        scaled - normed * jnp.mean(scaled * normed, axis=-1, keepdims=True)
    )
    grad_mid[...] = grad
    gb[own] = grad.astype(BF)
    gather_gb.begin()
    weight_m.cross()

    out_ref[...] = (middle[...] + sum_o.total()).astype(BF)
    dk[...] = jnp.zeros_like(dk)
    dv[...] = jnp.zeros_like(dv)
    gather_gb.wait_all()

    def back_rope(turned, pre, gain, cos, sin):
        r = lax.rsqrt(jnp.mean(pre * pre, axis=-1, keepdims=True) + EPS)
        normed = pre * r
        err = turned * cos - pltpu.roll(turned, 64, 1) * sin
        scaled = err * gain
        grad = r * (scaled - normed * jnp.mean(scaled * normed, axis=-1, keepdims=True))
        return grad, jnp.sum(err * normed, axis=0, keepdims=True)

    attn_part = jnp.zeros((1, WIDTH), F32)
    for qb in (3, 2, 1, 0):
        rows = slice(qb * CH, qb * CH + CH)
        keys = CH * (qb + 1)
        ok = allowed(qb, keys)
        cos, sin = cosine[rows], sine[rows]
        grad_mixed = dot(gb[rows], wa[:, 512:768]).astype(BF)
        for h in range(2):
            grad_h = grad_mixed[:, 128 * h : 128 * h + 128]
            scores = jnp.where(ok, dot_nt(q_rot[h, rows], k_rot[0:keys]) * SCALE, MASKED)
            probs = jnp.exp(scores - lse[h, rows])
            grad_probs = dot_nt(grad_h, vals[0:keys])
            inner = jnp.sum(probs * grad_probs, axis=-1, keepdims=True)
            grad_scores = (probs * (grad_probs - inner)).astype(BF)
            dk[0:keys] += dot_tn(grad_scores, q_rot[h, rows]) * SCALE
            dv[0:keys] += dot_tn(probs.astype(BF), grad_h)
            grad_q = (dot(grad_scores, k_rot[0:keys]) * SCALE).astype(BF).astype(F32)
            pre = qk_pre[rows, 128 * h : 128 * h + 128]
            grad, gain_part = back_rope(grad_q, pre, query_gain[0:1], cos, sin)
            dqkv[rows, 128 * h : 128 * h + 128] = grad.astype(BF)
            gg[16:17] += gain_part
        grad_k = dk[rows].astype(BF).astype(F32)
        grad, gain_part = back_rope(grad_k, qk_pre[rows, 256:384], key_gain[0:1], cos, sin)
        dqkv[rows, 256:384] = grad.astype(BF)
        gg[17:18] += gain_part
        dqkv[rows, 384:512] = dv[rows].astype(BF)
        err = dot_nt(dqkv[rows], wa[:, 0:512])
        p3[rows] = err.astype(BF)
        sum_3.send_block(2 * qb)
        sum_3.send_block(2 * qb + 1)
        attn_part += jnp.sum(err * (xs[rows].astype(F32) * r1[rows]), axis=0, keepdims=True)
        if qb == 2:
            weight_m.relay()
        if qb == 0:
            weight_m.pair()

    for k in range(8):
        gg[k : k + 1] = attn_part[:, 128 * k : 128 * k + 128]
    gg_id = links.recv_ids(8)
    for k in range(1, 8):
        links.send(gg, gg_t.at[t], place.tensor_peer((t + k) % 8), gg_id + t)

    def attn_weight_chunk(i, carry):
        cols = pl.ds(pl.multiple_of(i * CH, CH), CH)
        pair = pl.ds(i * 2, 2)
        ga_full[pair, :, :, 0:512] = dot_tn(h1[:, cols], dqkv[...]).astype(BF).reshape(2, 2, 64, 512)
        ga_full[pair, :, :, 512:768] = dot_tn(gb[:, cols], mixed[...]).astype(BF).reshape(2, 2, 64, 256)
        return carry

    lax.fori_loop(0, 4, attn_weight_chunk, 0)
    weight_a.begin()

    total = gg[...]
    for k in range(1, 8):
        src = (t + k) % 8
        links.wait(gg_t.at[src], place.tensor_peer(src), gg_id + src)
        total = total + gg_t[src]
    gg_sum[...] = total
    gg_id2 = links.recv_ids(16)
    for k in dp_peers:
        links.send(gg_sum, gg_d.at[d], place.dp_peer(*k), gg_id2 + d)

    weight_a.cross()
    weight_m.finish()
    weight_a.relay()

    gg_d[d] = gg_sum[...]
    for k in dp_peers:
        src = place.dp_index(*k)
        links.wait(gg_d.at[src], place.dp_peer(*k), gg_id2 + src)
    total = gg_d[0]
    for k in range(1, 16):
        total = total + gg_d[k]
    gains_ref[...] = total

    weight_a.pair()
    err = sum_3.total()
    r_one = r1[own]
    normed = x_own[...].astype(F32) * r_one
    scaled = err * gain_one[0:1]
    in_grad_ref[...] = (
        grad_mid[...]
        + r_one * (scaled - normed * jnp.mean(scaled * normed, axis=-1, keepdims=True))
    ).astype(BF)
    weight_a.finish()

    links.drain()
    for each in (sum_1, sum_2, sum_o, sum_3):
        each.drain()


def run_layer(*args):
    vmem = pl.BlockSpec(memory_space=pltpu.VMEM)

    def sds(shape, kind):
        return jax.ShapeDtypeStruct(shape, kind)

    def buf(shape, kind=BF):
        return pltpu.VMEM(shape, kind)

    group = (GROUP, WIDTH)
    landing = (8, TOK, WIDTH)
    scratch = [
        buf((WIDTH, NA)),
        buf((WIDTH, NM)),
        buf((16, 8, 128), F32),
        buf((1, WIDTH), F32),
        buf((1, WIDTH), F32),
        buf(group),
        buf(group),
        buf(group),
        buf((GROUP, 1), F32),
        buf((GROUP, 384), F32),
        buf((2, GROUP, HEAD)),
        buf((GROUP, HEAD)),
        buf((GROUP, HEAD)),
        buf((GROUP, 256)),
        buf((2, GROUP, 1), F32),
        buf(group),
        buf(landing),
        buf((TOK, WIDTH), F32),
        buf(group),
        buf((GROUP, 384), F32),
        buf((GROUP, 384)),
        buf((GROUP, 768)),
        buf(group),
        buf(landing),
        buf(group),
        buf(landing),
        buf(group),
        buf((TOK, WIDTH), F32),
        buf((GROUP, HEAD), F32),
        buf((GROUP, HEAD), F32),
        buf((GROUP, 512)),
        buf(group),
        buf(landing),
        buf((8, 2, 64, NM)),
        buf((8, 64, NM)),
        buf((8, 64, NM)),
        buf((10, 64, NM)),
        buf((2, 64, NM), F32),
        buf((8, 2, 64, NA)),
        buf((8, 64, NA)),
        buf((8, 64, NA)),
        buf((10, 64, NA)),
        buf((2, 64, NA), F32),
        buf((24, 128), F32),
        buf((24, 128), F32),
        buf((8, 24, 128), F32),
        buf((16, 24, 128), F32),
        pltpu.SemaphoreType.DMA((N_SEMS,)),
        pltpu.SemaphoreType.DMA((N_SEMS,)),
    ]
    return pl.pallas_call(
        layer_kernel,
        out_shape=(
            sds((TOK, WIDTH), BF),
            sds((TOK, WIDTH), BF),
            sds((64, NA), F32),
            sds((64, NM), F32),
            sds((24, 128), F32),
        ),
        in_specs=[vmem] * len(args),
        out_specs=(vmem,) * 5,
        scratch_shapes=scratch,
        name="layer",
        compiler_params=pltpu.CompilerParams(
            collective_id=0, has_side_effects=True, vmem_limit_bytes=63 * 2**20
        ),
    )(*args)


def tables(lengths):
    ends = jnp.cumsum(lengths)
    begins = ends - lengths
    at = jnp.arange(GROUP, dtype=jnp.int32)
    label = jnp.sum((at[:, None] >= ends[None, :]).astype(jnp.int32), axis=1)
    chosen = label[:, None] == jnp.arange(lengths.shape[0], dtype=jnp.int32)[None, :]
    starts = jnp.sum(jnp.where(chosen, begins[None, :], 0), axis=1)
    half = HEAD // 2
    frequency = ROPE_BASE ** (-(jnp.arange(half).astype(F32) * 2.0 / HEAD))
    angles = (at - starts).astype(F32)[:, None] * frequency[None, :]
    cos, sin = jnp.cos(angles), jnp.sin(angles)
    return (
        jnp.concatenate([cos, cos], axis=-1),
        jnp.concatenate([-sin, sin], axis=-1),
        starts[:, None],
    )


def per_device(
    layer_input,
    seq_lengths,
    attn_gain,
    w_query,
    key_projection,
    value_projection,
    query_gain,
    key_gain,
    w_out,
    mlp_gain,
    w_gate,
    w_up,
    w_down,
    out_grad,
):
    cosine, sine, starts = tables(seq_lengths[0])
    wa_own = jnp.concatenate([w_query, key_projection, value_projection, w_out.T], axis=1)
    wm_own = jnp.concatenate([w_gate, w_up, w_down.T], axis=1)
    gain_own = jnp.broadcast_to(jnp.concatenate([attn_gain, mlp_gain]).astype(F32)[None], (8, 128))
    out, in_grad, ga, gm, gains = run_layer(
        wa_own,
        wm_own,
        gain_own,
        layer_input,
        out_grad,
        query_gain.astype(F32)[None],
        key_gain.astype(F32)[None],
        cosine,
        sine,
        starts,
    )
    piece = attn_gain.shape[0]
    first = lax.axis_index("dp") * piece
    grad_attn_gain = lax.dynamic_slice_in_dim(gains[0:8].reshape(-1), first, piece, 0)
    grad_mlp_gain = lax.dynamic_slice_in_dim(gains[8:16].reshape(-1), first, piece, 0)
    return (
        out,
        in_grad,
        grad_attn_gain,
        ga[:, 0:256],
        ga[:, 256:384],
        ga[:, 384:512],
        gains[16],
        gains[17],
        ga[:, 512:768].T,
        grad_mlp_gain,
        gm[:, 0:384],
        gm[:, 384:768],
        gm[:, 768:1152].T,
    )


def solution(mesh):
    both = P(("dp", "tensor"), None)
    split = P("dp", "tensor")
    turned = P("tensor", "dp")
    in_specs = (
        both,
        P("dp", None),
        P("dp"),
        split,
        split,
        split,
        P(),
        P(),
        turned,
        P("dp"),
        split,
        split,
        turned,
        both,
    )
    out_specs = (both, both, P("dp"), split, split, split, P(), P(), turned, P("dp"), split, split, turned)
    return jax.shard_map(
        per_device, mesh=mesh, in_specs=in_specs, out_specs=out_specs, check_vma=False
    )
```

```python
import functools

import jax
import jax.numpy as jnp
from jax import lax
from jax.experimental import pallas as pl
from jax.experimental.pallas import tpu as pltpu
from jax.sharding import PartitionSpec as P

MESH = pl.DeviceIdType.MESH
BF = jnp.bfloat16
F32 = jnp.float32
HEAD = 128
EPS = 1e-06
ROPE_BASE = 1000000.0
MASKED = -1e30
SCALE = HEAD ** (-0.5)
TOK = 128
GROUP = 1024
WIDTH = 1024
NQ = 512
NO = 256
NM = 1152
CH = 256
N_SEMS = 240


def dot(a, b):
    return jnp.dot(a, b, preferred_element_type=F32)


def dot_nt(a, b):
    return lax.dot_general(a, b, (((1,), (1,)), ((), ())), preferred_element_type=F32)


def dot_tn(a, b):
    return lax.dot_general(a, b, (((0,), (0,)), ((), ())), preferred_element_type=F32)


class Links:
    def __init__(self, send_sems, recv_sems):
        self.send_sems, self.recv_sems = send_sems, recv_sems
        self.sends, self.recvs = 0, 0
        self.pending = []

    def recv_ids(self, count=1):
        first = self.recvs
        self.recvs += count
        assert self.recvs <= N_SEMS
        return first

    def copy(self, src, dst, device, send_id, recv_id):
        return pltpu.make_async_remote_copy(
            src_ref=src,
            dst_ref=dst,
            send_sem=self.send_sems.at[send_id],
            recv_sem=self.recv_sems.at[recv_id],
            device_id=device,
            device_id_type=MESH,
        )

    def send(self, src, dst, device, recv_id, when=None):
        copy = self.copy(src, dst, device, self.sends, recv_id)
        self.sends += 1
        assert self.sends <= N_SEMS
        if when is None:
            copy.start()
        else:
            pl.when(when)(copy.start)
        self.pending.append((copy, when))

    def wait(self, dst, device, recv_id, when=None):
        copy = self.copy(dst, dst, device, 0, recv_id)
        if when is None:
            copy.wait_recv()
        else:
            pl.when(when)(copy.wait_recv)

    def drain(self):
        for copy, when in self.pending:
            if when is None:
                copy.wait_send()
            else:
                pl.when(when)(copy.wait_send)


class Place:
    def __init__(self):
        d, t = lax.axis_index("dp"), lax.axis_index("tensor")
        self.d = d
        self.x, self.c = d // 4, d % 2
        self.y, self.z = (t // 4) * 2 + (d // 2) % 2, t % 4
        self.home = self.c == t // 4
        self.left_z, self.right_z = self.at(dz=3), self.at(dz=1)
        self.left_x, self.right_x = self.at(dx=3), self.at(dx=1)
        self.core = self.at(dc=1)
        self.swap = self.at(dy=2, dc=1)

    def device(self, x, y, z, c):
        return (x * 4 + (y % 2) * 2 + c, (y // 2) * 4 + z)

    def at(self, dx=0, dy=0, dz=0, dc=0):
        return self.device((self.x + dx) % 4, (self.y + dy) % 4, (self.z + dz) % 4, (self.c + dc) % 2)


class WeightGather:
    def __init__(self, links, place, own, buf):
        self.links, self.place, self.own, self.buf = links, place, own, buf
        self.y_id = links.recv_ids(4)
        self.ids = {name: links.recv_ids() for name in ("xm", "xp", "l", "r")}

    def block(self, index):
        return self.buf.at[pl.ds(pl.multiple_of(index * 64, 64), 64)]

    def rows(self, dx, half=None):
        first = ((self.place.x + dx) % 4) * 256
        if half is None:
            return self.buf.at[pl.ds(pl.multiple_of(first, 256), 256)]
        return self.buf.at[pl.ds(pl.multiple_of(first + 128 * half, 128), 128)]

    def begin(self):
        place, links = self.place, self.links
        side = place.y // 2
        for dy in (2, 1, 3, 0):
            device = place.device(place.x, (place.y + dy) % 4, place.z, side)
            links.send(
                self.own,
                self.block(place.d),
                device,
                self.y_id + place.d % 4,
                when=(place.c != side) if dy == 0 else None,
            )

        @pl.when(place.c == side)
        def _():
            self.block(place.d)[...] = self.own[...]

    def second(self):
        place, links = self.place, self.links
        for low in range(2):
            for core in range(2):
                y = 2 * place.c + low
                links.wait(
                    self.block(place.x * 4 + low * 2 + core),
                    place.device(place.x, y, place.z, core),
                    self.y_id + low * 2 + core,
                    when=(y != place.y) | (core != place.c),
                )
        mine = self.rows(0)
        links.send(mine, mine, place.right_x, self.ids["xm"])
        links.send(mine, mine, place.left_x, self.ids["xp"])

    def third(self):
        place, links = self.place, self.links
        links.wait(self.rows(3), place.left_x, self.ids["xm"])
        half = self.rows(3, 0)
        links.send(half, half, place.right_x, self.ids["l"])
        links.wait(self.rows(1), place.right_x, self.ids["xp"])
        half = self.rows(1, 1)
        links.send(half, half, place.left_x, self.ids["r"])

    def finish(self):
        place, links = self.place, self.links
        links.wait(self.rows(2, 0), place.left_x, self.ids["l"])
        links.wait(self.rows(2, 1), place.right_x, self.ids["r"])


class WeightSum:
    def __init__(self, links, place, full, side, land, out):
        self.links, self.place, self.full = links, place, full
        self.side, self.land, self.out = side, land, out
        self.ids = {n: links.recv_ids() for n in ("la", "lr", "ra", "rr", "lc", "rc")}
        self.y_id = links.recv_ids(4)

    def rows(self, dx, half):
        return pl.ds(pl.multiple_of(((self.place.x + dx) % 4) * 256 + 128 * half, 128), 128)

    def begin(self):
        place, links, side = self.place, self.links, self.side
        links.send(self.full.at[self.rows(2, 0)], side.at[0], place.right_x, self.ids["la"])
        links.send(self.full.at[self.rows(2, 1)], side.at[2], place.left_x, self.ids["ra"])
        links.send(self.full.at[self.rows(1, 1)], side.at[1], place.right_x, self.ids["lr"])
        links.send(self.full.at[self.rows(3, 0)], side.at[3], place.left_x, self.ids["rr"])

    def relay(self):
        place, links, side = self.place, self.links, self.side
        links.wait(side.at[0], place.left_x, self.ids["la"])
        side[6] = (self.full[self.rows(1, 0)].astype(F32) + side[0].astype(F32)).astype(BF)
        links.send(side.at[6], side.at[4], place.right_x, self.ids["lc"])
        links.wait(side.at[2], place.right_x, self.ids["ra"])
        side[7] = (self.full[self.rows(3, 1)].astype(F32) + side[2].astype(F32)).astype(BF)
        links.send(side.at[7], side.at[5], place.left_x, self.ids["rc"])

    def spread(self):
        place, links, side = self.place, self.links, self.side
        links.wait(side.at[1], place.left_x, self.ids["lr"])
        links.wait(side.at[3], place.right_x, self.ids["rr"])
        links.wait(side.at[4], place.left_x, self.ids["lc"])
        links.wait(side.at[5], place.right_x, self.ids["rc"])
        for half, first, other in ((0, 4, 3), (1, 5, 1)):
            side[8 + half] = (
                self.full[self.rows(0, half)].astype(F32)
                + side[first].astype(F32)
                + side[other].astype(F32)
            ).astype(BF)
        for low in range(2):
            for core in range(2):
                y = 2 * place.c + low
                away = (y != place.y) | (core != place.c)
                piece = side.at[8 + low, pl.ds(64 * core, 64)]
                links.send(
                    piece,
                    self.land.at[place.y],
                    place.device(place.x, y, place.z, core),
                    self.y_id + place.y,
                    when=away,
                )

                @pl.when(jnp.logical_not(away))
                def _():
                    self.land[place.y] = piece[...]

    def finish(self):
        place, links = self.place, self.links
        core = place.y // 2
        for k in range(4):
            y = (place.y + k) % 4
            links.wait(
                self.land.at[y],
                place.device(place.x, y, place.z, core),
                self.y_id + y,
                when=(place.c != core) if k == 0 else None,
            )
        total = self.land[0].astype(F32)
        for y in range(1, 4):
            total = total + self.land[y].astype(F32)
        self.out[...] = total


def token_rows(c, z, by_z):
    index = z * 2 + c if by_z else c * 4 + z
    return pl.multiple_of(index * TOK, TOK)


class TokenSum:
    def __init__(self, links, place, partial, core_in, side, by_z):
        self.links, self.place, self.partial = links, place, partial
        self.core_in, self.side, self.by_z = core_in, side, by_z
        self.core_id = links.recv_ids(4)
        self.ids = {n: links.recv_ids() for n in ("la", "lr", "ra", "rr", "lc", "rc")}

    def rows(self, c, z):
        return pl.ds(token_rows(c, z, self.by_z), TOK)

    def send_core(self, z, when=None):
        place = self.place
        self.links.send(
            self.partial.at[self.rows((place.c + 1) % 2, z)],
            self.core_in.at[z],
            place.core,
            self.core_id + z,
            when=when,
        )

    def half(self, z, h):
        return pl.ds(token_rows(self.place.c, z, self.by_z) + 64 * h, 64)

    def cross(self, k):
        place, links, side = self.place, self.links, self.side
        z = (place.z + k) % 4
        links.wait(self.core_in.at[z], place.core, self.core_id + z)
        rows = self.rows(place.c, z)
        self.partial[rows] = (
            self.partial[rows].astype(F32) + self.core_in[z].astype(F32)
        ).astype(BF)
        if k == 2:
            links.send(self.partial.at[self.half(z, 0)], side.at[0], place.right_z, self.ids["la"])
            links.send(self.partial.at[self.half(z, 1)], side.at[2], place.left_z, self.ids["ra"])
        if k == 1:
            links.send(self.partial.at[self.half(z, 1)], side.at[1], place.right_z, self.ids["lr"])
        if k == 3:
            links.send(self.partial.at[self.half(z, 0)], side.at[3], place.left_z, self.ids["rr"])

    def relay(self):
        place, links, side = self.place, self.links, self.side
        z = place.z
        links.wait(side.at[0], place.left_z, self.ids["la"])
        side[6] = (self.partial[self.half((z + 1) % 4, 0)].astype(F32) + side[0].astype(F32)).astype(BF)
        links.send(side.at[6], side.at[4], place.right_z, self.ids["lc"])
        links.wait(side.at[2], place.right_z, self.ids["ra"])
        side[7] = (self.partial[self.half((z + 3) % 4, 1)].astype(F32) + side[2].astype(F32)).astype(BF)
        links.send(side.at[7], side.at[5], place.left_z, self.ids["rc"])

    def total(self):
        place, links, side = self.place, self.links, self.side
        links.wait(side.at[1], place.left_z, self.ids["lr"])
        links.wait(side.at[3], place.right_z, self.ids["rr"])
        links.wait(side.at[4], place.left_z, self.ids["lc"])
        links.wait(side.at[5], place.right_z, self.ids["rc"])
        parts = []
        for half, first, other in ((0, 4, 3), (1, 5, 1)):
            parts.append(
                self.partial[self.half(place.z, half)].astype(F32)
                + side[first].astype(F32)
                + side[other].astype(F32)
            )
        return jnp.concatenate(parts, axis=0)


class TokenGather:
    def __init__(self, links, place, buf, by_z):
        self.links, self.place, self.buf, self.by_z = links, place, buf, by_z
        names = ("zm", "zp", "l", "r", "c0", "c1", "c2", "c3")
        self.ids = {name: links.recv_ids() for name in names}

    def rows(self, k, core=0, half=None):
        place = self.place
        first = token_rows((place.c + core) % 2, (place.z + k) % 4, self.by_z)
        if half is None:
            return self.buf.at[pl.ds(first, TOK)]
        return self.buf.at[pl.ds(first + 64 * half, 64)]

    def push(self, ref, device, name):
        self.links.send(ref, ref, device, self.ids[name])

    def begin(self):
        place, own = self.place, self.rows(0)
        self.push(own, place.right_z, "zm")
        self.push(own, place.left_z, "zp")
        self.push(own, place.core, "c0")

    def sides(self):
        place = self.place
        self.links.wait(self.rows(3), place.left_z, self.ids["zm"])
        self.push(self.rows(3, half=0), place.right_z, "l")
        self.push(self.rows(3), place.core, "c3")
        self.links.wait(self.rows(1), place.right_z, self.ids["zp"])
        self.push(self.rows(1, half=1), place.left_z, "r")
        self.push(self.rows(1), place.core, "c1")

    def far(self):
        place = self.place
        self.links.wait(self.rows(2, half=0), place.left_z, self.ids["l"])
        self.links.wait(self.rows(2, half=1), place.right_z, self.ids["r"])
        self.push(self.rows(2), place.core, "c2")

    def core(self, k):
        self.links.wait(self.rows(k, core=1), self.place.core, self.ids["c%d" % k])


def layer_kernel(
    wq_own,
    wo_own,
    wm_own,
    gain_own,
    x_own,
    og_own,
    query_gain,
    key_gain,
    trig_own,
    starts_own,
    out_ref,
    in_grad_ref,
    gq_ref,
    go_ref,
    gm_ref,
    gains_ref,
    wq,
    wo,
    wm,
    gain_in,
    gain_one,
    gain_two,
    trig,
    starts,
    cosine,
    sine,
    xs,
    ogs,
    h1,
    r1,
    qk_pre,
    q_rot,
    k_rot,
    vals,
    mixed,
    lse,
    p1,
    p1_core,
    p1_side,
    middle,
    h2,
    grad_act,
    act,
    dgu,
    p2,
    p2_core,
    p2_side,
    po,
    po_core,
    po_side,
    gb,
    grad_mid,
    dk,
    dv,
    dqkv,
    p3,
    p3_core,
    p3_side,
    gm_full,
    gm_side,
    gm_land,
    gq_full,
    gq_side,
    gq_land,
    go_full,
    go_side,
    go_land,
    out_tmp,
    in_grad_tmp,
    gg,
    gg_y,
    gg_a,
    gg_x,
    gg_b,
    gg_z,
    send_sems,
    recv_sems,
):
    links = Links(send_sems, recv_sems)
    place = Place()
    x, y, z, c = place.x, place.y, place.z, place.c
    home, away = place.home, jnp.logical_not(place.home)
    own = pl.ds(token_rows(c, z, False), TOK)
    own_z = pl.ds(token_rows(c, z, True), TOK)
    swap_own = pl.ds(token_rows((c + 1) % 2, z, False), TOK)
    swap_z = pl.ds(token_rows((c + 1) % 2, z, True), TOK)
    column = [(dy, dc) for dy in range(4) for dc in range(2) if dy or dc]

    barrier = pltpu.get_barrier_semaphore()
    for peer in (
        [place.at(dy=dy, dc=dc) for dy, dc in column]
        + [place.at(dx=k) for k in range(1, 4)]
        + [place.at(dz=k) for k in range(1, 4)]
    ):
        pl.semaphore_signal(barrier, inc=1, device_id=peer, device_id_type=MESH)

    gather_q = WeightGather(links, place, wq_own, wq)
    gather_o = WeightGather(links, place, wo_own, wo)
    gather_m = WeightGather(links, place, wm_own, wm)
    gather_x = TokenGather(links, place, xs, False)
    gather_og = TokenGather(links, place, ogs, True)
    gather_h2 = TokenGather(links, place, h2, True)
    gather_gb = TokenGather(links, place, gb, False)
    sum_1 = TokenSum(links, place, p1, p1_core, p1_side, False)
    sum_2 = TokenSum(links, place, p2, p2_core, p2_side, True)
    sum_o = TokenSum(links, place, po, po_core, po_side, True)
    sum_3 = TokenSum(links, place, p3, p3_core, p3_side, False)
    weight_m = WeightSum(links, place, gm_full, gm_side, gm_land, gm_ref)
    weight_q = WeightSum(links, place, gq_full, gq_side, gq_land, gq_ref)
    weight_o = WeightSum(links, place, go_full, go_side, go_land, go_ref)
    x_id, og_id, trig_id, starts_id, out_id, in_grad_id = [links.recv_ids() for _ in range(6)]
    gain_id, gain_x_id = links.recv_ids(4), links.recv_ids(4)
    gg_y_id, gg_x_id, gg_z_id = links.recv_ids(8), links.recv_ids(4), links.recv_ids(4)

    @pl.when(home)
    def _():
        xs[own] = x_own[...]
        ogs[own_z] = og_own[...]
        trig[...] = trig_own[...]
        starts[...] = starts_own[...]

    gain_in[place.d] = gain_own[...]

    pl.semaphore_wait(barrier, 13)

    links.send(x_own, xs.at[swap_own], place.swap, x_id, when=away)
    gather_q.begin()
    for dy, dc in ((0, 1), (1, 0), (1, 1)):
        other_y = (y // 2) * 2 + (y % 2 + dy) % 2
        peer = place.device(x, other_y, z, (c + dc) % 2)
        links.send(gain_in.at[place.d], gain_in.at[place.d], peer, gain_id + place.d % 4)
    links.send(trig_own, trig, place.core, trig_id, when=home)
    links.send(starts_own, starts, place.core, starts_id, when=home)
    gather_o.begin()

    links.wait(xs.at[own], place.swap, x_id, when=away)
    gather_x.begin()
    gather_q.second()
    for dy, dc in ((0, 1), (1, 0), (1, 1)):
        other_y = (y // 2) * 2 + (y % 2 + dy) % 2
        index = x * 4 + (other_y % 2) * 2 + (c + dc) % 2
        peer = place.device(x, other_y, z, (c + dc) % 2)
        links.wait(gain_in.at[index], peer, gain_id + index % 4)
    four = pl.ds(x * 4, 4)
    for k in range(1, 4):
        links.send(gain_in.at[four], gain_in.at[four], place.at(dx=k), gain_x_id + x)
    gather_o.second()
    links.send(og_own, ogs.at[swap_z], place.swap, og_id, when=away)

    gather_x.sides()
    gather_q.third()
    gather_m.begin()
    for k in range(1, 4):
        other = (x + k) % 4
        links.wait(gain_in.at[pl.ds(other * 4, 4)], place.at(dx=k), gain_x_id + other)
    low = lax.broadcasted_iota(jnp.int32, (1, 128), 1) < 64
    for k in range(8):
        even, odd = gain_in[2 * k][0:1], gain_in[2 * k + 1][0:1]
        cols = slice(128 * k, 128 * k + 128)
        gain_one[0:1, cols] = jnp.where(low, even, pltpu.roll(odd, 64, 1))
        gain_two[0:1, cols] = jnp.where(low, pltpu.roll(even, 64, 1), odd)

    links.wait(trig, place.core, trig_id, when=away)
    links.wait(starts, place.core, starts_id, when=away)

    def trig_chunk(i, carry):
        rows = pl.ds(pl.multiple_of(i * CH, CH), CH)
        pair = trig[rows]
        turned = pltpu.roll(pair, 64, 1)
        cosine[rows] = jnp.where(low, pair, turned)
        sine[rows] = jnp.where(low, -turned, pair)
        return carry

    lax.fori_loop(0, 4, trig_chunk, 0)

    gather_x.far()
    gather_o.third()
    for k in range(4):
        gather_x.core(k)
    links.wait(ogs.at[own_z], place.swap, og_id, when=away)
    gather_og.begin()

    def norm_chunk(i, carry):
        rows = pl.ds(pl.multiple_of(i * 128, 128), 128)
        wide = xs[rows].astype(F32)
        r = lax.rsqrt(jnp.mean(wide * wide, axis=-1, keepdims=True) + EPS)
        r1[rows] = r
        h1[rows] = (wide * r * gain_one[0:1]).astype(BF)
        return carry

    lax.fori_loop(0, 8, norm_chunk, 0)
    gather_q.finish()
    gather_m.second()

    def qkv_chunk(i, carry):
        rows = pl.ds(pl.multiple_of(i * CH, CH), CH)
        pre = dot(h1[rows], wq[...])
        qk_pre[rows] = pre[:, 0:384]
        vals[rows] = pre[:, 384:512].astype(BF)
        cos, sin = cosine[rows], sine[rows]
        for h in range(3):
            part = pre[:, 128 * h : 128 * h + 128]
            r = lax.rsqrt(jnp.mean(part * part, axis=-1, keepdims=True) + EPS)
            scaled = part * r * (query_gain if h < 2 else key_gain)[0:1]
            turned = (scaled * cos + pltpu.roll(scaled, 64, 1) * sin).astype(BF)
            if h < 2:
                q_rot[h, rows] = turned
            else:
                k_rot[rows] = turned
        return carry

    lax.fori_loop(0, 4, qkv_chunk, 0)
    gather_o.finish()
    gather_og.sides()

    def allowed(qb, keys):
        key_at = lax.broadcasted_iota(jnp.int32, (CH, keys), 1)
        query_at = lax.broadcasted_iota(jnp.int32, (CH, keys), 0) + qb * CH
        return (key_at >= starts[qb * CH : qb * CH + CH]) & (key_at <= query_at)

    def send_chunk(group_sum, qb):
        for b in (2 * qb, 2 * qb + 1):
            group_sum.send_core(b % 4, when=c != b // 4)

    for qb in range(4):
        rows = slice(qb * CH, qb * CH + CH)
        keys = CH * (qb + 1)
        ok = allowed(qb, keys)
        for h in range(2):
            scores = jnp.where(ok, dot_nt(q_rot[h, rows], k_rot[0:keys]) * SCALE, MASKED)
            top = jnp.max(scores, axis=-1, keepdims=True)
            terms = jnp.exp(scores - top)
            total = jnp.sum(terms, axis=-1, keepdims=True)
            lse[h, rows] = top + jnp.log(total)
            weights = (terms * (1.0 / total)).astype(BF)
            mixed[rows, 128 * h : 128 * h + 128] = dot(weights, vals[0:keys]).astype(BF)
        p1[rows] = dot_nt(mixed[rows], wo[...]).astype(BF)
        send_chunk(sum_1, qb)
        if qb == 1:
            gather_m.third()

    for k in (2, 1, 3, 0):
        sum_1.cross(k)
    gather_og.far()
    sum_1.relay()
    gather_m.finish()
    for k in range(4):
        gather_og.core(k)

    def grad_act_chunk(i, carry):
        rows = pl.ds(pl.multiple_of(i * CH, CH), CH)
        grad_act[rows] = dot(ogs[rows], wm[:, 768:1152])
        return carry

    lax.fori_loop(0, 4, grad_act_chunk, 0)

    mid = xs[own].astype(F32) + sum_1.total()
    middle[...] = mid
    r_two = lax.rsqrt(jnp.mean(mid * mid, axis=-1, keepdims=True) + EPS)
    h2[own_z] = (mid * r_two * gain_two[0:1]).astype(BF)
    gather_h2.begin()

    def mlp_chunk(k):
        gather_h2.core(k)
        at = (z + k) % 4
        rows = pl.ds(pl.multiple_of(at * CH, CH), CH)
        pre = dot(h2[rows], wm[:, 0:768])
        gate, up = pre[:, 0:384], pre[:, 384:768]
        sig = 1.0 / (1.0 + jnp.exp(-gate))
        silu = gate * sig
        acted = (silu * up).astype(BF)
        act[rows] = acted
        grad = grad_act[rows]
        dgu[rows, 0:384] = (grad * up * (sig * (1.0 + gate * (1.0 - sig)))).astype(BF)
        dgu[rows, 384:768] = (grad * silu).astype(BF)
        p2[rows] = dot_nt(dgu[rows], wm[:, 0:768]).astype(BF)
        sum_2.send_core(at)

    def down_chunk(i, carry):
        rows = pl.ds(pl.multiple_of(i * CH, CH), CH)
        po[rows] = dot_nt(act[rows], wm[:, 768:1152]).astype(BF)
        return carry

    mlp_chunk(0)
    gather_h2.sides()
    mlp_chunk(3)
    mlp_chunk(1)
    sum_2.cross(3)
    sum_2.cross(1)
    gather_h2.far()
    mlp_chunk(2)
    sum_2.cross(2)
    sum_2.cross(0)

    lax.fori_loop(0, 4, down_chunk, 0)
    sum_2.relay()
    for k in range(4):
        sum_o.send_core(k)

    def mlp_weight_chunk(i, carry):
        cols = pl.ds(pl.multiple_of(i * CH, CH), CH)
        gm_full[cols, 0:768] = dot_tn(h2[:, cols], dgu[...]).astype(BF)
        gm_full[cols, 768:1152] = dot_tn(ogs[:, cols], act[...]).astype(BF)
        return carry

    lax.fori_loop(0, 4, mlp_weight_chunk, 0)
    weight_m.begin()

    err = sum_2.total()
    mid = middle[...]
    r_two = lax.rsqrt(jnp.mean(mid * mid, axis=-1, keepdims=True) + EPS)
    normed = mid * r_two
    part = jnp.sum(err * normed, axis=0, keepdims=True)
    gg[...] = jnp.zeros_like(gg)
    for k in range(8):
        gg[8 + k : 9 + k] = part[:, 128 * k : 128 * k + 128]
    scaled = err * gain_two[0:1]
    grad = ogs[own_z].astype(F32) + r_two * (
        scaled - normed * jnp.mean(scaled * normed, axis=-1, keepdims=True)
    )
    grad_mid[...] = grad
    gb[own] = grad.astype(BF)
    gather_gb.begin()
    dk[...] = jnp.zeros_like(dk)
    dv[...] = jnp.zeros_like(dv)
    gather_gb.sides()
    for k in (2, 1, 3, 0):
        sum_o.cross(k)
    weight_m.relay()
    gather_gb.far()
    for k in range(4):
        gather_gb.core(k)

    def out_weight_chunk(i, carry):
        cols = pl.ds(pl.multiple_of(i * CH, CH), CH)
        go_full[cols] = dot_tn(gb[:, cols], mixed[...]).astype(BF)
        return carry

    def back_rope(turned, pre, gain, cos, sin):
        r = lax.rsqrt(jnp.mean(pre * pre, axis=-1, keepdims=True) + EPS)
        normed = pre * r
        err = turned * cos - pltpu.roll(turned, 64, 1) * sin
        scaled = err * gain
        grad = r * (scaled - normed * jnp.mean(scaled * normed, axis=-1, keepdims=True))
        return grad, jnp.sum(err * normed, axis=0, keepdims=True)

    attn_part = jnp.zeros((1, WIDTH), F32)
    for qb in (3, 2, 1, 0):
        rows = slice(qb * CH, qb * CH + CH)
        keys = CH * (qb + 1)
        ok = allowed(qb, keys)
        cos, sin = cosine[rows], sine[rows]
        grad_mixed = dot(gb[rows], wo[...]).astype(BF)
        for h in range(2):
            grad_h = grad_mixed[:, 128 * h : 128 * h + 128]
            scores = jnp.where(ok, dot_nt(q_rot[h, rows], k_rot[0:keys]) * SCALE, MASKED)
            probs = jnp.exp(scores - lse[h, rows])
            grad_probs = dot_nt(grad_h, vals[0:keys])
            inner = jnp.sum(probs * grad_probs, axis=-1, keepdims=True)
            grad_scores = (probs * (grad_probs - inner)).astype(BF)
            dk[0:keys] += dot_tn(grad_scores, q_rot[h, rows]) * SCALE
            dv[0:keys] += dot_tn(probs.astype(BF), grad_h)
            grad_q = (dot(grad_scores, k_rot[0:keys]) * SCALE).astype(BF).astype(F32)
            pre = qk_pre[rows, 128 * h : 128 * h + 128]
            grad, gain_part = back_rope(grad_q, pre, query_gain[0:1], cos, sin)
            dqkv[rows, 128 * h : 128 * h + 128] = grad.astype(BF)
            gg[16:17] += gain_part
        grad_k = dk[rows].astype(BF).astype(F32)
        grad, gain_part = back_rope(grad_k, qk_pre[rows, 256:384], key_gain[0:1], cos, sin)
        dqkv[rows, 256:384] = grad.astype(BF)
        gg[17:18] += gain_part
        dqkv[rows, 384:512] = dv[rows].astype(BF)
        err = dot_nt(dqkv[rows], wq[...])
        p3[rows] = err.astype(BF)
        send_chunk(sum_3, qb)
        attn_part += jnp.sum(err * (xs[rows].astype(F32) * r1[rows]), axis=0, keepdims=True)
        if qb == 3:
            sum_o.relay()
        if qb == 2:
            weight_m.spread()

    for k in (2, 1, 3, 0):
        sum_3.cross(k)
    for k in range(8):
        gg[k : k + 1] = attn_part[:, 128 * k : 128 * k + 128]
    for dy, dc in column:
        links.send(gg, gg_y.at[y * 2 + c], place.at(dy=dy, dc=dc), gg_y_id + y * 2 + c)

    def attn_weight_chunk(i, carry):
        cols = pl.ds(pl.multiple_of(i * CH, CH), CH)
        gq_full[cols] = dot_tn(h1[:, cols], dqkv[...]).astype(BF)
        return carry

    lax.fori_loop(0, 4, attn_weight_chunk, 0)
    weight_q.begin()
    sum_3.relay()
    lax.fori_loop(0, 4, out_weight_chunk, 0)
    weight_o.begin()

    out_tmp[...] = (middle[...] + sum_o.total()).astype(BF)
    links.send(out_tmp, out_ref, place.swap, out_id, when=away)

    gg_y[y * 2 + c] = gg[...]
    for dy, dc in column:
        index = ((y + dy) % 4) * 2 + (c + dc) % 2
        links.wait(gg_y.at[index], place.at(dy=dy, dc=dc), gg_y_id + index)
    total = gg_y[0]
    for k in range(1, 8):
        total = total + gg_y[k]
    gg_a[...] = total
    for k in range(1, 4):
        links.send(gg_a, gg_x.at[x], place.at(dx=k), gg_x_id + x)
    weight_q.relay()
    weight_o.relay()

    err = sum_3.total()
    r_one = r1[own]
    normed = xs[own].astype(F32) * r_one
    scaled = err * gain_one[0:1]
    in_grad_tmp[...] = (
        grad_mid[...]
        + r_one * (scaled - normed * jnp.mean(scaled * normed, axis=-1, keepdims=True))
    ).astype(BF)
    links.send(in_grad_tmp, in_grad_ref, place.swap, in_grad_id, when=away)

    gg_x[x] = gg_a[...]
    for k in range(1, 4):
        other = (x + k) % 4
        links.wait(gg_x.at[other], place.at(dx=k), gg_x_id + other)
    gg_b[...] = (gg_x[0] + gg_x[1]) + (gg_x[2] + gg_x[3])
    for k in range(1, 4):
        links.send(gg_b, gg_z.at[z], place.at(dz=k), gg_z_id + z)

    weight_q.spread()
    weight_o.spread()
    weight_m.finish()

    @pl.when(home)
    def _():
        out_ref[...] = out_tmp[...]
        in_grad_ref[...] = in_grad_tmp[...]

    gg_z[z] = gg_b[...]
    for k in range(1, 4):
        other = (z + k) % 4
        links.wait(gg_z.at[other], place.at(dz=k), gg_z_id + other)
    gains_ref[...] = (gg_z[0] + gg_z[1]) + (gg_z[2] + gg_z[3])

    weight_q.finish()
    weight_o.finish()
    links.wait(out_ref, place.swap, out_id, when=away)
    links.wait(in_grad_ref, place.swap, in_grad_id, when=away)
    links.drain()


def run_layer(*args):
    vmem = pl.BlockSpec(memory_space=pltpu.VMEM)

    def sds(shape, kind):
        return jax.ShapeDtypeStruct(shape, kind)

    def buf(shape, kind=BF):
        return pltpu.VMEM(shape, kind)

    group = (GROUP, WIDTH)
    table = (GROUP, HEAD)
    block = (TOK, WIDTH)
    landing = [buf(group), buf((4, TOK, WIDTH)), buf((8, 64, WIDTH))]
    gains = (24, 128)

    def weight_landing(cols):
        return [buf((WIDTH, cols)), buf((10, 128, cols)), buf((4, 64, cols))]

    scratch = [
        buf((WIDTH, NQ)),
        buf((WIDTH, NO)),
        buf((WIDTH, NM)),
        buf((16, 8, 128), F32),
        buf((1, WIDTH), F32),
        buf((1, WIDTH), F32),
        buf(table, F32),
        buf((GROUP, 1), jnp.int32),
        buf(table, F32),
        buf(table, F32),
        buf(group),
        buf(group),
        buf(group),
        buf((GROUP, 1), F32),
        buf((GROUP, 384), F32),
        buf((2, GROUP, HEAD)),
        buf(table),
        buf(table),
        buf((GROUP, 256)),
        buf((2, GROUP, 1), F32),
        *landing,
        buf(block, F32),
        buf(group),
        buf((GROUP, 384), F32),
        buf((GROUP, 384)),
        buf((GROUP, 768)),
        *landing,
        *landing,
        buf(group),
        buf(block, F32),
        buf(table, F32),
        buf(table, F32),
        buf((GROUP, 512)),
        *landing,
        *weight_landing(NM),
        *weight_landing(NQ),
        *weight_landing(NO),
        buf(block),
        buf(block),
        buf(gains, F32),
        buf((8, *gains), F32),
        buf(gains, F32),
        buf((4, *gains), F32),
        buf(gains, F32),
        buf((4, *gains), F32),
        pltpu.SemaphoreType.DMA((N_SEMS,)),
        pltpu.SemaphoreType.DMA((N_SEMS,)),
    ]
    return pl.pallas_call(
        layer_kernel,
        out_shape=(
            sds(block, BF),
            sds(block, BF),
            sds((64, NQ), F32),
            sds((64, NO), F32),
            sds((64, NM), F32),
            sds(gains, F32),
        ),
        in_specs=[vmem] * len(args),
        out_specs=(vmem,) * 6,
        scratch_shapes=scratch,
        name="layer",
        compiler_params=pltpu.CompilerParams(
            collective_id=0, has_side_effects=True, vmem_limit_bytes=63 * 2**20
        ),
    )(*args)


def tables(lengths):
    ends = jnp.cumsum(lengths)
    begins = ends - lengths
    at = jnp.arange(GROUP, dtype=jnp.int32)
    label = jnp.sum((at[:, None] >= ends[None, :]).astype(jnp.int32), axis=1)
    chosen = label[:, None] == jnp.arange(lengths.shape[0], dtype=jnp.int32)[None, :]
    starts = jnp.sum(jnp.where(chosen, begins[None, :], 0), axis=1)
    half = HEAD // 2
    frequency = ROPE_BASE ** (-(jnp.arange(half).astype(F32) * 2.0 / HEAD))
    angles = (at - starts).astype(F32)[:, None] * frequency[None, :]
    cos, sin = jnp.cos(angles), jnp.sin(angles)
    return jnp.concatenate([cos, sin], axis=-1), starts[:, None]


def per_device(
    layer_input,
    seq_lengths,
    attn_gain,
    w_query,
    key_projection,
    value_projection,
    query_gain,
    key_gain,
    w_out,
    mlp_gain,
    w_gate,
    w_up,
    w_down,
    out_grad,
):
    trig, starts = tables(seq_lengths[0])
    wq_own = jnp.concatenate([w_query, key_projection, value_projection], axis=1)
    wm_own = jnp.concatenate([w_gate, w_up, w_down.T], axis=1)
    gain_own = jnp.broadcast_to(jnp.concatenate([attn_gain, mlp_gain]).astype(F32)[None], (8, 128))
    out, in_grad, gq, go, gm, gains = run_layer(
        wq_own,
        w_out.T,
        wm_own,
        gain_own,
        layer_input,
        out_grad,
        query_gain.astype(F32)[None],
        key_gain.astype(F32)[None],
        trig,
        starts,
    )
    piece = attn_gain.shape[0]
    first = lax.axis_index("dp") * piece
    grad_attn_gain = lax.dynamic_slice_in_dim(gains[0:8].reshape(-1), first, piece, 0)
    grad_mlp_gain = lax.dynamic_slice_in_dim(gains[8:16].reshape(-1), first, piece, 0)
    return (
        out,
        in_grad,
        grad_attn_gain,
        gq[:, 0:256],
        gq[:, 256:384],
        gq[:, 384:512],
        gains[16],
        gains[17],
        go.T,
        grad_mlp_gain,
        gm[:, 0:384],
        gm[:, 384:768],
        gm[:, 768:1152].T,
    )


def solution(mesh):
    both = P(("dp", "tensor"), None)
    split = P("dp", "tensor")
    turned = P("tensor", "dp")
    in_specs = (
        both,
        P("dp", None),
        P("dp"),
        split,
        split,
        split,
        P(),
        P(),
        turned,
        P("dp"),
        split,
        split,
        turned,
        both,
    )
    out_specs = (both, both, P("dp"), split, split, split, P(), P(), turned, P("dp"), split, split, turned)
    return jax.shard_map(
        per_device, mesh=mesh, in_specs=in_specs, out_specs=out_specs, check_vma=False
    )
```

```python
import functools

import jax
import jax.numpy as jnp
from jax import lax
from jax.experimental import pallas as pl
from jax.experimental.pallas import tpu as pltpu
from jax.sharding import PartitionSpec as P

MESH = pl.DeviceIdType.MESH
BF = jnp.bfloat16
F32 = jnp.float32
HEAD = 128
EPS = 1e-06
ROPE_BASE = 1000000.0
MASKED = -1e30
SCALE = HEAD ** (-0.5)
TOK = 128
GROUP = 1024
WIDTH = 1024
NQ = 512
NO = 256
NU = 768
ND = 384
CH = 256
N_SEMS = 240


def dot(a, b):
    return jnp.dot(a, b, preferred_element_type=F32)


def dot_nt(a, b):
    return lax.dot_general(a, b, (((1,), (1,)), ((), ())), preferred_element_type=F32)


def dot_tn(a, b):
    return lax.dot_general(a, b, (((0,), (0,)), ((), ())), preferred_element_type=F32)


class Links:
    def __init__(self, send_sems, recv_sems):
        self.send_sems, self.recv_sems = send_sems, recv_sems
        self.sends, self.recvs = 0, 0
        self.pending = []

    def recv_ids(self, count=1):
        first = self.recvs
        self.recvs += count
        assert self.recvs <= N_SEMS
        return first

    def copy(self, src, dst, device, send_id, recv_id):
        return pltpu.make_async_remote_copy(
            src_ref=src,
            dst_ref=dst,
            send_sem=self.send_sems.at[send_id],
            recv_sem=self.recv_sems.at[recv_id],
            device_id=device,
            device_id_type=MESH,
        )

    def send(self, src, dst, device, recv_id, when=None):
        copy = self.copy(src, dst, device, self.sends, recv_id)
        self.sends += 1
        assert self.sends <= N_SEMS
        if when is None:
            copy.start()
        else:
            pl.when(when)(copy.start)
        self.pending.append((copy, when))

    def wait(self, dst, device, recv_id, when=None):
        copy = self.copy(dst, dst, device, 0, recv_id)
        if when is None:
            copy.wait_recv()
        else:
            pl.when(when)(copy.wait_recv)

    def drain(self):
        for copy, when in self.pending:
            if when is None:
                copy.wait_send()
            else:
                pl.when(when)(copy.wait_send)


class Place:
    def __init__(self):
        d, t = lax.axis_index("dp"), lax.axis_index("tensor")
        self.d = d
        self.x, self.c = d // 4, d % 2
        self.y, self.z = (t // 4) * 2 + (d // 2) % 2, t % 4
        self.home = self.c == t // 4
        self.left_z, self.right_z = self.at(dz=3), self.at(dz=1)
        self.left_x, self.right_x = self.at(dx=3), self.at(dx=1)
        self.core = self.at(dc=1)
        self.swap = self.at(dy=2, dc=1)

    def device(self, x, y, z, c):
        return (x * 4 + (y % 2) * 2 + c, (y // 2) * 4 + z)

    def at(self, dx=0, dy=0, dz=0, dc=0):
        return self.device((self.x + dx) % 4, (self.y + dy) % 4, (self.z + dz) % 4, (self.c + dc) % 2)


class WeightGather:
    def __init__(self, links, place, own, buf):
        self.links, self.place, self.own, self.buf = links, place, own, buf
        self.y_id = links.recv_ids(4)
        self.ids = {name: links.recv_ids() for name in ("xm", "xp", "l", "r")}

    def block(self, index):
        return self.buf.at[pl.ds(pl.multiple_of(index * 64, 64), 64)]

    def rows(self, dx, half=None):
        first = ((self.place.x + dx) % 4) * 256
        if half is None:
            return self.buf.at[pl.ds(pl.multiple_of(first, 256), 256)]
        return self.buf.at[pl.ds(pl.multiple_of(first + 128 * half, 128), 128)]

    def begin(self):
        place, links = self.place, self.links
        side = place.y // 2
        for dy in (2, 1, 3, 0):
            device = place.device(place.x, (place.y + dy) % 4, place.z, side)
            links.send(
                self.own,
                self.block(place.d),
                device,
                self.y_id + place.d % 4,
                when=(place.c != side) if dy == 0 else None,
            )

        @pl.when(place.c == side)
        def _():
            self.block(place.d)[...] = self.own[...]

    def second(self):
        place, links = self.place, self.links
        for low in range(2):
            for core in range(2):
                y = 2 * place.c + low
                links.wait(
                    self.block(place.x * 4 + low * 2 + core),
                    place.device(place.x, y, place.z, core),
                    self.y_id + low * 2 + core,
                    when=(y != place.y) | (core != place.c),
                )
        mine = self.rows(0)
        links.send(mine, mine, place.right_x, self.ids["xm"])
        links.send(mine, mine, place.left_x, self.ids["xp"])

    def third(self):
        place, links = self.place, self.links
        links.wait(self.rows(3), place.left_x, self.ids["xm"])
        half = self.rows(3, 0)
        links.send(half, half, place.right_x, self.ids["l"])
        links.wait(self.rows(1), place.right_x, self.ids["xp"])
        half = self.rows(1, 1)
        links.send(half, half, place.left_x, self.ids["r"])

    def finish(self):
        place, links = self.place, self.links
        links.wait(self.rows(2, 0), place.left_x, self.ids["l"])
        links.wait(self.rows(2, 1), place.right_x, self.ids["r"])


class WeightSum:
    def __init__(self, links, place, full, side, land, out):
        self.links, self.place, self.full = links, place, full
        self.side, self.land, self.out = side, land, out
        self.ids = {n: links.recv_ids() for n in ("la", "lr", "ra", "rr", "lc", "rc")}
        self.y_id = links.recv_ids(4)

    def rows(self, dx, half):
        return pl.ds(pl.multiple_of(((self.place.x + dx) % 4) * 256 + 128 * half, 128), 128)

    def begin(self):
        place, links, side = self.place, self.links, self.side
        links.send(self.full.at[self.rows(2, 0)], side.at[0], place.right_x, self.ids["la"])
        links.send(self.full.at[self.rows(2, 1)], side.at[2], place.left_x, self.ids["ra"])
        links.send(self.full.at[self.rows(1, 1)], side.at[1], place.right_x, self.ids["lr"])
        links.send(self.full.at[self.rows(3, 0)], side.at[3], place.left_x, self.ids["rr"])

    def relay(self):
        place, links, side = self.place, self.links, self.side
        links.wait(side.at[0], place.left_x, self.ids["la"])
        side[6] = (self.full[self.rows(1, 0)].astype(F32) + side[0].astype(F32)).astype(BF)
        links.send(side.at[6], side.at[4], place.right_x, self.ids["lc"])
        links.wait(side.at[2], place.right_x, self.ids["ra"])
        side[7] = (self.full[self.rows(3, 1)].astype(F32) + side[2].astype(F32)).astype(BF)
        links.send(side.at[7], side.at[5], place.left_x, self.ids["rc"])

    def gathered(self):
        place, links, side = self.place, self.links, self.side
        links.wait(side.at[1], place.left_x, self.ids["lr"])
        links.wait(side.at[3], place.right_x, self.ids["rr"])
        links.wait(side.at[4], place.left_x, self.ids["lc"])
        links.wait(side.at[5], place.right_x, self.ids["rc"])
        for half, first, other in ((0, 4, 3), (1, 5, 1)):
            side[8 + half] = (
                self.full[self.rows(0, half)].astype(F32)
                + side[first].astype(F32)
                + side[other].astype(F32)
            ).astype(BF)

    def spread(self):
        self.gathered()
        place, links, side = self.place, self.links, self.side
        for low in range(2):
            for core in range(2):
                y = 2 * place.c + low
                away = (y != place.y) | (core != place.c)
                piece = side.at[8 + low, pl.ds(64 * core, 64)]
                links.send(
                    piece,
                    self.land.at[place.y],
                    place.device(place.x, y, place.z, core),
                    self.y_id + place.y,
                    when=away,
                )

                @pl.when(jnp.logical_not(away))
                def _():
                    self.land[place.y] = piece[...]

    def finish(self):
        place, links = self.place, self.links
        core = place.y // 2
        for k in range(4):
            y = (place.y + k) % 4
            links.wait(
                self.land.at[y],
                place.device(place.x, y, place.z, core),
                self.y_id + y,
                when=(place.c != core) if k == 0 else None,
            )
        total = self.land[0].astype(F32)
        for y in range(1, 4):
            total = total + self.land[y].astype(F32)
        self.out[...] = total


class WeightSumDirect(WeightSum):
    def begin(self):
        place = self.place
        for k, name in ((2, "ra"), (1, "la"), (3, "lr")):
            self.links.send(
                self.full.at[pl.ds(((place.x + k) % 4) * 2, 2)],
                self.side.at[pl.ds(2 * (k - 1), 2)],
                place.at(dx=k),
                self.ids[name],
            )

    def gathered(self):
        place, side = self.place, self.side
        for k, name in ((1, "la"), (3, "lr"), (2, "ra")):
            self.links.wait(side.at[pl.ds(2 * (k - 1), 2)], place.at(dx=4 - k), self.ids[name])
        for half in range(2):
            total = self.full[place.x * 2 + half].astype(F32)
            for k in range(3):
                total = total + side[2 * k + half].astype(F32)
            side[8 + half] = total.astype(BF)


class WeightGatherX:
    def __init__(self, links, place, own, stage, buf):
        self.links, self.place, self.own, self.stage, self.buf = links, place, own, stage, buf
        self.y_id = links.recv_ids(4)
        self.ids = {name: links.recv_ids() for name in ("xm", "xp", "l", "r")}

    def block(self, dx, half=None):
        at = (self.place.x + dx) % 4
        if half is None:
            return self.stage.at[at]
        return self.stage.at[at, pl.ds(32 * half, 32)]

    def begin(self):
        place, links = self.place, self.links
        links.send(self.own, self.block(0), place.right_x, self.ids["xm"])
        links.send(self.own, self.block(0), place.left_x, self.ids["xp"])
        self.stage[place.x] = self.own[...]

    def relay(self):
        place, links = self.place, self.links
        links.wait(self.block(3), place.left_x, self.ids["xm"])
        links.send(self.block(3, 0), self.block(3, 0), place.right_x, self.ids["l"])
        links.wait(self.block(1), place.right_x, self.ids["xp"])
        links.send(self.block(1, 1), self.block(1, 1), place.left_x, self.ids["r"])

    def spread(self):
        place, links = self.place, self.links
        links.wait(self.block(2, 0), place.left_x, self.ids["l"])
        links.wait(self.block(2, 1), place.right_x, self.ids["r"])
        side = place.y // 2
        for dy in (2, 1, 3, 0):
            links.send(
                self.stage,
                self.buf.at[:, place.d % 4],
                place.device(place.x, (place.y + dy) % 4, place.z, side),
                self.y_id + place.d % 4,
                when=(place.c != side) if dy == 0 else None,
            )

        @pl.when(place.c == side)
        def _():
            self.buf[:, place.d % 4] = self.stage[...]

    def finish(self):
        place, links = self.place, self.links
        for low in range(2):
            for core in range(2):
                y = 2 * place.c + low
                links.wait(
                    self.buf.at[:, low * 2 + core],
                    place.device(place.x, y, place.z, core),
                    self.y_id + low * 2 + core,
                    when=(y != place.y) | (core != place.c),
                )


class WeightSumY:
    def __init__(self, links, place, full, land, total, side, last, out):
        self.links, self.place, self.full, self.land = links, place, full, land
        self.total, self.side, self.last, self.out = total, side, last, out
        self.y_id = links.recv_ids(4)
        self.ids = {n: links.recv_ids() for n in ("la", "lr", "ra", "rr", "lc", "rc", "core")}
        self.active = place.c == place.y // 2

    def begin(self):
        place = self.place
        for low in range(2):
            y = 2 * place.c + low
            self.links.send(
                self.full.at[:, pl.ds(2 * low, 2)],
                self.land.at[place.y],
                place.device(place.x, y, place.z, place.c),
                self.y_id + place.y,
                when=y != place.y,
            )

    def cross(self):
        place, links, side, active = self.place, self.links, self.side, self.active
        x = place.x
        for k in range(1, 4):
            y = (place.y + k) % 4
            links.wait(
                self.land.at[y], place.device(x, y, place.z, place.c), self.y_id + y, when=active
            )

        @pl.when(active)
        def _():
            def add(i, carry):
                acc = self.full[i, pl.ds((place.y % 2) * 2, 2)].astype(F32)
                for k in range(1, 4):
                    acc = acc + self.land[(place.y + k) % 4, i].astype(F32)
                self.total[i] = acc.astype(BF)
                return carry

            lax.fori_loop(0, 4, add, 0)

        self.ring()

    def ring(self):
        links, place, active, side, x = self.links, self.place, self.active, self.side, self.place.x
        total, ids = self.total, self.ids
        links.send(total.at[(x + 2) % 4, 0], side.at[0], place.right_x, ids["la"], when=active)
        links.send(total.at[(x + 2) % 4, 1], side.at[2], place.left_x, ids["ra"], when=active)
        links.send(total.at[(x + 1) % 4, 1], side.at[1], place.right_x, ids["lr"], when=active)
        links.send(total.at[(x + 3) % 4, 0], side.at[3], place.left_x, ids["rr"], when=active)

    def relay(self):
        place, links, side, ids, active = self.place, self.links, self.side, self.ids, self.active
        x = place.x
        links.wait(side.at[0], place.left_x, ids["la"], when=active)
        links.wait(side.at[2], place.right_x, ids["ra"], when=active)

        @pl.when(active)
        def _():
            side[6] = (self.total[(x + 1) % 4, 0].astype(F32) + side[0].astype(F32)).astype(BF)
            side[7] = (self.total[(x + 3) % 4, 1].astype(F32) + side[2].astype(F32)).astype(BF)

        links.send(side.at[6], side.at[4], place.right_x, ids["lc"], when=active)
        links.send(side.at[7], side.at[5], place.left_x, ids["rc"], when=active)

    def spread(self):
        place, links, side, ids, active = self.place, self.links, self.side, self.ids, self.active
        x = place.x
        links.wait(side.at[1], place.left_x, ids["lr"], when=active)
        links.wait(side.at[3], place.right_x, ids["rr"], when=active)
        links.wait(side.at[4], place.left_x, ids["lc"], when=active)
        links.wait(side.at[5], place.right_x, ids["rc"], when=active)

        self.deliver(((4, 3), (5, 1)))

    def deliver(self, slots):
        place, links, side, ids, active = self.place, self.links, self.side, self.ids, self.active
        x = place.x

        @pl.when(active)
        def _():
            sums = []
            for half in range(2):
                total = self.total[x, half].astype(F32)
                for slot in slots[half]:
                    total = total + side[slot].astype(F32)
                sums.append(total)
            zero, one = sums
            self.out[...] = jnp.where(place.c == 0, zero, one)
            side[8] = jnp.where(place.c == 0, one, zero).astype(BF)

        links.send(side.at[8], self.last, place.core, ids["core"], when=active)

    def finish(self):
        idle = jnp.logical_not(self.active)
        self.links.wait(self.last, self.place.core, self.ids["core"], when=idle)

        @pl.when(idle)
        def _():
            self.out[...] = self.last[...].astype(F32)


class WeightSumYDirect(WeightSumY):
    def ring(self):
        place = self.place
        for k, name in ((2, "ra"), (1, "la"), (3, "lr")):
            self.links.send(
                self.total.at[(place.x + k) % 4],
                self.side.at[pl.ds(2 * (k - 1), 2)],
                place.at(dx=k),
                self.ids[name],
                when=self.active,
            )

    def spread(self):
        for k, name in ((1, "la"), (3, "lr"), (2, "ra")):
            self.links.wait(
                self.side.at[pl.ds(2 * (k - 1), 2)],
                self.place.at(dx=4 - k),
                self.ids[name],
                when=self.active,
            )
        self.deliver(((0, 2, 4), (1, 3, 5)))


def token_rows(c, z, by_z):
    index = z * 2 + c if by_z else c * 4 + z
    return pl.multiple_of(index * TOK, TOK)


class TokenSum:
    def __init__(self, links, place, partial, core_in, side, by_z):
        self.links, self.place, self.partial = links, place, partial
        self.core_in, self.side, self.by_z = core_in, side, by_z
        self.core_id = links.recv_ids(4)
        self.ids = {n: links.recv_ids() for n in ("la", "lr", "ra", "rr", "lc", "rc")}

    def rows(self, c, z):
        return pl.ds(token_rows(c, z, self.by_z), TOK)

    def send_core(self, z, when=None):
        place = self.place
        self.links.send(
            self.partial.at[self.rows((place.c + 1) % 2, z)],
            self.core_in.at[z],
            place.core,
            self.core_id + z,
            when=when,
        )

    def half(self, z, h):
        return pl.ds(token_rows(self.place.c, z, self.by_z) + 64 * h, 64)

    def cross(self, k, when=None):
        place, links, side, ids = self.place, self.links, self.side, self.ids
        z = (place.z + k) % 4
        links.wait(self.core_in.at[z], place.core, self.core_id + z, when=when)

        def add():
            rows = self.rows(place.c, z)
            self.partial[rows] = (
                self.partial[rows].astype(F32) + self.core_in[z].astype(F32)
            ).astype(BF)

        if when is None:
            add()
        else:
            pl.when(when)(add)
        low, high = self.partial.at[self.half(z, 0)], self.partial.at[self.half(z, 1)]
        if k == 2:
            links.send(low, side.at[0], place.right_z, ids["la"], when=when)
            links.send(high, side.at[2], place.left_z, ids["ra"], when=when)
        if k == 1:
            links.send(high, side.at[1], place.right_z, ids["lr"], when=when)
        if k == 3:
            links.send(low, side.at[3], place.left_z, ids["rr"], when=when)

    def relay(self):
        place, links, side = self.place, self.links, self.side
        z = place.z
        links.wait(side.at[0], place.left_z, self.ids["la"])
        side[6] = (self.partial[self.half((z + 1) % 4, 0)].astype(F32) + side[0].astype(F32)).astype(BF)
        links.send(side.at[6], side.at[4], place.right_z, self.ids["lc"])
        links.wait(side.at[2], place.right_z, self.ids["ra"])
        side[7] = (self.partial[self.half((z + 3) % 4, 1)].astype(F32) + side[2].astype(F32)).astype(BF)
        links.send(side.at[7], side.at[5], place.left_z, self.ids["rc"])

    def total(self):
        place, links, side = self.place, self.links, self.side
        links.wait(side.at[1], place.left_z, self.ids["lr"])
        links.wait(side.at[3], place.right_z, self.ids["rr"])
        links.wait(side.at[4], place.left_z, self.ids["lc"])
        links.wait(side.at[5], place.right_z, self.ids["rc"])
        parts = []
        for half, first, other in ((0, 4, 3), (1, 5, 1)):
            parts.append(
                self.partial[self.half(place.z, half)].astype(F32)
                + side[first].astype(F32)
                + side[other].astype(F32)
            )
        return jnp.concatenate(parts, axis=0)


class TokenGather:
    def __init__(self, links, place, buf, by_z):
        self.links, self.place, self.buf, self.by_z = links, place, buf, by_z
        names = ("zm0", "zm1", "zp0", "zp1", "l", "r", "c0", "c1", "c2", "c3")
        self.ids = {name: links.recv_ids() for name in names}

    def rows(self, k, core=0, half=None):
        place = self.place
        first = token_rows((place.c + core) % 2, (place.z + k) % 4, self.by_z)
        if half is None:
            return self.buf.at[pl.ds(first, TOK)]
        return self.buf.at[pl.ds(first + 64 * half, 64)]

    def push(self, ref, device, name):
        self.links.send(ref, ref, device, self.ids[name])

    def begin(self):
        place = self.place
        self.push(self.rows(0, half=0), place.right_z, "zm0")
        self.push(self.rows(0, half=1), place.left_z, "zp1")
        self.push(self.rows(0), place.core, "c0")
        self.push(self.rows(0, half=1), place.right_z, "zm1")
        self.push(self.rows(0, half=0), place.left_z, "zp0")

    def sides(self):
        place, links, ids = self.place, self.links, self.ids
        links.wait(self.rows(3, half=0), place.left_z, ids["zm0"])
        self.push(self.rows(3, half=0), place.right_z, "l")
        links.wait(self.rows(1, half=1), place.right_z, ids["zp1"])
        self.push(self.rows(1, half=1), place.left_z, "r")
        links.wait(self.rows(3, half=1), place.left_z, ids["zm1"])
        self.push(self.rows(3), place.core, "c3")
        links.wait(self.rows(1, half=0), place.right_z, ids["zp0"])
        self.push(self.rows(1), place.core, "c1")

    def far(self):
        place = self.place
        self.links.wait(self.rows(2, half=0), place.left_z, self.ids["l"])
        self.links.wait(self.rows(2, half=1), place.right_z, self.ids["r"])
        self.push(self.rows(2), place.core, "c2")

    def core(self, k):
        self.links.wait(self.rows(k, core=1), self.place.core, self.ids["c%d" % k])


def layer_kernel(
    w_query,
    w_key,
    w_value,
    w_out,
    w_gate,
    w_up,
    w_down,
    gain_own,
    x_own,
    og_own,
    query_gain_in,
    key_gain_in,
    lengths_own,
    frequency,
    out_ref,
    in_grad_ref,
    gq_ref,
    gk_ref,
    go_ref,
    gu_ref,
    gd_ref,
    gains_ref,
    wq_own,
    wu_own,
    wo_stage,
    wd_stage,
    wq,
    wu,
    wo,
    wd,
    gain_in,
    gain_one,
    gain_two,
    lengths,
    starts,
    cosine,
    sine,
    xs,
    ogs,
    h1,
    r1,
    qk_pre,
    q_rot,
    k_rot,
    vals,
    mixed,
    probs_low,
    probs_high,
    p1,
    p1_core,
    p1_side,
    middle,
    h2,
    grad_act,
    act,
    dgu,
    p2,
    p2_core,
    p2_side,
    po,
    po_core,
    po_side,
    gb,
    grad_mid,
    dk,
    dv,
    dqkv,
    p3,
    p3_core,
    p3_side,
    gu_full,
    gu_side,
    gu_land,
    gq_full,
    gq_side,
    gq_land,
    gk_full,
    gk_land,
    gk_total,
    gk_side,
    gk_last,
    go_full,
    go_land,
    go_total,
    go_side,
    go_last,
    gd_full,
    gd_land,
    gd_total,
    gd_side,
    gd_last,
    out_tmp,
    in_grad_tmp,
    gg,
    gg_y,
    gg_a,
    gg_x,
    gg_b,
    gg_z,
    send_sems,
    recv_sems,
):
    links = Links(send_sems, recv_sems)
    place = Place()
    x, y, z, c = place.x, place.y, place.z, place.c
    home, away = place.home, jnp.logical_not(place.home)
    own = pl.ds(token_rows(c, z, False), TOK)
    own_z = pl.ds(token_rows(c, z, True), TOK)
    swap_own = pl.ds(token_rows((c + 1) % 2, z, False), TOK)
    swap_z = pl.ds(token_rows((c + 1) % 2, z, True), TOK)
    column = [(dy, dc) for dy in range(4) for dc in range(2) if dy or dc]

    barrier = pltpu.get_barrier_semaphore()
    for peer in (
        [place.at(dy=dy, dc=dc) for dy, dc in column]
        + [place.at(dx=k) for k in range(1, 4)]
        + [place.at(dz=k) for k in range(1, 4)]
    ):
        pl.semaphore_signal(barrier, inc=1, device_id=peer, device_id_type=MESH)

    gather_q = WeightGather(links, place, wq_own, wq)
    gather_u = WeightGather(links, place, wu_own, wu)
    gather_o = WeightGatherX(links, place, w_out, wo_stage, wo)
    gather_d = WeightGatherX(links, place, w_down, wd_stage, wd)
    gather_x = TokenGather(links, place, xs, False)
    gather_og = TokenGather(links, place, ogs, True)
    gather_h2 = TokenGather(links, place, h2, True)
    gather_gb = TokenGather(links, place, gb, False)
    sum_1 = TokenSum(links, place, p1, p1_core, p1_side, False)
    sum_2 = TokenSum(links, place, p2, p2_core, p2_side, True)
    sum_o = TokenSum(links, place, po, po_core, po_side, True)
    sum_3 = TokenSum(links, place, p3, p3_core, p3_side, False)
    weight_u = WeightSum(links, place, gu_full, gu_side, gu_land, gu_ref)
    weight_q = WeightSumDirect(links, place, gq_full, gq_side, gq_land, gq_ref)
    weight_k = WeightSumYDirect(links, place, gk_full, gk_land, gk_total, gk_side, gk_last, gk_ref)
    weight_o = WeightSumY(links, place, go_full, go_land, go_total, go_side, go_last, go_ref)
    weight_d = WeightSumY(links, place, gd_full, gd_land, gd_total, gd_side, gd_last, gd_ref)
    x_id, og_id, lengths_id, out_id, in_grad_id = [links.recv_ids() for _ in range(5)]
    gain_id, gain_x_id = links.recv_ids(4), links.recv_ids(4)
    gg_y_id, gg_x_id, gg_z_id = links.recv_ids(8), links.recv_ids(4), links.recv_ids(4)

    @pl.when(home)
    def _():
        xs[own] = x_own[...]
        ogs[own_z] = og_own[...]
        lengths[...] = lengths_own[...]

    wq_own[:, 0:256] = w_query[...]
    wq_own[:, 256:384] = w_key[...]
    wq_own[:, 384:512] = w_value[...]
    wu_own[:, 0:384] = w_gate[...]
    wu_own[:, 384:768] = w_up[...]
    gain_in[place.d] = jnp.broadcast_to(gain_own[...], (8, 128))
    query_gain, key_gain = query_gain_in[...].astype(F32), key_gain_in[...].astype(F32)

    pl.semaphore_wait(barrier, 13)

    links.send(x_own, xs.at[swap_own], place.swap, x_id, when=away)
    gather_o.begin()
    gather_d.begin()
    gather_q.begin()
    for dy, dc in ((0, 1), (1, 0), (1, 1)):
        other_y = (y // 2) * 2 + (y % 2 + dy) % 2
        peer = place.device(x, other_y, z, (c + dc) % 2)
        links.send(gain_in.at[place.d], gain_in.at[place.d], peer, gain_id + place.d % 4)
    links.send(lengths_own, lengths, place.core, lengths_id, when=home)

    links.wait(xs.at[own], place.swap, x_id, when=away)
    gather_x.begin()
    gather_o.relay()
    gather_d.relay()
    gather_q.second()
    for dy, dc in ((0, 1), (1, 0), (1, 1)):
        other_y = (y // 2) * 2 + (y % 2 + dy) % 2
        index = x * 4 + (other_y % 2) * 2 + (c + dc) % 2
        peer = place.device(x, other_y, z, (c + dc) % 2)
        links.wait(gain_in.at[index], peer, gain_id + index % 4)
    four = pl.ds(x * 4, 4)
    for k in range(1, 4):
        links.send(gain_in.at[four], gain_in.at[four], place.at(dx=k), gain_x_id + x)
    links.send(og_own, ogs.at[swap_z], place.swap, og_id, when=away)
    gather_o.spread()
    gather_u.begin()

    gather_x.sides()
    gather_q.third()
    gather_d.spread()
    for k in range(1, 4):
        other = (x + k) % 4
        links.wait(gain_in.at[pl.ds(other * 4, 4)], place.at(dx=k), gain_x_id + other)
    low = lax.broadcasted_iota(jnp.int32, (1, 128), 1) < 64
    for k in range(8):
        even, odd = gain_in[2 * k][0:1], gain_in[2 * k + 1][0:1]
        cols = slice(128 * k, 128 * k + 128)
        gain_one[0:1, cols] = jnp.where(low, even, pltpu.roll(odd, 64, 1))
        gain_two[0:1, cols] = jnp.where(low, pltpu.roll(even, 64, 1), odd)

    links.wait(lengths, place.core, lengths_id, when=away)

    def trig_chunk(i, carry):
        rows = pl.ds(pl.multiple_of(i * CH, CH), CH)
        at = lax.broadcasted_iota(jnp.int32, (CH, 1), 0) + i * CH
        end, start = jnp.zeros((1, 1), jnp.int32), jnp.zeros((CH, 1), jnp.int32)
        for k in range(3):
            end = end + lengths[0:1, k : k + 1]
            start = jnp.where(at >= end, end, start)
        starts[rows] = start
        angles = (at - start).astype(F32) * frequency[0:1]
        cosine[rows] = jnp.cos(angles)
        turned = jnp.sin(angles)
        sine[rows] = jnp.where(low, -turned, turned)
        return carry

    lax.fori_loop(0, 4, trig_chunk, 0)

    gather_x.far()
    for k in range(4):
        gather_x.core(k)
    def norm_chunk(i, carry):
        rows = pl.ds(pl.multiple_of(i * 128, 128), 128)
        wide = xs[rows].astype(F32)
        r = lax.rsqrt(jnp.mean(wide * wide, axis=-1, keepdims=True) + EPS)
        r1[rows] = r
        h1[rows] = (wide * r * gain_one[0:1]).astype(BF)
        return carry

    lax.fori_loop(0, 8, norm_chunk, 0)
    links.wait(ogs.at[own_z], place.swap, og_id, when=away)
    gather_og.begin()
    gather_q.finish()

    def qkv_chunk(i, carry):
        rows = pl.ds(pl.multiple_of(i * CH, CH), CH)
        pre = dot(h1[rows], wq[...])
        qk_pre[rows] = pre[:, 0:384]
        vals[rows] = pre[:, 384:512].astype(BF)
        cos, sin = cosine[rows], sine[rows]
        for h in range(3):
            part = pre[:, 128 * h : 128 * h + 128]
            r = lax.rsqrt(jnp.mean(part * part, axis=-1, keepdims=True) + EPS)
            scaled = part * r * (query_gain if h < 2 else key_gain)
            turned = (scaled * cos + pltpu.roll(scaled, 64, 1) * sin).astype(BF)
            if h < 2:
                q_rot[h, rows] = turned
            else:
                k_rot[rows] = turned
        return carry

    lax.fori_loop(0, 4, qkv_chunk, 0)
    gather_u.second()
    gather_o.finish()
    gather_og.sides()

    def allowed(qb, keys):
        key_at = lax.broadcasted_iota(jnp.int32, (CH, keys), 1)
        query_at = lax.broadcasted_iota(jnp.int32, (CH, keys), 0) + qb * CH
        return (key_at >= starts[qb * CH : qb * CH + CH]) & (key_at <= query_at)

    def probs_of(qb):
        return probs_low if qb < 2 else probs_high

    def probs_rows(qb):
        return slice((qb % 2) * CH, (qb % 2) * CH + CH)

    def send_chunk(group_sum, qb):
        for b in (2 * qb, 2 * qb + 1):
            group_sum.send_core(b % 4, when=c != b // 4)

    for qb in range(4):
        rows = slice(qb * CH, qb * CH + CH)
        keys = CH * (qb + 1)
        ok = allowed(qb, keys)
        for h in range(2):
            scores = jnp.where(ok, dot_nt(q_rot[h, rows], k_rot[0:keys]) * SCALE, MASKED)
            top = jnp.max(scores, axis=-1, keepdims=True)
            terms = jnp.exp(scores - top)
            total = jnp.sum(terms, axis=-1, keepdims=True)
            weights = (terms * (1.0 / total)).astype(BF)
            probs_of(qb)[h, probs_rows(qb), 0:keys] = weights
            mixed[rows, 128 * h : 128 * h + 128] = dot(weights, vals[0:keys]).astype(BF)
        p1[rows] = dot_nt(mixed[rows], wo[...].reshape(WIDTH, 256)).astype(BF)
        send_chunk(sum_1, qb)
        if qb == 2:
            for k in (2, 1, 3):
                sum_1.cross(k, when=c == 0)

    for k in (2, 1, 3):
        sum_1.cross(k, when=c == 1)
    sum_1.cross(0)
    gather_u.third()
    gather_og.far()
    sum_1.relay()

    mid = xs[own].astype(F32) + sum_1.total()
    middle[...] = mid
    r_two = lax.rsqrt(jnp.mean(mid * mid, axis=-1, keepdims=True) + EPS)
    h2[own_z] = (mid * r_two * gain_two[0:1]).astype(BF)
    gather_h2.begin()
    gather_d.finish()
    for k in range(4):
        gather_og.core(k)

    def grad_act_chunk(i, carry):
        rows = pl.ds(pl.multiple_of(i * CH, CH), CH)
        grad_act[rows] = dot(ogs[rows], wd[...].reshape(WIDTH, 384))
        return carry

    lax.fori_loop(0, 4, grad_act_chunk, 0)

    def mlp_chunk(k):
        gather_h2.core(k)
        at = (z + k) % 4
        rows = pl.ds(pl.multiple_of(at * CH, CH), CH)
        pre = dot(h2[rows], wu[...])
        gate, up = pre[:, 0:384], pre[:, 384:768]
        sig = 1.0 / (1.0 + jnp.exp(-gate))
        silu = gate * sig
        acted = (silu * up).astype(BF)
        act[rows] = acted
        grad = grad_act[rows]
        dgu[rows, 0:384] = (grad * up * (sig * (1.0 + gate * (1.0 - sig)))).astype(BF)
        dgu[rows, 384:768] = (grad * silu).astype(BF)
        p2[rows] = dot_nt(dgu[rows], wu[...]).astype(BF)
        sum_2.send_core(at)

    def down_chunk(i, carry):
        rows = pl.ds(pl.multiple_of(i * CH, CH), CH)
        po[rows] = dot_nt(act[rows], wd[...].reshape(WIDTH, 384)).astype(BF)
        return carry

    gather_u.finish()
    mlp_chunk(0)
    gather_h2.sides()
    mlp_chunk(3)
    mlp_chunk(1)
    sum_2.cross(3)
    sum_2.cross(1)
    gather_h2.far()
    mlp_chunk(2)
    sum_2.cross(2)
    sum_2.cross(0)

    lax.fori_loop(0, 4, down_chunk, 0)
    sum_2.relay()
    for k in range(4):
        sum_o.send_core(k)

    def mlp_weight_chunk(i, carry):
        cols = pl.ds(pl.multiple_of(i * CH, CH), CH)
        gu_full[cols] = dot_tn(h2[:, cols], dgu[...]).astype(BF)
        gd_full[i] = dot_tn(ogs[:, cols], act[...]).astype(BF).reshape(4, 64, 384)
        return carry

    lax.fori_loop(0, 4, mlp_weight_chunk, 0)
    weight_u.begin()
    weight_d.begin()

    err = sum_2.total()
    mid = middle[...]
    r_two = lax.rsqrt(jnp.mean(mid * mid, axis=-1, keepdims=True) + EPS)
    normed = mid * r_two
    part = jnp.sum(err * normed, axis=0, keepdims=True)
    gg[...] = jnp.zeros_like(gg)
    for k in range(8):
        gg[8 + k : 9 + k] = part[:, 128 * k : 128 * k + 128]
    scaled = err * gain_two[0:1]
    grad = ogs[own_z].astype(F32) + r_two * (
        scaled - normed * jnp.mean(scaled * normed, axis=-1, keepdims=True)
    )
    grad_mid[...] = grad
    gb[own] = grad.astype(BF)
    gather_gb.begin()
    dk[...] = jnp.zeros_like(dk)
    dv[...] = jnp.zeros_like(dv)
    gather_gb.sides()
    for k in (2, 1, 3, 0):
        sum_o.cross(k)
    weight_u.relay()
    weight_d.cross()
    gather_gb.far()
    for k in range(4):
        gather_gb.core(k)

    def out_weight_chunk(i, carry):
        cols = pl.ds(pl.multiple_of(i * CH, CH), CH)
        go_full[i] = dot_tn(gb[:, cols], mixed[...]).astype(BF).reshape(4, 64, 256)
        return carry

    def back_rope(turned, pre, gain, cos, sin):
        r = lax.rsqrt(jnp.mean(pre * pre, axis=-1, keepdims=True) + EPS)
        normed = pre * r
        err = turned * cos - pltpu.roll(turned, 64, 1) * sin
        scaled = err * gain
        grad = r * (scaled - normed * jnp.mean(scaled * normed, axis=-1, keepdims=True))
        return grad, jnp.sum(err * normed, axis=0, keepdims=True)

    lax.fori_loop(0, 4, out_weight_chunk, 0)
    weight_o.begin()

    attn_part = jnp.zeros((1, WIDTH), F32)
    for qb in (3, 2, 1, 0):
        rows = slice(qb * CH, qb * CH + CH)
        keys = CH * (qb + 1)
        cos, sin = cosine[rows], sine[rows]
        grad_mixed = dot(gb[rows], wo[...].reshape(WIDTH, 256)).astype(BF)
        for h in range(2):
            grad_h = grad_mixed[:, 128 * h : 128 * h + 128]
            weights = probs_of(qb)[h, probs_rows(qb), 0:keys]
            wide = weights.astype(F32)
            grad_probs = dot_nt(grad_h, vals[0:keys])
            inner = jnp.sum(wide * grad_probs, axis=-1, keepdims=True)
            grad_scores = (wide * (grad_probs - inner)).astype(BF)
            dk[0:keys] += dot_tn(grad_scores, q_rot[h, rows]) * SCALE
            dv[0:keys] += dot_tn(weights, grad_h)
            grad_q = (dot(grad_scores, k_rot[0:keys]) * SCALE).astype(BF).astype(F32)
            pre = qk_pre[rows, 128 * h : 128 * h + 128]
            grad, gain_part = back_rope(grad_q, pre, query_gain, cos, sin)
            dqkv[rows, 128 * h : 128 * h + 128] = grad.astype(BF)
            gg[16:17] += gain_part
        grad_k = dk[rows].astype(BF).astype(F32)
        grad, gain_part = back_rope(grad_k, qk_pre[rows, 256:384], key_gain, cos, sin)
        dqkv[rows, 256:384] = grad.astype(BF)
        gg[17:18] += gain_part
        dqkv[rows, 384:512] = dv[rows].astype(BF)
        err = dot_nt(dqkv[rows], wq[...])
        p3[rows] = err.astype(BF)
        send_chunk(sum_3, qb)
        attn_part += jnp.sum(err * (xs[rows].astype(F32) * r1[rows]), axis=0, keepdims=True)
        if qb == 3:
            sum_o.relay()
            weight_d.relay()
        if qb == 2:
            weight_u.spread()
            weight_o.cross()
        if qb == 1:
            for k in (2, 1, 3):
                sum_3.cross(k, when=c == 1)
            weight_d.spread()
            weight_o.relay()
            out_tmp[...] = (middle[...] + sum_o.total()).astype(BF)
            links.send(out_tmp, out_ref, place.swap, out_id, when=away)

    for k in (2, 1, 3):
        sum_3.cross(k, when=c == 0)
    sum_3.cross(0)
    for k in range(8):
        gg[k : k + 1] = attn_part[:, 128 * k : 128 * k + 128]
    for dy, dc in column:
        links.send(gg, gg_y.at[y * 2 + c], place.at(dy=dy, dc=dc), gg_y_id + y * 2 + c)

    def attn_weight_chunk(i, carry):
        cols = pl.ds(pl.multiple_of(i * CH, CH), CH)
        grad = dot_tn(h1[:, cols], dqkv[...]).astype(BF)
        gq_full[pl.ds(2 * i, 2)] = grad[:, 0:256].reshape(2, 128, 256)
        gk_full[i] = grad[:, 256:512].reshape(4, 64, 256)
        return carry

    lax.fori_loop(0, 4, attn_weight_chunk, 0)
    weight_k.begin()
    weight_q.begin()
    sum_3.relay()

    gg_y[y * 2 + c] = gg[...]
    for dy, dc in column:
        index = ((y + dy) % 4) * 2 + (c + dc) % 2
        links.wait(gg_y.at[index], place.at(dy=dy, dc=dc), gg_y_id + index)
    total = gg_y[0]
    for k in range(1, 8):
        total = total + gg_y[k]
    gg_a[...] = total
    for k in range(1, 4):
        links.send(gg_a, gg_x.at[x], place.at(dx=k), gg_x_id + x)
    weight_o.spread()
    weight_u.finish()
    weight_d.finish()
    weight_k.cross()
    weight_q.spread()

    err = sum_3.total()
    r_one = r1[own]
    normed = xs[own].astype(F32) * r_one
    scaled = err * gain_one[0:1]
    in_grad_tmp[...] = (
        grad_mid[...]
        + r_one * (scaled - normed * jnp.mean(scaled * normed, axis=-1, keepdims=True))
    ).astype(BF)
    links.send(in_grad_tmp, in_grad_ref, place.swap, in_grad_id, when=away)

    gg_x[x] = gg_a[...]
    for k in range(1, 4):
        other = (x + k) % 4
        links.wait(gg_x.at[other], place.at(dx=k), gg_x_id + other)
    gg_b[...] = (gg_x[0] + gg_x[1]) + (gg_x[2] + gg_x[3])
    for k in range(1, 4):
        links.send(gg_b, gg_z.at[z], place.at(dz=k), gg_z_id + z)

    weight_k.spread()
    weight_o.finish()

    @pl.when(home)
    def _():
        out_ref[...] = out_tmp[...]
        in_grad_ref[...] = in_grad_tmp[...]

    gg_z[z] = gg_b[...]
    for k in range(1, 4):
        other = (z + k) % 4
        links.wait(gg_z.at[other], place.at(dz=k), gg_z_id + other)
    gains_ref[...] = (gg_z[0] + gg_z[1]) + (gg_z[2] + gg_z[3])

    weight_q.finish()
    weight_k.finish()
    links.wait(out_ref, place.swap, out_id, when=away)
    links.wait(in_grad_ref, place.swap, in_grad_id, when=away)
    links.drain()


def run_layer(*args):
    vmem = pl.BlockSpec(memory_space=pltpu.VMEM)

    def sds(shape, kind):
        return jax.ShapeDtypeStruct(shape, kind)

    def buf(shape, kind=BF):
        return pltpu.VMEM(shape, kind)

    group = (GROUP, WIDTH)
    table = (GROUP, HEAD)
    block = (TOK, WIDTH)
    landing = [buf(group), buf((4, TOK, WIDTH)), buf((8, 64, WIDTH))]
    gains = (24, 128)

    def weight_landing(cols):
        return [buf((WIDTH, cols)), buf((10, 128, cols)), buf((4, 64, cols))]

    def weight_landing_y(cols):
        return [
            buf((4, 4, 64, cols)),
            buf((4, 4, 2, 64, cols)),
            buf((4, 2, 64, cols)),
            buf((9, 64, cols)),
            buf((64, cols)),
        ]

    scratch = [
        buf((64, NQ)),
        buf((64, NU)),
        buf((4, 64, NO)),
        buf((4, 64, ND)),
        buf((WIDTH, NQ)),
        buf((WIDTH, NU)),
        buf((4, 4, 64, NO)),
        buf((4, 4, 64, ND)),
        buf((16, 8, 128), F32),
        buf((1, WIDTH), F32),
        buf((1, WIDTH), F32),
        buf((1, 4), jnp.int32),
        buf((GROUP, 1), jnp.int32),
        buf(table, F32),
        buf(table, F32),
        buf(group),
        buf(group),
        buf(group),
        buf((GROUP, 1), F32),
        buf((GROUP, 384), F32),
        buf((2, GROUP, HEAD)),
        buf(table),
        buf(table),
        buf((GROUP, 256)),
        buf((2, 512, 512)),
        buf((2, 512, GROUP)),
        *landing,
        buf(block, F32),
        buf(group),
        buf((GROUP, 384), F32),
        buf((GROUP, 384)),
        buf((GROUP, 768)),
        *landing,
        *landing,
        buf(group),
        buf(block, F32),
        buf(table, F32),
        buf(table, F32),
        buf((GROUP, 512)),
        *landing,
        *weight_landing(NU),
        buf((8, 128, 256)),
        *weight_landing(256)[1:],
        *weight_landing_y(NO),
        *weight_landing_y(NO),
        *weight_landing_y(ND),
        buf(block),
        buf(block),
        buf(gains, F32),
        buf((8, *gains), F32),
        buf(gains, F32),
        buf((4, *gains), F32),
        buf(gains, F32),
        buf((4, *gains), F32),
        pltpu.SemaphoreType.DMA((N_SEMS,)),
        pltpu.SemaphoreType.DMA((N_SEMS,)),
    ]
    return pl.pallas_call(
        layer_kernel,
        out_shape=(
            sds(block, BF),
            sds(block, BF),
            sds((64, 256), F32),
            sds((64, 256), F32),
            sds((64, NO), F32),
            sds((64, NU), F32),
            sds((64, ND), F32),
            sds(gains, F32),
        ),
        in_specs=[vmem] * len(args),
        out_specs=(vmem,) * 8,
        scratch_shapes=scratch,
        name="layer",
        compiler_params=pltpu.CompilerParams(
            collective_id=0, has_side_effects=True, vmem_limit_bytes=63 * 2**20
        ),
    )(*args)


def results_kernel(
    out_in,
    in_grad_in,
    gq,
    gk,
    go,
    gu,
    gd,
    gains,
    out,
    in_grad,
    attn_gain,
    query,
    key,
    value,
    query_gain,
    key_gain,
    w_out,
    mlp_gain,
    gate,
    up,
    down,
):
    d = lax.axis_index("dp")
    out[...] = out_in[...]
    in_grad[...] = in_grad_in[...]
    query[...] = gq[...]
    key[...] = gk[:, 0:128]
    value[...] = gk[:, 128:256]
    w_out[...] = go[...]
    gate[...] = gu[:, 0:384]
    up[...] = gu[:, 384:768]
    down[...] = gd[...]
    query_gain[...] = gains[16:17]
    key_gain[...] = gains[17:18]
    for first, ref in ((0, attn_gain), (8, mlp_gain)):
        row = gains[pl.ds(first + d // 2, 1)]
        ref[...] = jnp.where(d % 2 == 1, pltpu.roll(row, 64, 1), row)[:, 0:64]


def write_results(*args):
    vmem = pl.BlockSpec(memory_space=pltpu.VMEM)
    shapes = [
        ((TOK, WIDTH), BF),
        ((TOK, WIDTH), BF),
        ((1, 64), F32),
        ((64, 256), F32),
        ((64, 128), F32),
        ((64, 128), F32),
        ((1, 128), F32),
        ((1, 128), F32),
        ((64, 256), F32),
        ((1, 64), F32),
        ((64, 384), F32),
        ((64, 384), F32),
        ((64, 384), F32),
    ]
    return pl.pallas_call(
        results_kernel,
        out_shape=tuple(jax.ShapeDtypeStruct(shape, kind) for shape, kind in shapes),
        in_specs=[vmem] * len(args),
        out_specs=(vmem,) * len(shapes),
        name="results",
    )(*args)


def per_device(
    layer_input,
    seq_lengths,
    attn_gain,
    w_query,
    key_projection,
    value_projection,
    query_gain,
    key_gain,
    w_out,
    mlp_gain,
    w_gate,
    w_up,
    w_down,
    out_grad,
):
    half = HEAD // 2
    frequency = ROPE_BASE ** (-(jnp.arange(half).astype(F32) * 2.0 / HEAD))
    parts = run_layer(
        w_query,
        key_projection,
        value_projection,
        w_out.T,
        w_gate,
        w_up,
        w_down.T,
        jnp.concatenate([attn_gain, mlp_gain]).astype(F32)[None],
        layer_input,
        out_grad,
        query_gain[None],
        key_gain[None],
        seq_lengths,
        jnp.concatenate([frequency, frequency])[None],
    )
    results = list(write_results(*parts))
    for k in (2, 6, 7, 9):
        results[k] = results[k].reshape(-1)
    results[8], results[12] = results[8].T, results[12].T
    return tuple(results)


def solution(mesh):
    both = P(("dp", "tensor"), None)
    split = P("dp", "tensor")
    turned = P("tensor", "dp")
    in_specs = (
        both,
        P("dp", None),
        P("dp"),
        split,
        split,
        split,
        P(),
        P(),
        turned,
        P("dp"),
        split,
        split,
        turned,
        both,
    )
    out_specs = (both, both, P("dp"), split, split, split, P(), P(), turned, P("dp"), split, split, turned)
    return jax.shard_map(
        per_device, mesh=mesh, in_specs=in_specs, out_specs=out_specs, check_vma=False
    )
```

```python
import functools

import jax
import jax.numpy as jnp
import numpy as np
from jax import lax
from jax.experimental import pallas as pl
from jax.experimental.pallas import tpu as pltpu
from jax.sharding import PartitionSpec as P

MESH = pl.DeviceIdType.MESH
BF = jnp.bfloat16
F32 = jnp.float32
HEAD = 128
EPS = 1e-06
ROPE_BASE = 1000000.0
MASKED = -1e30
SCALE = HEAD ** (-0.5)
TOK = 128
GROUP = 1024
WIDTH = 1024
NQ = 512
NO = 256
NU = 768
ND = 384
CH = 256
N_SENDS = 101
N_RECVS = 195


def dot(a, b):
    return jnp.dot(a, b, preferred_element_type=F32)


def dot_nt(a, b):
    return lax.dot_general(a, b, (((1,), (1,)), ((), ())), preferred_element_type=F32)


def dot_tn(a, b):
    return lax.dot_general(a, b, (((0,), (0,)), ((), ())), preferred_element_type=F32)


class Links:
    def __init__(self, send_sems, recv_sems):
        self.send_sems, self.recv_sems = send_sems, recv_sems
        self.sends, self.recvs = 0, 0
        self.pending, self.free, self.drained = [], [], 0

    def recv_ids(self, count=1):
        first = self.recvs
        self.recvs += count
        assert self.recvs <= N_RECVS
        return first

    def copy(self, src, dst, device, send_id, recv_id):
        return pltpu.make_async_remote_copy(
            src_ref=src,
            dst_ref=dst,
            send_sem=self.send_sems.at[send_id],
            recv_sem=self.recv_sems.at[recv_id],
            device_id=device,
            device_id_type=MESH,
        )

    def send_id(self):
        if self.free:
            return self.free.pop()
        self.sends += 1
        assert self.sends <= N_SENDS
        return self.sends - 1

    def send(self, src, dst, device, recv_id, when=None, send_id=None):
        if send_id is None:
            send_id = self.send_id()
        copy = self.copy(src, dst, device, send_id, recv_id)
        if when is None:
            copy.start()
        else:
            pl.when(when)(copy.start)
        self.pending.append((copy, when, send_id))

    def wait(self, dst, device, recv_id, when=None):
        copy = self.copy(dst, dst, device, 0, recv_id)
        if when is None:
            copy.wait_recv()
        else:
            pl.when(when)(copy.wait_recv)

    def issued(self):
        return self.drained + len(self.pending)

    def drain(self, upto):
        count = upto - self.drained
        done, self.pending, self.drained = self.pending[:count], self.pending[count:], upto
        for copy, when, _ in done:
            if when is None:
                copy.wait_send()
            else:
                pl.when(when)(copy.wait_send)
        self.free += sorted({send_id for _, _, send_id in done})


class Place:
    def __init__(self):
        d, t = lax.axis_index("dp"), lax.axis_index("tensor")
        self.d = d
        self.x, self.c = d // 4, d % 2
        self.y, self.z = (t // 4) * 2 + (d // 2) % 2, t % 4
        self.home = self.c == t // 4
        self.left_z, self.right_z = self.at(dz=3), self.at(dz=1)
        self.left_x, self.right_x = self.at(dx=3), self.at(dx=1)
        self.core = self.at(dc=1)
        self.swap = self.at(dy=2, dc=1)

    def device(self, x, y, z, c):
        return (x * 4 + (y % 2) * 2 + c, (y // 2) * 4 + z)

    def at(self, dx=0, dy=0, dz=0, dc=0):
        return self.device((self.x + dx) % 4, (self.y + dy) % 4, (self.z + dz) % 4, (self.c + dc) % 2)


class WeightGather:
    def __init__(self, links, place, own, buf):
        self.links, self.place, self.own, self.buf = links, place, own, buf
        self.y_id = links.recv_ids(4)
        self.ids = {name: links.recv_ids() for name in ("xm", "xp", "l", "r")}

    def block(self, index):
        return self.buf.at[pl.ds(pl.multiple_of(index * 64, 64), 64)]

    def rows(self, dx, half=None):
        first = ((self.place.x + dx) % 4) * 256
        if half is None:
            return self.buf.at[pl.ds(pl.multiple_of(first, 256), 256)]
        return self.buf.at[pl.ds(pl.multiple_of(first + 128 * half, 128), 128)]

    def begin(self):
        place, links = self.place, self.links
        side = place.y // 2
        for dy in (2, 1, 3, 0):
            device = place.device(place.x, (place.y + dy) % 4, place.z, side)
            links.send(
                self.own,
                self.block(place.d),
                device,
                self.y_id + place.d % 4,
                when=(place.c != side) if dy == 0 else None,
            )

        @pl.when(place.c == side)
        def _():
            self.block(place.d)[...] = self.own[...]

    def second(self):
        place, links = self.place, self.links
        for low in range(2):
            for core in range(2):
                y = 2 * place.c + low
                links.wait(
                    self.block(place.x * 4 + low * 2 + core),
                    place.device(place.x, y, place.z, core),
                    self.y_id + low * 2 + core,
                    when=(y != place.y) | (core != place.c),
                )
        mine = self.rows(0)
        links.send(mine, mine, place.right_x, self.ids["xm"])
        links.send(mine, mine, place.left_x, self.ids["xp"])

    def third(self):
        place, links = self.place, self.links
        links.wait(self.rows(3), place.left_x, self.ids["xm"])
        half = self.rows(3, 0)
        links.send(half, half, place.right_x, self.ids["l"])
        links.wait(self.rows(1), place.right_x, self.ids["xp"])
        half = self.rows(1, 1)
        links.send(half, half, place.left_x, self.ids["r"])

    def finish(self):
        place, links = self.place, self.links
        links.wait(self.rows(2, 0), place.left_x, self.ids["l"])
        links.wait(self.rows(2, 1), place.right_x, self.ids["r"])


class WeightSum:
    def __init__(self, links, place, full, side, land, out):
        self.links, self.place, self.full = links, place, full
        self.side, self.land, self.out = side, land, out
        self.ids = {n: links.recv_ids() for n in ("la", "lr", "ra", "rr", "lc", "rc")}
        self.y_id = links.recv_ids(4)

    def rows(self, dx, half):
        return pl.ds(pl.multiple_of(((self.place.x + dx) % 4) * 256 + 128 * half, 128), 128)

    def begin(self):
        place, links, side = self.place, self.links, self.side
        links.send(self.full.at[self.rows(2, 0)], side.at[0], place.right_x, self.ids["la"])
        links.send(self.full.at[self.rows(2, 1)], side.at[2], place.left_x, self.ids["ra"])
        links.send(self.full.at[self.rows(1, 1)], side.at[1], place.right_x, self.ids["lr"])
        links.send(self.full.at[self.rows(3, 0)], side.at[3], place.left_x, self.ids["rr"])

    def relay(self):
        place, links, side = self.place, self.links, self.side
        links.wait(side.at[0], place.left_x, self.ids["la"])
        side[6] = (self.full[self.rows(1, 0)].astype(F32) + side[0].astype(F32)).astype(BF)
        links.send(side.at[6], side.at[4], place.right_x, self.ids["lc"])
        links.wait(side.at[2], place.right_x, self.ids["ra"])
        side[7] = (self.full[self.rows(3, 1)].astype(F32) + side[2].astype(F32)).astype(BF)
        links.send(side.at[7], side.at[5], place.left_x, self.ids["rc"])

    def gathered(self):
        place, links, side = self.place, self.links, self.side
        links.wait(side.at[1], place.left_x, self.ids["lr"])
        links.wait(side.at[3], place.right_x, self.ids["rr"])
        links.wait(side.at[4], place.left_x, self.ids["lc"])
        links.wait(side.at[5], place.right_x, self.ids["rc"])
        for half, first, other in ((0, 4, 3), (1, 5, 1)):
            side[8 + half] = (
                self.full[self.rows(0, half)].astype(F32)
                + side[first].astype(F32)
                + side[other].astype(F32)
            ).astype(BF)

    def spread(self):
        self.gathered()
        place, links, side = self.place, self.links, self.side
        for low in range(2):
            for core in range(2):
                y = 2 * place.c + low
                away = (y != place.y) | (core != place.c)
                piece = side.at[8 + low, pl.ds(64 * core, 64)]
                links.send(
                    piece,
                    self.land.at[place.y],
                    place.device(place.x, y, place.z, core),
                    self.y_id + place.y,
                    when=away,
                )

                @pl.when(jnp.logical_not(away))
                def _():
                    self.land[place.y] = piece[...]

    def finish(self):
        place, links = self.place, self.links
        core = place.y // 2
        for k in range(4):
            y = (place.y + k) % 4
            links.wait(
                self.land.at[y],
                place.device(place.x, y, place.z, core),
                self.y_id + y,
                when=(place.c != core) if k == 0 else None,
            )
        total = self.land[0].astype(F32)
        for y in range(1, 4):
            total = total + self.land[y].astype(F32)
        self.out[...] = total


class WeightSumDirect(WeightSum):
    def begin(self):
        place = self.place
        for k, name in ((2, "ra"), (1, "la"), (3, "lr")):
            self.links.send(
                self.full.at[pl.ds(((place.x + k) % 4) * 2, 2)],
                self.side.at[pl.ds(2 * (k - 1), 2)],
                place.at(dx=k),
                self.ids[name],
            )

    def gathered(self):
        place, side = self.place, self.side
        for k, name in ((1, "la"), (3, "lr"), (2, "ra")):
            self.links.wait(side.at[pl.ds(2 * (k - 1), 2)], place.at(dx=4 - k), self.ids[name])
        for half in range(2):
            total = self.full[place.x * 2 + half].astype(F32)
            for k in range(3):
                total = total + side[2 * k + half].astype(F32)
            side[8 + half] = total.astype(BF)


class WeightGatherX:
    def __init__(self, links, place, own, stage, buf):
        self.links, self.place, self.own, self.stage, self.buf = links, place, own, stage, buf
        self.y_id = links.recv_ids(4)
        self.ids = {name: links.recv_ids() for name in ("xm", "xp", "l", "r")}

    def block(self, dx, half=None):
        at = (self.place.x + dx) % 4
        if half is None:
            return self.stage.at[at]
        return self.stage.at[at, pl.ds(32 * half, 32)]

    def begin(self):
        place, links = self.place, self.links
        links.send(self.own, self.block(0), place.right_x, self.ids["xm"])
        links.send(self.own, self.block(0), place.left_x, self.ids["xp"])
        self.stage[place.x] = self.own[...]

    def relay(self):
        place, links = self.place, self.links
        links.wait(self.block(3), place.left_x, self.ids["xm"])
        links.send(self.block(3, 0), self.block(3, 0), place.right_x, self.ids["l"])
        links.wait(self.block(1), place.right_x, self.ids["xp"])
        links.send(self.block(1, 1), self.block(1, 1), place.left_x, self.ids["r"])

    def spread(self):
        place, links = self.place, self.links
        links.wait(self.block(2, 0), place.left_x, self.ids["l"])
        links.wait(self.block(2, 1), place.right_x, self.ids["r"])
        side = place.y // 2
        for dy in (2, 1, 3, 0):
            links.send(
                self.stage,
                self.buf.at[:, place.d % 4],
                place.device(place.x, (place.y + dy) % 4, place.z, side),
                self.y_id + place.d % 4,
                when=(place.c != side) if dy == 0 else None,
            )

        @pl.when(place.c == side)
        def _():
            self.buf[:, place.d % 4] = self.stage[...]

    def finish(self):
        place, links = self.place, self.links
        for low in range(2):
            for core in range(2):
                y = 2 * place.c + low
                links.wait(
                    self.buf.at[:, low * 2 + core],
                    place.device(place.x, y, place.z, core),
                    self.y_id + low * 2 + core,
                    when=(y != place.y) | (core != place.c),
                )


class WeightSumY:
    def __init__(self, links, place, full, land, total, side, last, out):
        self.links, self.place, self.full, self.land = links, place, full, land
        self.total, self.side, self.last, self.out = total, side, last, out
        self.y_id = links.recv_ids(4)
        self.ids = {n: links.recv_ids() for n in ("la", "lr", "ra", "rr", "lc", "rc", "core")}
        self.active = place.c == place.y // 2

    def begin(self):
        place = self.place
        for low in range(2):
            y = 2 * place.c + low
            self.links.send(
                self.full.at[:, pl.ds(2 * low, 2)],
                self.land.at[place.y],
                place.device(place.x, y, place.z, place.c),
                self.y_id + place.y,
                when=y != place.y,
            )

    def cross(self):
        place, links, side, active = self.place, self.links, self.side, self.active
        x = place.x
        for k in range(1, 4):
            y = (place.y + k) % 4
            links.wait(
                self.land.at[y], place.device(x, y, place.z, place.c), self.y_id + y, when=active
            )

        @pl.when(active)
        def _():
            def add(i, carry):
                acc = self.full[i, pl.ds((place.y % 2) * 2, 2)].astype(F32)
                for k in range(1, 4):
                    acc = acc + self.land[(place.y + k) % 4, i].astype(F32)
                self.total[i] = acc.astype(BF)
                return carry

            lax.fori_loop(0, 4, add, 0)

        self.ring()

    def ring(self):
        links, place, active, side, x = self.links, self.place, self.active, self.side, self.place.x
        total, ids = self.total, self.ids
        links.send(total.at[(x + 2) % 4, 0], side.at[0], place.right_x, ids["la"], when=active)
        links.send(total.at[(x + 2) % 4, 1], side.at[2], place.left_x, ids["ra"], when=active)
        links.send(total.at[(x + 1) % 4, 1], side.at[1], place.right_x, ids["lr"], when=active)
        links.send(total.at[(x + 3) % 4, 0], side.at[3], place.left_x, ids["rr"], when=active)

    def relay(self):
        place, links, side, ids, active = self.place, self.links, self.side, self.ids, self.active
        x = place.x
        links.wait(side.at[0], place.left_x, ids["la"], when=active)
        links.wait(side.at[2], place.right_x, ids["ra"], when=active)

        @pl.when(active)
        def _():
            side[6] = (self.total[(x + 1) % 4, 0].astype(F32) + side[0].astype(F32)).astype(BF)
            side[7] = (self.total[(x + 3) % 4, 1].astype(F32) + side[2].astype(F32)).astype(BF)

        links.send(side.at[6], side.at[4], place.right_x, ids["lc"], when=active)
        links.send(side.at[7], side.at[5], place.left_x, ids["rc"], when=active)

    def spread(self):
        place, links, side, ids, active = self.place, self.links, self.side, self.ids, self.active
        x = place.x
        links.wait(side.at[1], place.left_x, ids["lr"], when=active)
        links.wait(side.at[3], place.right_x, ids["rr"], when=active)
        links.wait(side.at[4], place.left_x, ids["lc"], when=active)
        links.wait(side.at[5], place.right_x, ids["rc"], when=active)

        self.deliver(((4, 3), (5, 1)))

    def deliver(self, slots):
        place, links, side, ids, active = self.place, self.links, self.side, self.ids, self.active
        x = place.x

        @pl.when(active)
        def _():
            sums = []
            for half in range(2):
                total = self.total[x, half].astype(F32)
                for slot in slots[half]:
                    total = total + side[slot].astype(F32)
                sums.append(total)
            zero, one = sums
            self.out[...] = jnp.where(place.c == 0, zero, one)
            side[8] = jnp.where(place.c == 0, one, zero).astype(BF)

        links.send(side.at[8], self.last, place.core, ids["core"], when=active)

    def finish(self):
        idle = jnp.logical_not(self.active)
        self.links.wait(self.last, self.place.core, self.ids["core"], when=idle)

        @pl.when(idle)
        def _():
            self.out[...] = self.last[...].astype(F32)


class WeightSumYDirect(WeightSumY):
    def ring(self):
        place = self.place
        for k, name in ((2, "ra"), (1, "la"), (3, "lr")):
            self.links.send(
                self.total.at[(place.x + k) % 4],
                self.side.at[pl.ds(2 * (k - 1), 2)],
                place.at(dx=k),
                self.ids[name],
                when=self.active,
            )

    def spread(self):
        for k, name in ((1, "la"), (3, "lr"), (2, "ra")):
            self.links.wait(
                self.side.at[pl.ds(2 * (k - 1), 2)],
                self.place.at(dx=4 - k),
                self.ids[name],
                when=self.active,
            )
        self.deliver(((0, 2, 4), (1, 3, 5)))


def token_rows(c, z, by_z):
    index = z * 2 + c if by_z else c * 4 + z
    return pl.multiple_of(index * TOK, TOK)


class TokenSum:
    def __init__(self, links, place, partial, core_in, side, by_z):
        self.links, self.place, self.partial = links, place, partial
        self.core_in, self.side, self.by_z = core_in, side, by_z
        self.core_id = links.recv_ids(4)
        self.ids = {n: links.recv_ids() for n in ("la", "lr", "ra", "rr", "lc", "rc")}
        self.shared = {}

    def send_id(self, name):
        if name not in self.shared:
            self.shared[name] = self.links.send_id()
        return self.shared[name]

    def rows(self, c, z):
        return pl.ds(token_rows(c, z, self.by_z), TOK)

    def send_core(self, z, when=None):
        place = self.place
        self.links.send(
            self.partial.at[self.rows((place.c + 1) % 2, z)],
            self.core_in.at[z],
            place.core,
            self.core_id + z,
            when=when,
            send_id=None if when is None else self.send_id(z),
        )

    def half(self, z, h):
        return pl.ds(token_rows(self.place.c, z, self.by_z) + 64 * h, 64)

    def cross(self, k, when=None):
        place, links, side, ids = self.place, self.links, self.side, self.ids
        z = (place.z + k) % 4
        links.wait(self.core_in.at[z], place.core, self.core_id + z, when=when)

        def add():
            rows = self.rows(place.c, z)
            self.partial[rows] = (
                self.partial[rows].astype(F32) + self.core_in[z].astype(F32)
            ).astype(BF)

        if when is None:
            add()
        else:
            pl.when(when)(add)
        low, high = self.partial.at[self.half(z, 0)], self.partial.at[self.half(z, 1)]
        for at, ref, slot, device, name in (
            (2, low, 0, place.right_z, "la"),
            (2, high, 2, place.left_z, "ra"),
            (1, high, 1, place.right_z, "lr"),
            (3, low, 3, place.left_z, "rr"),
        ):
            if k == at:
                send_id = None if when is None else self.send_id(name)
                links.send(ref, side.at[slot], device, ids[name], when=when, send_id=send_id)

    def relay(self):
        place, links, side = self.place, self.links, self.side
        z = place.z
        links.wait(side.at[0], place.left_z, self.ids["la"])
        side[6] = (self.partial[self.half((z + 1) % 4, 0)].astype(F32) + side[0].astype(F32)).astype(BF)
        links.send(side.at[6], side.at[4], place.right_z, self.ids["lc"])
        links.wait(side.at[2], place.right_z, self.ids["ra"])
        side[7] = (self.partial[self.half((z + 3) % 4, 1)].astype(F32) + side[2].astype(F32)).astype(BF)
        links.send(side.at[7], side.at[5], place.left_z, self.ids["rc"])

    def total(self):
        place, links, side = self.place, self.links, self.side
        links.wait(side.at[1], place.left_z, self.ids["lr"])
        links.wait(side.at[3], place.right_z, self.ids["rr"])
        links.wait(side.at[4], place.left_z, self.ids["lc"])
        links.wait(side.at[5], place.right_z, self.ids["rc"])
        return jnp.concatenate([self.half_sum(0), self.half_sum(1)], axis=0)

    def half_sum(self, half):
        first, other = ((4, 3), (5, 1))[half]
        return (
            self.partial[self.half(self.place.z, half)].astype(F32)
            + self.side[first].astype(F32)
            + self.side[other].astype(F32)
        )

    def half_total(self, half):
        place, links, side = self.place, self.links, self.side
        if half == 0:
            links.wait(side.at[3], place.right_z, self.ids["rr"])
            links.wait(side.at[4], place.left_z, self.ids["lc"])
        else:
            links.wait(side.at[1], place.left_z, self.ids["lr"])
            links.wait(side.at[5], place.right_z, self.ids["rc"])
        return self.half_sum(half)


class TokenGather:
    def __init__(self, links, place, buf, by_z):
        self.links, self.place, self.buf, self.by_z = links, place, buf, by_z
        names = ("zm0", "zm1", "zp0", "zp1", "l", "r", "c0", "c1", "c2", "c3")
        self.ids = {name: links.recv_ids() for name in names}

    def rows(self, k, core=0, half=None):
        place = self.place
        first = token_rows((place.c + core) % 2, (place.z + k) % 4, self.by_z)
        if half is None:
            return self.buf.at[pl.ds(first, TOK)]
        return self.buf.at[pl.ds(first + 64 * half, 64)]

    def push(self, ref, device, name):
        self.links.send(ref, ref, device, self.ids[name])

    def begin(self):
        place = self.place
        self.push(self.rows(0, half=0), place.right_z, "zm0")
        self.push(self.rows(0, half=1), place.left_z, "zp1")
        self.push(self.rows(0), place.core, "c0")
        self.push(self.rows(0, half=1), place.right_z, "zm1")
        self.push(self.rows(0, half=0), place.left_z, "zp0")

    def sides(self):
        place, links, ids = self.place, self.links, self.ids
        links.wait(self.rows(3, half=0), place.left_z, ids["zm0"])
        self.push(self.rows(3, half=0), place.right_z, "l")
        links.wait(self.rows(1, half=1), place.right_z, ids["zp1"])
        self.push(self.rows(1, half=1), place.left_z, "r")
        links.wait(self.rows(3, half=1), place.left_z, ids["zm1"])
        self.push(self.rows(3), place.core, "c3")
        links.wait(self.rows(1, half=0), place.right_z, ids["zp0"])
        self.push(self.rows(1), place.core, "c1")

    def far(self):
        place = self.place
        self.links.wait(self.rows(2, half=0), place.left_z, self.ids["l"])
        self.links.wait(self.rows(2, half=1), place.right_z, self.ids["r"])
        self.push(self.rows(2), place.core, "c2")

    def core(self, k):
        self.links.wait(self.rows(k, core=1), self.place.core, self.ids["c%d" % k])


def layer_kernel(
    w_query,
    w_key,
    w_value,
    w_out,
    w_gate,
    w_up,
    w_down,
    attn_gain,
    mlp_gain,
    x_own,
    og_own,
    query_gain_in,
    key_gain_in,
    lengths_own,
    frequency,
    out_ref,
    in_grad_ref,
    gq_ref,
    gk_ref,
    go_ref,
    gu_ref,
    gd_ref,
    gains_ref,
    wq_own,
    wu_own,
    wo_stage,
    wd_stage,
    wq,
    wu,
    wo,
    wd,
    gain_in,
    gain_one,
    gain_two,
    lengths,
    starts,
    cosine,
    sine,
    xs,
    ogs,
    h1,
    r1,
    qk_pre,
    q_rot,
    k_rot,
    vals,
    mixed,
    probs_low,
    probs_high,
    p1,
    p1_core,
    p1_side,
    middle,
    h2,
    grad_act,
    act,
    dgu,
    p2,
    p2_core,
    p2_side,
    po,
    po_core,
    po_side,
    gb,
    grad_mid,
    p3_core,
    p3_side,
    gu_full,
    gu_side,
    gu_land,
    gq_full,
    gq_side,
    gq_land,
    gk_full,
    gk_land,
    gk_total,
    gk_side,
    gk_last,
    go_full,
    go_land,
    go_total,
    go_side,
    go_last,
    gd_full,
    gd_land,
    gd_total,
    gd_side,
    gd_last,
    out_tmp,
    in_grad_tmp,
    gg,
    gg_y,
    gg_a,
    gg_x,
    gg_b,
    gg_z,
    send_sems,
    recv_sems,
):
    links = Links(send_sems, recv_sems)
    place = Place()
    x, y, z, c = place.x, place.y, place.z, place.c
    home, away = place.home, jnp.logical_not(place.home)
    own = pl.ds(token_rows(c, z, False), TOK)
    own_z = pl.ds(token_rows(c, z, True), TOK)
    swap_own = pl.ds(token_rows((c + 1) % 2, z, False), TOK)
    swap_z = pl.ds(token_rows((c + 1) % 2, z, True), TOK)
    column = [(dy, dc) for dy in range(4) for dc in range(2) if dy or dc]

    barrier = pltpu.get_barrier_semaphore()
    for peer in (
        [place.at(dy=dy, dc=dc) for dy, dc in column]
        + [place.at(dx=k) for k in range(1, 4)]
        + [place.at(dz=k) for k in range(1, 4)]
    ):
        pl.semaphore_signal(barrier, inc=1, device_id=peer, device_id_type=MESH)

    gather_q = WeightGather(links, place, wq_own, wq)
    gather_u = WeightGather(links, place, wu_own, wu)
    gather_o = WeightGatherX(links, place, w_out, wo_stage, wo)
    gather_d = WeightGatherX(links, place, w_down, wd_stage, wd)
    gather_x = TokenGather(links, place, xs, False)
    gather_og = TokenGather(links, place, ogs, True)
    gather_h2 = TokenGather(links, place, h2, True)
    gather_gb = TokenGather(links, place, gb, False)
    sum_1 = TokenSum(links, place, p1, p1_core, p1_side, False)
    sum_2 = TokenSum(links, place, p2, p2_core, p2_side, True)
    sum_o = TokenSum(links, place, po, po_core, po_side, True)
    sum_3 = TokenSum(links, place, h2, p3_core, p3_side, False)
    weight_u = WeightSum(links, place, gu_full, gu_side, gu_land, gu_ref)
    weight_q = WeightSumDirect(links, place, gq_full, gq_side, gq_land, gq_ref)
    weight_k = WeightSumYDirect(links, place, gk_full, gk_land, gk_total, gk_side, gk_last, gk_ref)
    weight_o = WeightSumY(links, place, go_full, go_land, go_total, go_side, go_last, go_ref)
    weight_d = WeightSumY(links, place, gd_full, gd_land, gd_total, gd_side, gd_last, gd_ref)
    x_id, og_id, lengths_id, out_id = [links.recv_ids() for _ in range(4)]
    in_grad_id = links.recv_ids(2)
    gain_id, gain_x_id = links.recv_ids(4), links.recv_ids(4)
    gg_y_id, gg_x_id, gg_z_id = links.recv_ids(8), links.recv_ids(4), links.recv_ids(4)

    @pl.when(home)
    def _():
        xs[own] = x_own[...]
        ogs[own_z] = og_own[...]
        lengths[...] = lengths_own[...]

    wq_own[:, 0:256] = w_query[...]
    wq_own[:, 256:384] = w_key[...]
    wq_own[:, 384:512] = w_value[...]
    wu_own[:, 0:384] = w_gate[...]
    wu_own[:, 384:768] = w_up[...]
    gain_in[place.d, :, 0:64] = jnp.broadcast_to(attn_gain[...].astype(F32), (8, 64))
    gain_in[place.d, :, 64:128] = jnp.broadcast_to(mlp_gain[...].astype(F32), (8, 64))
    query_gain, key_gain = query_gain_in[...].astype(F32), key_gain_in[...].astype(F32)

    pl.semaphore_wait(barrier, 13)

    links.send(x_own, xs.at[swap_own], place.swap, x_id, when=away)
    gather_o.begin()
    gather_d.begin()
    gather_q.begin()
    for dy, dc in ((0, 1), (1, 0), (1, 1)):
        other_y = (y // 2) * 2 + (y % 2 + dy) % 2
        peer = place.device(x, other_y, z, (c + dc) % 2)
        links.send(gain_in.at[place.d], gain_in.at[place.d], peer, gain_id + place.d % 4)
    links.send(lengths_own, lengths, place.core, lengths_id, when=home)

    links.wait(xs.at[own], place.swap, x_id, when=away)
    gather_x.begin()
    gather_o.relay()
    gather_d.relay()
    gather_q.second()
    for dy, dc in ((0, 1), (1, 0), (1, 1)):
        other_y = (y // 2) * 2 + (y % 2 + dy) % 2
        index = x * 4 + (other_y % 2) * 2 + (c + dc) % 2
        peer = place.device(x, other_y, z, (c + dc) % 2)
        links.wait(gain_in.at[index], peer, gain_id + index % 4)
    four = pl.ds(x * 4, 4)
    for k in range(1, 4):
        links.send(gain_in.at[four], gain_in.at[four], place.at(dx=k), gain_x_id + x)
    links.send(og_own, ogs.at[swap_z], place.swap, og_id, when=away)
    gather_o.spread()
    gather_u.begin()

    gather_x.sides()
    gather_q.third()
    gather_d.spread()
    for k in range(1, 4):
        other = (x + k) % 4
        links.wait(gain_in.at[pl.ds(other * 4, 4)], place.at(dx=k), gain_x_id + other)
    low = lax.broadcasted_iota(jnp.int32, (1, 128), 1) < 64
    for k in range(8):
        even, odd = gain_in[2 * k][0:1], gain_in[2 * k + 1][0:1]
        cols = slice(128 * k, 128 * k + 128)
        gain_one[0:1, cols] = jnp.where(low, even, pltpu.roll(odd, 64, 1))
        gain_two[0:1, cols] = jnp.where(low, pltpu.roll(even, 64, 1), odd)

    links.wait(lengths, place.core, lengths_id, when=away)

    def trig_chunk(i, carry):
        rows = pl.ds(pl.multiple_of(i * CH, CH), CH)
        at = lax.broadcasted_iota(jnp.int32, (CH, 1), 0) + i * CH
        end, start = jnp.zeros((1, 1), jnp.int32), jnp.zeros((CH, 1), jnp.int32)
        for k in range(3):
            end = end + lengths[0:1, k : k + 1]
            start = jnp.where(at >= end, end, start)
        starts[rows] = start
        angles = (at - start).astype(F32) * frequency[0:1]
        cosine[rows] = jnp.cos(angles)
        turned = jnp.sin(angles)
        sine[rows] = jnp.where(low, -turned, turned)
        return carry

    lax.fori_loop(0, 4, trig_chunk, 0)

    def norm_pair(k):
        for core in range(2):
            norm_rows(pl.ds(token_rows((c + core) % 2, (z + k) % 4, False), TOK))

    def norm_rows(rows):
        wide = xs[rows].astype(F32)
        r = lax.rsqrt(jnp.mean(wide * wide, axis=-1, keepdims=True) + EPS)
        r1[rows] = r
        h1[rows] = (wide * r * gain_one[0:1]).astype(BF)

    for k in (0, 3, 1):
        gather_x.core(k)
        norm_pair(k)
    gather_x.far()
    links.wait(ogs.at[own_z], place.swap, og_id, when=away)
    gather_og.begin()
    gather_x.core(2)
    norm_pair(2)
    gather_q.finish()

    def qkv_chunk(i, carry):
        rows = pl.ds(pl.multiple_of(i * CH, CH), CH)
        pre = dot(h1[rows], wq[...])
        qk_pre[rows] = pre[:, 0:384]
        vals[rows] = pre[:, 384:512].astype(BF)
        cos, sin = cosine[rows], sine[rows]
        for h in range(3):
            part = pre[:, 128 * h : 128 * h + 128]
            r = lax.rsqrt(jnp.mean(part * part, axis=-1, keepdims=True) + EPS)
            scaled = part * r * (query_gain if h < 2 else key_gain)
            turned = (scaled * cos + pltpu.roll(scaled, 64, 1) * sin).astype(BF)
            if h < 2:
                q_rot[pl.ds(pl.multiple_of(i * 512 + h * CH, CH), CH)] = turned
            else:
                k_rot[rows] = turned
        return carry

    lax.fori_loop(0, 4, qkv_chunk, 0)
    gather_u.second()
    gather_o.finish()
    gather_og.sides()

    def allowed(qb, keys):
        key_at = lax.broadcasted_iota(jnp.int32, (CH, keys), 1)
        query_at = lax.broadcasted_iota(jnp.int32, (CH, keys), 0) + qb * CH
        return (key_at >= starts[qb * CH : qb * CH + CH]) & (key_at <= query_at)

    def probs_of(qb):
        return probs_low if qb < 2 else probs_high

    def probs_rows(qb):
        return slice((qb % 2) * 512, (qb % 2) * 512 + 512)

    def send_chunk(group_sum, qb):
        for b in (2 * qb, 2 * qb + 1):
            group_sum.send_core(b % 4, when=c != b // 4)

    for qb in range(4):
        rows = slice(qb * CH, qb * CH + CH)
        keys = CH * (qb + 1)
        ok = allowed(qb, keys)
        scores = dot_nt(q_rot[qb * 512 : qb * 512 + 512], k_rot[0:keys]).reshape(2, CH, keys)
        scores = jnp.where(ok[None], scores * SCALE, MASKED)
        terms = jnp.exp(scores - jnp.max(scores, axis=-1, keepdims=True))
        weights = terms * (1.0 / jnp.sum(terms, axis=-1, keepdims=True))
        weights = weights.astype(BF).reshape(512, keys)
        probs_of(qb)[probs_rows(qb), 0:keys] = weights
        both = dot(weights, vals[0:keys]).astype(BF)
        mixed[rows, 0:128] = both[0:CH]
        mixed[rows, 128:256] = both[CH:512]
        p1[rows] = dot_nt(mixed[rows], wo[...].reshape(WIDTH, 256)).astype(BF)
        send_chunk(sum_1, qb)
        if qb == 2:
            for k in (2, 1, 3):
                sum_1.cross(k, when=c == 0)

    for k in (2, 1, 3):
        sum_1.cross(k, when=c == 1)
    sum_1.cross(0)
    gather_u.third()
    gather_og.far()
    sum_1.relay()

    gather_d.finish()
    for k in range(4):
        gather_og.core(k)

    def grad_act_chunk(i, carry):
        rows = pl.ds(pl.multiple_of(i * CH, CH), CH)
        grad_act[rows] = dot(ogs[rows], wd[...].reshape(WIDTH, 384))
        return carry

    lax.fori_loop(0, 4, grad_act_chunk, 0)

    mid = xs[own].astype(F32) + sum_1.total()
    middle[...] = mid
    r_two = lax.rsqrt(jnp.mean(mid * mid, axis=-1, keepdims=True) + EPS)
    h2[own_z] = (mid * r_two * gain_two[0:1]).astype(BF)
    before_h2 = links.issued()
    gather_h2.begin()
    def mlp_chunk(k):
        gather_h2.core(k)
        at = (z + k) % 4
        rows = pl.ds(pl.multiple_of(at * CH, CH), CH)
        pre = dot(h2[rows], wu[...])
        gate, up = pre[:, 0:384], pre[:, 384:768]
        sig = 1.0 / (1.0 + jnp.exp(-gate))
        silu = gate * sig
        acted = (silu * up).astype(BF)
        act[rows] = acted
        grad = grad_act[rows]
        dgu[rows, 0:384] = (grad * up * (sig * (1.0 + gate * (1.0 - sig)))).astype(BF)
        dgu[rows, 384:768] = (grad * silu).astype(BF)
        p2[rows] = dot_nt(dgu[rows], wu[...]).astype(BF)
        sum_2.send_core(at)

    def down_chunk(i, carry):
        rows = pl.ds(pl.multiple_of(i * CH, CH), CH)
        po[rows] = dot_nt(act[rows], wd[...].reshape(WIDTH, 384)).astype(BF)
        return carry

    gather_u.finish()
    mlp_chunk(0)
    gather_h2.sides()
    mlp_chunk(3)
    mlp_chunk(1)
    sum_2.cross(3)
    sum_2.cross(1)
    gather_h2.far()
    after_h2 = links.issued()
    mlp_chunk(2)
    sum_2.cross(2)
    sum_2.cross(0)

    lax.fori_loop(0, 4, down_chunk, 0)
    sum_2.relay()
    for k in range(4):
        sum_o.send_core(k)

    def mlp_weight_chunk(i, carry):
        cols = pl.ds(pl.multiple_of(i * CH, CH), CH)
        gu_full[cols] = dot_tn(h2[:, cols], dgu[...]).astype(BF)
        gd_full[i] = dot_tn(ogs[:, cols], act[...]).astype(BF).reshape(4, 64, 384)
        return carry

    lax.fori_loop(0, 4, mlp_weight_chunk, 0)
    weight_u.begin()
    weight_d.begin()

    links.drain(before_h2)
    err = sum_2.total()
    mid = middle[...]
    r_two = lax.rsqrt(jnp.mean(mid * mid, axis=-1, keepdims=True) + EPS)
    normed = mid * r_two
    part = jnp.sum(err * normed, axis=0, keepdims=True)
    gg[...] = jnp.zeros_like(gg)
    for k in range(8):
        gg[8 + k : 9 + k] = part[:, 128 * k : 128 * k + 128]
    scaled = err * gain_two[0:1]
    grad = ogs[own_z].astype(F32) + r_two * (
        scaled - normed * jnp.mean(scaled * normed, axis=-1, keepdims=True)
    )
    grad_mid[...] = grad
    gb[own] = grad.astype(BF)
    before_gb = links.issued()
    gather_gb.begin()
    dk, dv, dqkv = grad_act.at[:, 0:128], grad_act.at[:, 128:256], dgu.at[:, 0:512]
    grad_act[:, 0:256] = jnp.zeros((GROUP, 256), F32)
    gather_gb.sides()
    weight_u.relay()
    weight_d.cross()
    gather_gb.far()
    for k in range(4):
        gather_gb.core(k)
    for k in (2, 1, 3, 0):
        sum_o.cross(k)

    def out_weight_chunk(i, carry):
        cols = pl.ds(pl.multiple_of(i * CH, CH), CH)
        go_full[i] = dot_tn(gb[:, cols], mixed[...]).astype(BF).reshape(4, 64, 256)
        return carry

    def back_rope(turned, pre, gain, cos, sin):
        r = lax.rsqrt(jnp.mean(pre * pre, axis=-1, keepdims=True) + EPS)
        normed = pre * r
        err = turned * cos - pltpu.roll(turned, 64, 1) * sin
        scaled = err * gain
        grad = r * (scaled - normed * jnp.mean(scaled * normed, axis=-1, keepdims=True))
        return grad, jnp.sum(err * normed, axis=0, keepdims=True)

    lax.fori_loop(0, 4, out_weight_chunk, 0)
    weight_o.begin()

    attn_part = jnp.zeros((1, WIDTH), F32)
    p3 = h2
    links.drain(after_h2)
    for qb in (3, 2, 1, 0):
        rows = slice(qb * CH, qb * CH + CH)
        keys = CH * (qb + 1)
        cos, sin = cosine[rows], sine[rows]
        grad_mixed = dot(gb[rows], wo[...].reshape(WIDTH, 256)).astype(BF)
        grad_h = jnp.concatenate([grad_mixed[:, 0:128], grad_mixed[:, 128:256]], axis=0)
        weights = probs_of(qb)[probs_rows(qb), 0:keys]
        wide = weights.astype(F32)
        grad_probs = dot_nt(grad_h, vals[0:keys])
        inner = jnp.sum(wide * grad_probs, axis=-1, keepdims=True)
        grad_scores = (wide * (grad_probs - inner)).astype(BF)
        dk[0:keys] += dot_tn(grad_scores, q_rot[qb * 512 : qb * 512 + 512]) * SCALE
        dv[0:keys] += dot_tn(weights, grad_h)
        grad_q = (dot(grad_scores, k_rot[0:keys]) * SCALE).astype(BF).astype(F32)
        for h in range(2):
            pre = qk_pre[rows, 128 * h : 128 * h + 128]
            grad, gain_part = back_rope(grad_q[CH * h : CH * h + CH], pre, query_gain, cos, sin)
            dqkv[rows, 128 * h : 128 * h + 128] = grad.astype(BF)
            gg[16:17] += gain_part
        grad_k = dk[rows].astype(BF).astype(F32)
        grad, gain_part = back_rope(grad_k, qk_pre[rows, 256:384], key_gain, cos, sin)
        dqkv[rows, 256:384] = grad.astype(BF)
        gg[17:18] += gain_part
        dqkv[rows, 384:512] = dv[rows].astype(BF)
        err = dot_nt(dqkv[rows], wq[...])
        p3[rows] = err.astype(BF)
        send_chunk(sum_3, qb)
        attn_part += jnp.sum(err * (xs[rows].astype(F32) * r1[rows]), axis=0, keepdims=True)
        if qb == 3:
            weight_d.relay()
        if qb == 2:
            sum_o.relay()
            weight_u.spread()
            weight_o.cross()
        if qb == 1:
            for k in (2, 1, 3):
                sum_3.cross(k, when=c == 1)
            weight_d.spread()
            weight_o.relay()
            links.drain(before_gb)

    for k in (2, 1, 3):
        sum_3.cross(k, when=c == 0)
    sum_3.cross(0)
    for k in range(8):
        gg[k : k + 1] = attn_part[:, 128 * k : 128 * k + 128]
    out_tmp[...] = (middle[...] + sum_o.total()).astype(BF)
    links.send(out_tmp, out_ref, place.swap, out_id, when=away)
    for dy, dc in column:
        links.send(gg, gg_y.at[y * 2 + c], place.at(dy=dy, dc=dc), gg_y_id + y * 2 + c)

    def attn_weight_chunk(i, carry):
        cols = pl.ds(pl.multiple_of(i * CH, CH), CH)
        grad = dot_tn(h1[:, cols], dqkv[...]).astype(BF)
        gq_full[pl.ds(2 * i, 2)] = grad[:, 0:256].reshape(2, 128, 256)
        gk_full[i] = grad[:, 256:512].reshape(4, 64, 256)
        return carry

    lax.fori_loop(0, 4, attn_weight_chunk, 0)
    weight_k.begin()
    weight_q.begin()
    sum_3.relay()

    gg_y[y * 2 + c] = gg[...]
    for dy, dc in column:
        index = ((y + dy) % 4) * 2 + (c + dc) % 2
        links.wait(gg_y.at[index], place.at(dy=dy, dc=dc), gg_y_id + index)
    total = gg_y[0]
    for k in range(1, 8):
        total = total + gg_y[k]
    gg_a[...] = total
    for k in range(1, 4):
        links.send(gg_a, gg_x.at[x], place.at(dx=k), gg_x_id + x)
    weight_o.spread()
    weight_u.finish()
    weight_d.finish()
    weight_k.cross()
    weight_q.spread()

    for half in range(2):
        part = pl.ds(64 * half, 64)
        mine = pl.ds(token_rows(c, z, False) + 64 * half, 64)
        err = sum_3.half_total(half)
        r_one = r1[mine]
        normed = xs[mine].astype(F32) * r_one
        scaled = err * gain_one[0:1]
        in_grad_tmp[part] = (
            grad_mid[part]
            + r_one * (scaled - normed * jnp.mean(scaled * normed, axis=-1, keepdims=True))
        ).astype(BF)
        links.send(
            in_grad_tmp.at[part], in_grad_ref.at[part], place.swap, in_grad_id + half, when=away
        )

    gg_x[x] = gg_a[...]
    for k in range(1, 4):
        other = (x + k) % 4
        links.wait(gg_x.at[other], place.at(dx=k), gg_x_id + other)
    gg_b[...] = (gg_x[0] + gg_x[1]) + (gg_x[2] + gg_x[3])
    for k in range(1, 4):
        links.send(gg_b, gg_z.at[z], place.at(dz=k), gg_z_id + z)

    weight_k.spread()
    weight_o.finish()

    @pl.when(home)
    def _():
        out_ref[...] = out_tmp[...]
        in_grad_ref[...] = in_grad_tmp[...]

    gg_z[z] = gg_b[...]
    for k in range(1, 4):
        other = (z + k) % 4
        links.wait(gg_z.at[other], place.at(dz=k), gg_z_id + other)
    gains_ref[...] = (gg_z[0] + gg_z[1]) + (gg_z[2] + gg_z[3])

    weight_q.finish()
    weight_k.finish()
    links.wait(out_ref, place.swap, out_id, when=away)
    for half in range(2):
        part = in_grad_ref.at[pl.ds(64 * half, 64)]
        links.wait(part, place.swap, in_grad_id + half, when=away)
    links.drain(links.issued())


def run_layer(*args):
    vmem = pl.BlockSpec(memory_space=pltpu.VMEM)

    def sds(shape, kind):
        return jax.ShapeDtypeStruct(shape, kind)

    def buf(shape, kind=BF):
        return pltpu.VMEM(shape, kind)

    group = (GROUP, WIDTH)
    table = (GROUP, HEAD)
    block = (TOK, WIDTH)
    landing = [buf(group), buf((4, TOK, WIDTH)), buf((8, 64, WIDTH))]
    gains = (24, 128)

    def weight_landing(cols):
        return [buf((WIDTH, cols)), buf((10, 128, cols)), buf((4, 64, cols))]

    def weight_landing_y(cols):
        return [
            buf((4, 4, 64, cols)),
            buf((4, 4, 2, 64, cols)),
            buf((4, 2, 64, cols)),
            buf((9, 64, cols)),
            buf((64, cols)),
        ]

    scratch = [
        buf((64, NQ)),
        buf((64, NU)),
        buf((4, 64, NO)),
        buf((4, 64, ND)),
        buf((WIDTH, NQ)),
        buf((WIDTH, NU)),
        buf((4, 4, 64, NO)),
        buf((4, 4, 64, ND)),
        buf((16, 8, 128), F32),
        buf((1, WIDTH), F32),
        buf((1, WIDTH), F32),
        buf((1, 4), jnp.int32),
        buf((GROUP, 1), jnp.int32),
        buf(table, F32),
        buf(table, F32),
        buf(group),
        buf(group),
        buf(group),
        buf((GROUP, 1), F32),
        buf((GROUP, 384), F32),
        buf((2 * GROUP, HEAD)),
        buf(table),
        buf(table),
        buf((GROUP, 256)),
        buf((GROUP, 512)),
        buf((GROUP, GROUP)),
        *landing,
        buf(block, F32),
        buf(group),
        buf((GROUP, 384), F32),
        buf((GROUP, 384)),
        buf((GROUP, 768)),
        *landing,
        *landing,
        buf(group),
        buf(block, F32),
        *landing[1:],
        *weight_landing(NU),
        buf((8, 128, 256)),
        *weight_landing(256)[1:],
        *weight_landing_y(NO),
        *weight_landing_y(NO),
        *weight_landing_y(ND),
        buf(block),
        buf(block),
        buf(gains, F32),
        buf((8, *gains), F32),
        buf(gains, F32),
        buf((4, *gains), F32),
        buf(gains, F32),
        buf((4, *gains), F32),
        pltpu.SemaphoreType.DMA((N_SENDS,)),
        pltpu.SemaphoreType.DMA((N_RECVS,)),
    ]
    return pl.pallas_call(
        layer_kernel,
        out_shape=(
            sds(block, BF),
            sds(block, BF),
            sds((64, 256), F32),
            sds((64, 256), F32),
            sds((64, NO), F32),
            sds((64, NU), F32),
            sds((64, ND), F32),
            sds(gains, F32),
        ),
        in_specs=[vmem] * len(args),
        out_specs=(vmem,) * 8,
        scratch_shapes=scratch,
        name="layer",
        compiler_params=pltpu.CompilerParams(
            collective_id=0, has_side_effects=True, vmem_limit_bytes=63 * 2**20
        ),
    )(*args)


def results_kernel(
    out_in,
    in_grad_in,
    gq,
    gk,
    go,
    gu,
    gd,
    gains,
    out,
    in_grad,
    attn_gain,
    query,
    key,
    value,
    query_gain,
    key_gain,
    w_out,
    mlp_gain,
    gate,
    up,
    down,
):
    d = lax.axis_index("dp")
    out[...] = out_in[...]
    in_grad[...] = in_grad_in[...]
    query[...] = gq[...]
    key[...] = gk[:, 0:128]
    value[...] = gk[:, 128:256]
    w_out[...] = go[...]
    gate[...] = gu[:, 0:384]
    up[...] = gu[:, 384:768]
    down[...] = gd[...]
    query_gain[...] = gains[16:17]
    key_gain[...] = gains[17:18]
    for first, ref in ((0, attn_gain), (8, mlp_gain)):
        row = gains[pl.ds(first + d // 2, 1)]
        ref[...] = jnp.where(d % 2 == 1, pltpu.roll(row, 64, 1), row)[:, 0:64]


def write_results(*args):
    vmem = pl.BlockSpec(memory_space=pltpu.VMEM)
    shapes = [
        ((TOK, WIDTH), BF),
        ((TOK, WIDTH), BF),
        ((1, 64), F32),
        ((64, 256), F32),
        ((64, 128), F32),
        ((64, 128), F32),
        ((1, 128), F32),
        ((1, 128), F32),
        ((64, 256), F32),
        ((1, 64), F32),
        ((64, 384), F32),
        ((64, 384), F32),
        ((64, 384), F32),
    ]
    return pl.pallas_call(
        results_kernel,
        out_shape=tuple(jax.ShapeDtypeStruct(shape, kind) for shape, kind in shapes),
        in_specs=[vmem] * len(args),
        out_specs=(vmem,) * len(shapes),
        name="results",
    )(*args)


def per_device(
    layer_input,
    seq_lengths,
    attn_gain,
    w_query,
    key_projection,
    value_projection,
    query_gain,
    key_gain,
    w_out,
    mlp_gain,
    w_gate,
    w_up,
    w_down,
    out_grad,
):
    frequency = ROPE_BASE ** (-(np.arange(HEAD // 2) * 2.0 / HEAD)).astype(np.float32)
    parts = run_layer(
        w_query,
        key_projection,
        value_projection,
        w_out.T,
        w_gate,
        w_up,
        w_down.T,
        attn_gain[None],
        mlp_gain[None],
        layer_input,
        out_grad,
        query_gain[None],
        key_gain[None],
        seq_lengths,
        np.concatenate([frequency, frequency]).astype(np.float32)[None],
    )
    results = list(write_results(*parts))
    for k in (2, 6, 7, 9):
        results[k] = results[k].reshape(-1)
    results[8], results[12] = results[8].T, results[12].T
    return tuple(results)


def solution(mesh):
    both = P(("dp", "tensor"), None)
    split = P("dp", "tensor")
    turned = P("tensor", "dp")
    in_specs = (
        both,
        P("dp", None),
        P("dp"),
        split,
        split,
        split,
        P(),
        P(),
        turned,
        P("dp"),
        split,
        split,
        turned,
        both,
    )
    out_specs = (both, both, P("dp"), split, split, split, P(), P(), turned, P("dp"), split, split, turned)
    return jax.shard_map(
        per_device, mesh=mesh, in_specs=in_specs, out_specs=out_specs, check_vma=False
    )
```

```python
import functools

import jax
import jax.numpy as jnp
import numpy as np
from jax import lax
from jax.experimental import pallas as pl
from jax.experimental.pallas import tpu as pltpu
from jax.sharding import PartitionSpec as P

MESH = pl.DeviceIdType.MESH
BF = jnp.bfloat16
F32 = jnp.float32
HEAD = 128
EPS = 1e-06
ROPE_BASE = 1000000.0
MASKED = -1e30
SCALE = HEAD ** (-0.5)
TOK = 128
GROUP = 1024
WIDTH = 1024
NQ = 512
NO = 256
NU = 768
ND = 384
CH = 256
N_SENDS = 101
N_RECVS = 195


def dot(a, b):
    return jnp.dot(a, b, preferred_element_type=F32)


def dot_nt(a, b):
    return lax.dot_general(a, b, (((1,), (1,)), ((), ())), preferred_element_type=F32)


def dot_tn(a, b):
    return lax.dot_general(a, b, (((0,), (0,)), ((), ())), preferred_element_type=F32)


class Links:
    def __init__(self, send_sems, recv_sems):
        self.send_sems, self.recv_sems = send_sems, recv_sems
        self.sends, self.recvs = 0, 0
        self.pending, self.free, self.drained = [], [], 0

    def recv_ids(self, count=1):
        first = self.recvs
        self.recvs += count
        assert self.recvs <= N_RECVS
        return first

    def copy(self, src, dst, device, send_id, recv_id):
        return pltpu.make_async_remote_copy(
            src_ref=src,
            dst_ref=dst,
            send_sem=self.send_sems.at[send_id],
            recv_sem=self.recv_sems.at[recv_id],
            device_id=device,
            device_id_type=MESH,
        )

    def send_id(self):
        if self.free:
            return self.free.pop()
        self.sends += 1
        assert self.sends <= N_SENDS
        return self.sends - 1

    def send(self, src, dst, device, recv_id, when=None, send_id=None):
        if send_id is None:
            send_id = self.send_id()
        copy = self.copy(src, dst, device, send_id, recv_id)
        if when is None:
            copy.start()
        else:
            pl.when(when)(copy.start)
        self.pending.append((copy, when, send_id))

    def wait(self, dst, device, recv_id, when=None):
        copy = self.copy(dst, dst, device, 0, recv_id)
        if when is None:
            copy.wait_recv()
        else:
            pl.when(when)(copy.wait_recv)

    def issued(self):
        return self.drained + len(self.pending)

    def drain(self, upto):
        count = upto - self.drained
        done, self.pending, self.drained = self.pending[:count], self.pending[count:], upto
        for copy, when, _ in done:
            if when is None:
                copy.wait_send()
            else:
                pl.when(when)(copy.wait_send)
        self.free += sorted({send_id for _, _, send_id in done})


class Place:
    def __init__(self):
        d, t = lax.axis_index("dp"), lax.axis_index("tensor")
        self.d = d
        self.x, self.c = d // 4, d % 2
        self.y, self.z = (t // 4) * 2 + (d // 2) % 2, t % 4
        self.home = self.c == t // 4
        self.left_z, self.right_z = self.at(dz=3), self.at(dz=1)
        self.left_x, self.right_x = self.at(dx=3), self.at(dx=1)
        self.core = self.at(dc=1)
        self.swap = self.at(dy=2, dc=1)

    def device(self, x, y, z, c):
        return (x * 4 + (y % 2) * 2 + c, (y // 2) * 4 + z)

    def at(self, dx=0, dy=0, dz=0, dc=0):
        return self.device((self.x + dx) % 4, (self.y + dy) % 4, (self.z + dz) % 4, (self.c + dc) % 2)


class WeightGather:
    def __init__(self, links, place, own, buf):
        self.links, self.place, self.own, self.buf = links, place, own, buf
        self.y_id = links.recv_ids(4)
        self.ids = {name: links.recv_ids() for name in ("xm", "xp", "l", "r")}

    def block(self, index):
        return self.buf.at[pl.ds(pl.multiple_of(index * 64, 64), 64)]

    def rows(self, dx, half=None):
        first = ((self.place.x + dx) % 4) * 256
        if half is None:
            return self.buf.at[pl.ds(pl.multiple_of(first, 256), 256)]
        return self.buf.at[pl.ds(pl.multiple_of(first + 128 * half, 128), 128)]

    def begin(self):
        place, links = self.place, self.links
        side = place.y // 2
        for dy in (2, 1, 3, 0):
            device = place.device(place.x, (place.y + dy) % 4, place.z, side)
            links.send(
                self.own,
                self.block(place.d),
                device,
                self.y_id + place.d % 4,
                when=(place.c != side) if dy == 0 else None,
            )

        @pl.when(place.c == side)
        def _():
            self.block(place.d)[...] = self.own[...]

    def second(self):
        place, links = self.place, self.links
        for low in range(2):
            for core in range(2):
                y = 2 * place.c + low
                links.wait(
                    self.block(place.x * 4 + low * 2 + core),
                    place.device(place.x, y, place.z, core),
                    self.y_id + low * 2 + core,
                    when=(y != place.y) | (core != place.c),
                )
        mine = self.rows(0)
        links.send(mine, mine, place.right_x, self.ids["xm"])
        links.send(mine, mine, place.left_x, self.ids["xp"])

    def third(self):
        place, links = self.place, self.links
        links.wait(self.rows(3), place.left_x, self.ids["xm"])
        half = self.rows(3, 0)
        links.send(half, half, place.right_x, self.ids["l"])
        links.wait(self.rows(1), place.right_x, self.ids["xp"])
        half = self.rows(1, 1)
        links.send(half, half, place.left_x, self.ids["r"])

    def finish(self):
        place, links = self.place, self.links
        links.wait(self.rows(2, 0), place.left_x, self.ids["l"])
        links.wait(self.rows(2, 1), place.right_x, self.ids["r"])


class WeightSum:
    def __init__(self, links, place, full, side, land, out):
        self.links, self.place, self.full = links, place, full
        self.side, self.land, self.out = side, land, out
        self.ids = {n: links.recv_ids() for n in ("la", "lr", "ra", "rr", "lc", "rc")}
        self.y_id = links.recv_ids(4)

    def rows(self, dx, half):
        return pl.ds(pl.multiple_of(((self.place.x + dx) % 4) * 256 + 128 * half, 128), 128)

    def begin(self):
        place, links, side = self.place, self.links, self.side
        links.send(self.full.at[self.rows(2, 0)], side.at[0], place.right_x, self.ids["la"])
        links.send(self.full.at[self.rows(2, 1)], side.at[2], place.left_x, self.ids["ra"])
        links.send(self.full.at[self.rows(1, 1)], side.at[1], place.right_x, self.ids["lr"])
        links.send(self.full.at[self.rows(3, 0)], side.at[3], place.left_x, self.ids["rr"])

    def relay(self):
        place, links, side = self.place, self.links, self.side
        links.wait(side.at[0], place.left_x, self.ids["la"])
        side[6] = (self.full[self.rows(1, 0)].astype(F32) + side[0].astype(F32)).astype(BF)
        links.send(side.at[6], side.at[4], place.right_x, self.ids["lc"])
        links.wait(side.at[2], place.right_x, self.ids["ra"])
        side[7] = (self.full[self.rows(3, 1)].astype(F32) + side[2].astype(F32)).astype(BF)
        links.send(side.at[7], side.at[5], place.left_x, self.ids["rc"])

    def gathered(self):
        place, links, side = self.place, self.links, self.side
        links.wait(side.at[1], place.left_x, self.ids["lr"])
        links.wait(side.at[3], place.right_x, self.ids["rr"])
        links.wait(side.at[4], place.left_x, self.ids["lc"])
        links.wait(side.at[5], place.right_x, self.ids["rc"])
        for half, first, other in ((0, 4, 3), (1, 5, 1)):
            side[8 + half] = (
                self.full[self.rows(0, half)].astype(F32)
                + side[first].astype(F32)
                + side[other].astype(F32)
            ).astype(BF)

    def spread(self):
        self.gathered()
        place, links, side = self.place, self.links, self.side
        for low in range(2):
            for core in range(2):
                y = 2 * place.c + low
                away = (y != place.y) | (core != place.c)
                piece = side.at[8 + low, pl.ds(64 * core, 64)]
                links.send(
                    piece,
                    self.land.at[place.y],
                    place.device(place.x, y, place.z, core),
                    self.y_id + place.y,
                    when=away,
                )

                @pl.when(jnp.logical_not(away))
                def _():
                    self.land[place.y] = piece[...]

    def finish(self):
        place, links = self.place, self.links
        core = place.y // 2
        for k in range(4):
            y = (place.y + k) % 4
            links.wait(
                self.land.at[y],
                place.device(place.x, y, place.z, core),
                self.y_id + y,
                when=(place.c != core) if k == 0 else None,
            )
        total = self.land[0].astype(F32)
        for y in range(1, 4):
            total = total + self.land[y].astype(F32)
        self.out[...] = total


class WeightSumDirect(WeightSum):
    def begin(self):
        place = self.place
        for k, name in ((2, "ra"), (1, "la"), (3, "lr")):
            self.links.send(
                self.full.at[pl.ds(((place.x + k) % 4) * 2, 2)],
                self.side.at[pl.ds(2 * (k - 1), 2)],
                place.at(dx=k),
                self.ids[name],
            )

    def gathered(self):
        place, side = self.place, self.side
        for k, name in ((1, "la"), (3, "lr"), (2, "ra")):
            self.links.wait(side.at[pl.ds(2 * (k - 1), 2)], place.at(dx=4 - k), self.ids[name])
        for half in range(2):
            total = self.full[place.x * 2 + half].astype(F32)
            for k in range(3):
                total = total + side[2 * k + half].astype(F32)
            side[8 + half] = total.astype(BF)


class WeightGatherX:
    def __init__(self, links, place, own, stage, buf):
        self.links, self.place, self.own, self.stage, self.buf = links, place, own, stage, buf
        self.y_id = links.recv_ids(4)
        self.ids = {name: links.recv_ids() for name in ("xm", "xp", "l", "r")}

    def block(self, dx, half=None):
        at = (self.place.x + dx) % 4
        if half is None:
            return self.stage.at[at]
        return self.stage.at[at, pl.ds(32 * half, 32)]

    def begin(self):
        place, links = self.place, self.links
        links.send(self.own, self.block(0), place.right_x, self.ids["xm"])
        links.send(self.own, self.block(0), place.left_x, self.ids["xp"])
        self.stage[place.x] = self.own[...]

    def relay(self):
        place, links = self.place, self.links
        links.wait(self.block(3), place.left_x, self.ids["xm"])
        links.send(self.block(3, 0), self.block(3, 0), place.right_x, self.ids["l"])
        links.wait(self.block(1), place.right_x, self.ids["xp"])
        links.send(self.block(1, 1), self.block(1, 1), place.left_x, self.ids["r"])

    def spread(self):
        place, links = self.place, self.links
        links.wait(self.block(2, 0), place.left_x, self.ids["l"])
        links.wait(self.block(2, 1), place.right_x, self.ids["r"])
        side = place.y // 2
        for dy in (2, 1, 3, 0):
            links.send(
                self.stage,
                self.buf.at[:, place.d % 4],
                place.device(place.x, (place.y + dy) % 4, place.z, side),
                self.y_id + place.d % 4,
                when=(place.c != side) if dy == 0 else None,
            )

        @pl.when(place.c == side)
        def _():
            self.buf[:, place.d % 4] = self.stage[...]

    def finish(self):
        place, links = self.place, self.links
        for low in range(2):
            for core in range(2):
                y = 2 * place.c + low
                links.wait(
                    self.buf.at[:, low * 2 + core],
                    place.device(place.x, y, place.z, core),
                    self.y_id + low * 2 + core,
                    when=(y != place.y) | (core != place.c),
                )


class WeightSumY:
    def __init__(self, links, place, full, land, total, side, last, out):
        self.links, self.place, self.full, self.land = links, place, full, land
        self.total, self.side, self.last, self.out = total, side, last, out
        self.y_id = links.recv_ids(4)
        self.ids = {n: links.recv_ids() for n in ("la", "lr", "ra", "rr", "lc", "rc", "core")}
        self.active = place.c == place.y // 2

    def begin(self):
        place = self.place
        for low in range(2):
            y = 2 * place.c + low
            self.links.send(
                self.full.at[:, pl.ds(2 * low, 2)],
                self.land.at[place.y],
                place.device(place.x, y, place.z, place.c),
                self.y_id + place.y,
                when=y != place.y,
            )

    def cross(self):
        place, links, side, active = self.place, self.links, self.side, self.active
        x = place.x
        for k in range(1, 4):
            y = (place.y + k) % 4
            links.wait(
                self.land.at[y], place.device(x, y, place.z, place.c), self.y_id + y, when=active
            )

        @pl.when(active)
        def _():
            def add(i, carry):
                acc = self.full[i, pl.ds((place.y % 2) * 2, 2)].astype(F32)
                for k in range(1, 4):
                    acc = acc + self.land[(place.y + k) % 4, i].astype(F32)
                self.total[i] = acc.astype(BF)
                return carry

            lax.fori_loop(0, 4, add, 0)

        self.ring()

    def ring(self):
        links, place, active, side, x = self.links, self.place, self.active, self.side, self.place.x
        total, ids = self.total, self.ids
        links.send(total.at[(x + 2) % 4, 0], side.at[0], place.right_x, ids["la"], when=active)
        links.send(total.at[(x + 2) % 4, 1], side.at[2], place.left_x, ids["ra"], when=active)
        links.send(total.at[(x + 1) % 4, 1], side.at[1], place.right_x, ids["lr"], when=active)
        links.send(total.at[(x + 3) % 4, 0], side.at[3], place.left_x, ids["rr"], when=active)

    def relay(self):
        place, links, side, ids, active = self.place, self.links, self.side, self.ids, self.active
        x = place.x
        links.wait(side.at[0], place.left_x, ids["la"], when=active)
        links.wait(side.at[2], place.right_x, ids["ra"], when=active)

        @pl.when(active)
        def _():
            side[6] = (self.total[(x + 1) % 4, 0].astype(F32) + side[0].astype(F32)).astype(BF)
            side[7] = (self.total[(x + 3) % 4, 1].astype(F32) + side[2].astype(F32)).astype(BF)

        links.send(side.at[6], side.at[4], place.right_x, ids["lc"], when=active)
        links.send(side.at[7], side.at[5], place.left_x, ids["rc"], when=active)

    def spread(self):
        place, links, side, ids, active = self.place, self.links, self.side, self.ids, self.active
        x = place.x
        links.wait(side.at[1], place.left_x, ids["lr"], when=active)
        links.wait(side.at[3], place.right_x, ids["rr"], when=active)
        links.wait(side.at[4], place.left_x, ids["lc"], when=active)
        links.wait(side.at[5], place.right_x, ids["rc"], when=active)

        self.deliver(((4, 3), (5, 1)))

    def deliver(self, slots):
        place, links, side, ids, active = self.place, self.links, self.side, self.ids, self.active
        x = place.x

        @pl.when(active)
        def _():
            sums = []
            for half in range(2):
                total = self.total[x, half].astype(F32)
                for slot in slots[half]:
                    total = total + side[slot].astype(F32)
                sums.append(total)
            zero, one = sums
            self.out[...] = jnp.where(place.c == 0, zero, one)
            side[8] = jnp.where(place.c == 0, one, zero).astype(BF)

        links.send(side.at[8], self.last, place.core, ids["core"], when=active)

    def finish(self):
        idle = jnp.logical_not(self.active)
        self.links.wait(self.last, self.place.core, self.ids["core"], when=idle)

        @pl.when(idle)
        def _():
            self.out[...] = self.last[...].astype(F32)


class WeightSumYDirect(WeightSumY):
    def ring(self):
        place = self.place
        for k, name in ((2, "ra"), (1, "la"), (3, "lr")):
            self.links.send(
                self.total.at[(place.x + k) % 4],
                self.side.at[pl.ds(2 * (k - 1), 2)],
                place.at(dx=k),
                self.ids[name],
                when=self.active,
            )

    def spread(self):
        for k, name in ((1, "la"), (3, "lr"), (2, "ra")):
            self.links.wait(
                self.side.at[pl.ds(2 * (k - 1), 2)],
                self.place.at(dx=4 - k),
                self.ids[name],
                when=self.active,
            )
        self.deliver(((0, 2, 4), (1, 3, 5)))


def token_rows(c, z, by_z):
    index = z * 2 + c if by_z else c * 4 + z
    return pl.multiple_of(index * TOK, TOK)


class TokenSum:
    def __init__(self, links, place, partial, core_in, side, by_z):
        self.links, self.place, self.partial = links, place, partial
        self.core_in, self.side, self.by_z = core_in, side, by_z
        self.core_id = links.recv_ids(4)
        self.ids = {n: links.recv_ids() for n in ("la", "lr", "ra", "rr", "lc", "rc")}
        self.shared = {}

    def send_id(self, name):
        if name not in self.shared:
            self.shared[name] = self.links.send_id()
        return self.shared[name]

    def rows(self, c, z):
        return pl.ds(token_rows(c, z, self.by_z), TOK)

    def send_core(self, z, when=None):
        place = self.place
        self.links.send(
            self.partial.at[self.rows((place.c + 1) % 2, z)],
            self.core_in.at[z],
            place.core,
            self.core_id + z,
            when=when,
            send_id=None if when is None else self.send_id(z),
        )

    def half(self, z, h):
        return pl.ds(token_rows(self.place.c, z, self.by_z) + 64 * h, 64)

    def cross(self, k, when=None):
        place, links, side, ids = self.place, self.links, self.side, self.ids
        z = (place.z + k) % 4
        links.wait(self.core_in.at[z], place.core, self.core_id + z, when=when)

        def add():
            rows = self.rows(place.c, z)
            self.partial[rows] = (
                self.partial[rows].astype(F32) + self.core_in[z].astype(F32)
            ).astype(BF)

        if when is None:
            add()
        else:
            pl.when(when)(add)
        low, high = self.partial.at[self.half(z, 0)], self.partial.at[self.half(z, 1)]
        for at, ref, slot, device, name in (
            (2, low, 0, place.right_z, "la"),
            (2, high, 2, place.left_z, "ra"),
            (1, high, 1, place.right_z, "lr"),
            (3, low, 3, place.left_z, "rr"),
        ):
            if k == at:
                send_id = None if when is None else self.send_id(name)
                links.send(ref, side.at[slot], device, ids[name], when=when, send_id=send_id)

    def relay(self):
        place, links, side = self.place, self.links, self.side
        z = place.z
        links.wait(side.at[0], place.left_z, self.ids["la"])
        side[6] = (self.partial[self.half((z + 1) % 4, 0)].astype(F32) + side[0].astype(F32)).astype(BF)
        links.send(side.at[6], side.at[4], place.right_z, self.ids["lc"])
        links.wait(side.at[2], place.right_z, self.ids["ra"])
        side[7] = (self.partial[self.half((z + 3) % 4, 1)].astype(F32) + side[2].astype(F32)).astype(BF)
        links.send(side.at[7], side.at[5], place.left_z, self.ids["rc"])

    def total(self):
        place, links, side = self.place, self.links, self.side
        links.wait(side.at[1], place.left_z, self.ids["lr"])
        links.wait(side.at[3], place.right_z, self.ids["rr"])
        links.wait(side.at[4], place.left_z, self.ids["lc"])
        links.wait(side.at[5], place.right_z, self.ids["rc"])
        return jnp.concatenate([self.half_sum(0), self.half_sum(1)], axis=0)

    def half_sum(self, half):
        first, other = ((4, 3), (5, 1))[half]
        return (
            self.partial[self.half(self.place.z, half)].astype(F32)
            + self.side[first].astype(F32)
            + self.side[other].astype(F32)
        )

    def half_total(self, half):
        place, links, side = self.place, self.links, self.side
        if half == 0:
            links.wait(side.at[3], place.right_z, self.ids["rr"])
            links.wait(side.at[4], place.left_z, self.ids["lc"])
        else:
            links.wait(side.at[1], place.left_z, self.ids["lr"])
            links.wait(side.at[5], place.right_z, self.ids["rc"])
        return self.half_sum(half)


class TokenGather:
    def __init__(self, links, place, buf, by_z):
        self.links, self.place, self.buf, self.by_z = links, place, buf, by_z
        names = ("zm0", "zm1", "zp0", "zp1", "l", "r", "c0", "c1", "c2", "c3")
        self.ids = {name: links.recv_ids() for name in names}

    def rows(self, k, core=0, half=None):
        place = self.place
        first = token_rows((place.c + core) % 2, (place.z + k) % 4, self.by_z)
        if half is None:
            return self.buf.at[pl.ds(first, TOK)]
        return self.buf.at[pl.ds(first + 64 * half, 64)]

    def push(self, ref, device, name):
        self.links.send(ref, ref, device, self.ids[name])

    def begin(self):
        place = self.place
        self.push(self.rows(0, half=0), place.right_z, "zm0")
        self.push(self.rows(0, half=1), place.left_z, "zp1")
        self.push(self.rows(0), place.core, "c0")
        self.push(self.rows(0, half=1), place.right_z, "zm1")
        self.push(self.rows(0, half=0), place.left_z, "zp0")

    def sides(self):
        place, links, ids = self.place, self.links, self.ids
        links.wait(self.rows(3, half=0), place.left_z, ids["zm0"])
        self.push(self.rows(3, half=0), place.right_z, "l")
        links.wait(self.rows(1, half=1), place.right_z, ids["zp1"])
        self.push(self.rows(1, half=1), place.left_z, "r")
        links.wait(self.rows(3, half=1), place.left_z, ids["zm1"])
        self.push(self.rows(3), place.core, "c3")
        links.wait(self.rows(1, half=0), place.right_z, ids["zp0"])
        self.push(self.rows(1), place.core, "c1")

    def far(self):
        place = self.place
        self.links.wait(self.rows(2, half=0), place.left_z, self.ids["l"])
        self.links.wait(self.rows(2, half=1), place.right_z, self.ids["r"])
        self.push(self.rows(2), place.core, "c2")

    def core(self, k):
        self.links.wait(self.rows(k, core=1), self.place.core, self.ids["c%d" % k])


def layer_kernel(
    w_query,
    w_key,
    w_value,
    w_out,
    w_gate,
    w_up,
    w_down,
    attn_gain,
    mlp_gain,
    x_own,
    og_own,
    query_gain_in,
    key_gain_in,
    lengths_own,
    frequency,
    out_ref,
    in_grad_ref,
    gq_ref,
    gk_ref,
    go_ref,
    gu_ref,
    gd_ref,
    gains_ref,
    wq_own,
    wu_own,
    wo_stage,
    wd_stage,
    wq,
    wu,
    wo,
    wd,
    gain_in,
    gain_one,
    gain_two,
    lengths,
    starts,
    cosine,
    sine,
    xs,
    ogs,
    h1,
    r1,
    qk_pre,
    q_rot,
    k_rot,
    vals,
    mixed,
    probs_low,
    probs_high,
    p1,
    p1_core,
    p1_side,
    middle,
    h2,
    grad_act,
    act,
    dgu,
    p2,
    p2_core,
    p2_side,
    po,
    po_core,
    po_side,
    gb,
    grad_mid,
    p3_core,
    p3_side,
    gu_full,
    gu_side,
    gu_land,
    gq_full,
    gq_side,
    gq_land,
    gk_full,
    gk_land,
    gk_total,
    gk_side,
    gk_last,
    go_full,
    go_land,
    go_total,
    go_side,
    go_last,
    gd_full,
    gd_land,
    gd_total,
    gd_side,
    gd_last,
    out_tmp,
    in_grad_tmp,
    gg,
    gg_y,
    gg_a,
    gg_x,
    gg_b,
    gg_z,
    send_sems,
    recv_sems,
):
    links = Links(send_sems, recv_sems)
    place = Place()
    x, y, z, c = place.x, place.y, place.z, place.c
    home, away = place.home, jnp.logical_not(place.home)
    own = pl.ds(token_rows(c, z, False), TOK)
    own_z = pl.ds(token_rows(c, z, True), TOK)
    swap_own = pl.ds(token_rows((c + 1) % 2, z, False), TOK)
    swap_z = pl.ds(token_rows((c + 1) % 2, z, True), TOK)
    column = [(dy, dc) for dy in range(4) for dc in range(2) if dy or dc]

    barrier = pltpu.get_barrier_semaphore()
    for peer in (
        [place.at(dy=dy, dc=dc) for dy, dc in column]
        + [place.at(dx=k) for k in range(1, 4)]
        + [place.at(dz=k) for k in range(1, 4)]
    ):
        pl.semaphore_signal(barrier, inc=1, device_id=peer, device_id_type=MESH)

    gather_q = WeightGather(links, place, wq_own, wq)
    gather_u = WeightGather(links, place, wu_own, wu)
    gather_o = WeightGatherX(links, place, w_out, wo_stage, wo)
    gather_d = WeightGatherX(links, place, w_down, wd_stage, wd)
    gather_x = TokenGather(links, place, xs, False)
    gather_og = TokenGather(links, place, ogs, True)
    gather_h2 = TokenGather(links, place, h2, True)
    gather_gb = TokenGather(links, place, gb, False)
    sum_1 = TokenSum(links, place, p1, p1_core, p1_side, False)
    sum_2 = TokenSum(links, place, p2, p2_core, p2_side, True)
    sum_o = TokenSum(links, place, po, po_core, po_side, True)
    sum_3 = TokenSum(links, place, h2, p3_core, p3_side, False)
    weight_u = WeightSum(links, place, gu_full, gu_side, gu_land, gu_ref)
    weight_q = WeightSumDirect(links, place, gq_full, gq_side, gq_land, gq_ref)
    weight_k = WeightSumYDirect(links, place, gk_full, gk_land, gk_total, gk_side, gk_last, gk_ref)
    weight_o = WeightSumY(links, place, go_full, go_land, go_total, go_side, go_last, go_ref)
    weight_d = WeightSumY(links, place, gd_full, gd_land, gd_total, gd_side, gd_last, gd_ref)
    x_id, og_id, lengths_id, out_id = [links.recv_ids() for _ in range(4)]
    in_grad_id = links.recv_ids(2)
    gain_id, gain_x_id = links.recv_ids(4), links.recv_ids(4)
    gg_y_id, gg_x_id, gg_z_id = links.recv_ids(8), links.recv_ids(4), links.recv_ids(4)

    @pl.when(home)
    def _():
        xs[own] = x_own[...]
        ogs[own_z] = og_own[...]
        lengths[...] = lengths_own[...]

    wq_own[:, 0:256] = w_query[...]
    wq_own[:, 256:384] = w_key[...]
    wq_own[:, 384:512] = w_value[...]
    wu_own[:, 0:384] = w_gate[...]
    wu_own[:, 384:768] = w_up[...]
    gain_in[place.d, :, 0:64] = jnp.broadcast_to(attn_gain[...].astype(F32), (8, 64))
    gain_in[place.d, :, 64:128] = jnp.broadcast_to(mlp_gain[...].astype(F32), (8, 64))
    query_gain, key_gain = query_gain_in[...].astype(F32), key_gain_in[...].astype(F32)

    pl.semaphore_wait(barrier, 13)

    links.send(x_own, xs.at[swap_own], place.swap, x_id, when=away)
    gather_o.begin()
    gather_d.begin()
    gather_q.begin()
    for dy, dc in ((0, 1), (1, 0), (1, 1)):
        other_y = (y // 2) * 2 + (y % 2 + dy) % 2
        peer = place.device(x, other_y, z, (c + dc) % 2)
        links.send(gain_in.at[place.d], gain_in.at[place.d], peer, gain_id + place.d % 4)
    links.send(lengths_own, lengths, place.core, lengths_id, when=home)

    links.wait(xs.at[own], place.swap, x_id, when=away)
    gather_x.begin()
    gather_o.relay()
    gather_d.relay()
    gather_q.second()
    for dy, dc in ((0, 1), (1, 0), (1, 1)):
        other_y = (y // 2) * 2 + (y % 2 + dy) % 2
        index = x * 4 + (other_y % 2) * 2 + (c + dc) % 2
        peer = place.device(x, other_y, z, (c + dc) % 2)
        links.wait(gain_in.at[index], peer, gain_id + index % 4)
    four = pl.ds(x * 4, 4)
    for k in range(1, 4):
        links.send(gain_in.at[four], gain_in.at[four], place.at(dx=k), gain_x_id + x)
    links.send(og_own, ogs.at[swap_z], place.swap, og_id, when=away)
    gather_o.spread()
    gather_u.begin()

    low = lax.broadcasted_iota(jnp.int32, (1, 128), 1) < 64
    links.wait(lengths, place.core, lengths_id, when=away)

    def trig_chunk(i, carry):
        rows = pl.ds(pl.multiple_of(i * CH, CH), CH)
        at = lax.broadcasted_iota(jnp.int32, (CH, 1), 0) + i * CH
        end, start = jnp.zeros((1, 1), jnp.int32), jnp.zeros((CH, 1), jnp.int32)
        for k in range(3):
            end = end + lengths[0:1, k : k + 1]
            start = jnp.where(at >= end, end, start)
        starts[rows] = start
        angles = (at - start).astype(F32) * frequency[0:1]
        cosine[rows] = jnp.cos(angles)
        turned = jnp.sin(angles)
        sine[rows] = jnp.where(low, -turned, turned)
        return carry

    lax.fori_loop(0, 4, trig_chunk, 0)

    gather_x.sides()
    gather_q.third()
    gather_d.spread()
    for k in range(1, 4):
        other = (x + k) % 4
        links.wait(gain_in.at[pl.ds(other * 4, 4)], place.at(dx=k), gain_x_id + other)
    for k in range(8):
        even, odd = gain_in[2 * k][0:1], gain_in[2 * k + 1][0:1]
        cols = slice(128 * k, 128 * k + 128)
        gain_one[0:1, cols] = jnp.where(low, even, pltpu.roll(odd, 64, 1))
        gain_two[0:1, cols] = jnp.where(low, pltpu.roll(even, 64, 1), odd)


    def norm_pair(k):
        for core in range(2):
            norm_rows(pl.ds(token_rows((c + core) % 2, (z + k) % 4, False), TOK))

    def norm_rows(rows):
        wide = xs[rows].astype(F32)
        r = lax.rsqrt(jnp.mean(wide * wide, axis=-1, keepdims=True) + EPS)
        r1[rows] = r
        h1[rows] = (wide * r * gain_one[0:1]).astype(BF)

    for k in (0, 3, 1):
        gather_x.core(k)
        norm_pair(k)
    gather_x.far()
    links.wait(ogs.at[own_z], place.swap, og_id, when=away)
    gather_og.begin()
    gather_x.core(2)
    norm_pair(2)
    gather_q.finish()

    def qkv_chunk(i, carry):
        rows = pl.ds(pl.multiple_of(i * CH, CH), CH)
        pre = dot(h1[rows], wq[...])
        qk_pre[rows] = pre[:, 0:384]
        vals[rows] = pre[:, 384:512].astype(BF)
        cos, sin = cosine[rows], sine[rows]
        for h in range(3):
            part = pre[:, 128 * h : 128 * h + 128]
            r = lax.rsqrt(jnp.mean(part * part, axis=-1, keepdims=True) + EPS)
            scaled = part * r * (query_gain if h < 2 else key_gain)
            turned = (scaled * cos + pltpu.roll(scaled, 64, 1) * sin).astype(BF)
            if h < 2:
                q_rot[pl.ds(pl.multiple_of(i * 512 + h * CH, CH), CH)] = turned
            else:
                k_rot[rows] = turned
        return carry

    lax.fori_loop(0, 4, qkv_chunk, 0)
    gather_u.second()
    gather_o.finish()
    gather_og.sides()

    def allowed(qb, keys):
        key_at = lax.broadcasted_iota(jnp.int32, (CH, keys), 1)
        query_at = lax.broadcasted_iota(jnp.int32, (CH, keys), 0) + qb * CH
        return (key_at >= starts[qb * CH : qb * CH + CH]) & (key_at <= query_at)

    def probs_of(qb):
        return probs_low if qb < 2 else probs_high

    def probs_rows(qb):
        return slice((qb % 2) * 512, (qb % 2) * 512 + 512)

    def send_chunk(group_sum, qb):
        for b in (2 * qb, 2 * qb + 1):
            group_sum.send_core(b % 4, when=c != b // 4)

    for qb in range(4):
        rows = slice(qb * CH, qb * CH + CH)
        keys = CH * (qb + 1)
        ok = allowed(qb, keys)
        scores = dot_nt(q_rot[qb * 512 : qb * 512 + 512], k_rot[0:keys]).reshape(2, CH, keys)
        scores = jnp.where(ok[None], scores * SCALE, MASKED)
        terms = jnp.exp(scores - jnp.max(scores, axis=-1, keepdims=True))
        weights = terms * (1.0 / jnp.sum(terms, axis=-1, keepdims=True))
        weights = weights.astype(BF).reshape(512, keys)
        probs_of(qb)[probs_rows(qb), 0:keys] = weights
        both = dot(weights, vals[0:keys]).astype(BF)
        mixed[rows, 0:128] = both[0:CH]
        mixed[rows, 128:256] = both[CH:512]
        p1[rows] = dot_nt(mixed[rows], wo[...].reshape(WIDTH, 256)).astype(BF)
        send_chunk(sum_1, qb)
        if qb == 2:
            for k in (2, 1, 3):
                sum_1.cross(k, when=c == 0)

    for k in (2, 1, 3):
        sum_1.cross(k, when=c == 1)
    sum_1.cross(0)
    gather_u.third()
    gather_og.far()
    sum_1.relay()

    gather_d.finish()
    for k in range(4):
        gather_og.core(k)

    def grad_act_chunk(i, carry):
        rows = pl.ds(pl.multiple_of(i * CH, CH), CH)
        grad_act[rows] = dot(ogs[rows], wd[...].reshape(WIDTH, 384))
        return carry

    lax.fori_loop(0, 4, grad_act_chunk, 0)

    mid = xs[own].astype(F32) + sum_1.total()
    middle[...] = mid
    r_two = lax.rsqrt(jnp.mean(mid * mid, axis=-1, keepdims=True) + EPS)
    h2[own_z] = (mid * r_two * gain_two[0:1]).astype(BF)
    before_h2 = links.issued()
    gather_h2.begin()
    def mlp_chunk(k):
        gather_h2.core(k)
        at = (z + k) % 4
        rows = pl.ds(pl.multiple_of(at * CH, CH), CH)
        pre = dot(h2[rows], wu[...])
        gate, up = pre[:, 0:384], pre[:, 384:768]
        sig = 1.0 / (1.0 + jnp.exp(-gate))
        silu = gate * sig
        acted = (silu * up).astype(BF)
        act[rows] = acted
        grad = grad_act[rows]
        dgu[rows, 0:384] = (grad * up * (sig * (1.0 + gate * (1.0 - sig)))).astype(BF)
        dgu[rows, 384:768] = (grad * silu).astype(BF)
        p2[rows] = dot_nt(dgu[rows], wu[...]).astype(BF)
        sum_2.send_core(at)

    def down_chunk(i, carry):
        rows = pl.ds(pl.multiple_of(i * CH, CH), CH)
        po[rows] = dot_nt(act[rows], wd[...].reshape(WIDTH, 384)).astype(BF)
        return carry

    gather_u.finish()
    mlp_chunk(0)
    gather_h2.sides()
    mlp_chunk(3)
    mlp_chunk(1)
    sum_2.cross(3)
    sum_2.cross(1)
    gather_h2.far()
    after_h2 = links.issued()
    mlp_chunk(2)
    sum_2.cross(2)
    sum_2.cross(0)

    lax.fori_loop(0, 4, down_chunk, 0)
    sum_2.relay()
    for k in range(4):
        sum_o.send_core(k)

    def mlp_weight_chunk(i, carry):
        cols = pl.ds(pl.multiple_of(i * CH, CH), CH)
        gu_full[cols] = dot_tn(h2[:, cols], dgu[...]).astype(BF)
        gd_full[i] = dot_tn(ogs[:, cols], act[...]).astype(BF).reshape(4, 64, 384)
        return carry

    lax.fori_loop(0, 4, mlp_weight_chunk, 0)
    weight_u.begin()
    weight_d.begin()

    links.drain(before_h2)
    err = sum_2.total()
    mid = middle[...]
    r_two = lax.rsqrt(jnp.mean(mid * mid, axis=-1, keepdims=True) + EPS)
    normed = mid * r_two
    part = jnp.sum(err * normed, axis=0, keepdims=True)
    gg[...] = jnp.zeros_like(gg)
    for k in range(8):
        gg[8 + k : 9 + k] = part[:, 128 * k : 128 * k + 128]
    scaled = err * gain_two[0:1]
    grad = ogs[own_z].astype(F32) + r_two * (
        scaled - normed * jnp.mean(scaled * normed, axis=-1, keepdims=True)
    )
    grad_mid[...] = grad
    gb[own] = grad.astype(BF)
    before_gb = links.issued()
    gather_gb.begin()
    dk, dv, dqkv = grad_act.at[:, 0:128], grad_act.at[:, 128:256], dgu.at[:, 0:512]
    grad_act[:, 0:256] = jnp.zeros((GROUP, 256), F32)
    gather_gb.sides()
    weight_u.relay()
    weight_d.cross()
    gather_gb.far()
    for k in range(4):
        gather_gb.core(k)
    for k in (2, 1, 3, 0):
        sum_o.cross(k)

    def out_weight_chunk(i, carry):
        cols = pl.ds(pl.multiple_of(i * CH, CH), CH)
        go_full[i] = dot_tn(gb[:, cols], mixed[...]).astype(BF).reshape(4, 64, 256)
        return carry

    def back_rope(turned, pre, gain, cos, sin):
        r = lax.rsqrt(jnp.mean(pre * pre, axis=-1, keepdims=True) + EPS)
        normed = pre * r
        err = turned * cos - pltpu.roll(turned, 64, 1) * sin
        scaled = err * gain
        grad = r * (scaled - normed * jnp.mean(scaled * normed, axis=-1, keepdims=True))
        return grad, jnp.sum(err * normed, axis=0, keepdims=True)

    lax.fori_loop(0, 4, out_weight_chunk, 0)
    weight_o.begin()

    attn_part = jnp.zeros((1, WIDTH), F32)
    p3 = h2
    links.drain(after_h2)
    for qb in (3, 2, 1, 0):
        rows = slice(qb * CH, qb * CH + CH)
        keys = CH * (qb + 1)
        cos, sin = cosine[rows], sine[rows]
        grad_mixed = dot(gb[rows], wo[...].reshape(WIDTH, 256)).astype(BF)
        grad_h = jnp.concatenate([grad_mixed[:, 0:128], grad_mixed[:, 128:256]], axis=0)
        weights = probs_of(qb)[probs_rows(qb), 0:keys]
        wide = weights.astype(F32)
        grad_probs = dot_nt(grad_h, vals[0:keys])
        inner = jnp.sum(wide * grad_probs, axis=-1, keepdims=True)
        grad_scores = (wide * (grad_probs - inner)).astype(BF)
        dk[0:keys] += dot_tn(grad_scores, q_rot[qb * 512 : qb * 512 + 512]) * SCALE
        dv[0:keys] += dot_tn(weights, grad_h)
        grad_q = (dot(grad_scores, k_rot[0:keys]) * SCALE).astype(BF).astype(F32)
        for h in range(2):
            pre = qk_pre[rows, 128 * h : 128 * h + 128]
            grad, gain_part = back_rope(grad_q[CH * h : CH * h + CH], pre, query_gain, cos, sin)
            dqkv[rows, 128 * h : 128 * h + 128] = grad.astype(BF)
            gg[16:17] += gain_part
        grad_k = dk[rows].astype(BF).astype(F32)
        grad, gain_part = back_rope(grad_k, qk_pre[rows, 256:384], key_gain, cos, sin)
        dqkv[rows, 256:384] = grad.astype(BF)
        gg[17:18] += gain_part
        dqkv[rows, 384:512] = dv[rows].astype(BF)
        err = dot_nt(dqkv[rows], wq[...])
        p3[rows] = err.astype(BF)
        send_chunk(sum_3, qb)
        attn_part += jnp.sum(err * (xs[rows].astype(F32) * r1[rows]), axis=0, keepdims=True)
        if qb == 3:
            weight_d.relay()
        if qb == 2:
            sum_o.relay()
            weight_u.spread()
        if qb == 1:
            for k in (2, 1, 3):
                sum_3.cross(k, when=c == 1)
            weight_d.spread()
            weight_o.cross()
            links.drain(before_gb)

    for k in (2, 1, 3):
        sum_3.cross(k, when=c == 0)
    sum_3.cross(0)
    for k in range(8):
        gg[k : k + 1] = attn_part[:, 128 * k : 128 * k + 128]
    out_tmp[...] = (middle[...] + sum_o.total()).astype(BF)
    links.send(out_tmp, out_ref, place.swap, out_id, when=away)
    for dy, dc in column:
        links.send(gg, gg_y.at[y * 2 + c], place.at(dy=dy, dc=dc), gg_y_id + y * 2 + c)

    def attn_weight_chunk(i, carry):
        cols = pl.ds(pl.multiple_of(i * CH, CH), CH)
        grad = dot_tn(h1[:, cols], dqkv[...]).astype(BF)
        gq_full[pl.ds(2 * i, 2)] = grad[:, 0:256].reshape(2, 128, 256)
        gk_full[i] = grad[:, 256:512].reshape(4, 64, 256)
        return carry

    lax.fori_loop(0, 4, attn_weight_chunk, 0)
    weight_k.begin()
    weight_q.begin()
    sum_3.relay()
    weight_o.relay()

    gg_y[y * 2 + c] = gg[...]
    for dy, dc in column:
        index = ((y + dy) % 4) * 2 + (c + dc) % 2
        links.wait(gg_y.at[index], place.at(dy=dy, dc=dc), gg_y_id + index)
    total = gg_y[0]
    for k in range(1, 8):
        total = total + gg_y[k]
    gg_a[...] = total
    for k in range(1, 4):
        links.send(gg_a, gg_x.at[x], place.at(dx=k), gg_x_id + x)
    weight_o.spread()
    weight_u.finish()
    weight_d.finish()
    weight_k.cross()
    weight_q.spread()

    for half in range(2):
        part = pl.ds(64 * half, 64)
        mine = pl.ds(token_rows(c, z, False) + 64 * half, 64)
        err = sum_3.half_total(half)
        r_one = r1[mine]
        normed = xs[mine].astype(F32) * r_one
        scaled = err * gain_one[0:1]
        in_grad_tmp[part] = (
            grad_mid[part]
            + r_one * (scaled - normed * jnp.mean(scaled * normed, axis=-1, keepdims=True))
        ).astype(BF)
        links.send(
            in_grad_tmp.at[part], in_grad_ref.at[part], place.swap, in_grad_id + half, when=away
        )

    gg_x[x] = gg_a[...]
    for k in range(1, 4):
        other = (x + k) % 4
        links.wait(gg_x.at[other], place.at(dx=k), gg_x_id + other)
    gg_b[...] = (gg_x[0] + gg_x[1]) + (gg_x[2] + gg_x[3])
    for k in range(1, 4):
        links.send(gg_b, gg_z.at[z], place.at(dz=k), gg_z_id + z)

    weight_k.spread()
    weight_o.finish()

    @pl.when(home)
    def _():
        out_ref[...] = out_tmp[...]
        in_grad_ref[...] = in_grad_tmp[...]

    gg_z[z] = gg_b[...]
    for k in range(1, 4):
        other = (z + k) % 4
        links.wait(gg_z.at[other], place.at(dz=k), gg_z_id + other)
    gains_ref[...] = (gg_z[0] + gg_z[1]) + (gg_z[2] + gg_z[3])

    weight_q.finish()
    weight_k.finish()
    links.wait(out_ref, place.swap, out_id, when=away)
    for half in range(2):
        part = in_grad_ref.at[pl.ds(64 * half, 64)]
        links.wait(part, place.swap, in_grad_id + half, when=away)
    links.drain(links.issued())


def run_layer(*args):
    vmem = pl.BlockSpec(memory_space=pltpu.VMEM)

    def sds(shape, kind):
        return jax.ShapeDtypeStruct(shape, kind)

    def buf(shape, kind=BF):
        return pltpu.VMEM(shape, kind)

    group = (GROUP, WIDTH)
    table = (GROUP, HEAD)
    block = (TOK, WIDTH)
    landing = [buf(group), buf((4, TOK, WIDTH)), buf((8, 64, WIDTH))]
    gains = (24, 128)

    def weight_landing(cols):
        return [buf((WIDTH, cols)), buf((10, 128, cols)), buf((4, 64, cols))]

    def weight_landing_y(cols):
        return [
            buf((4, 4, 64, cols)),
            buf((4, 4, 2, 64, cols)),
            buf((4, 2, 64, cols)),
            buf((9, 64, cols)),
            buf((64, cols)),
        ]

    scratch = [
        buf((64, NQ)),
        buf((64, NU)),
        buf((4, 64, NO)),
        buf((4, 64, ND)),
        buf((WIDTH, NQ)),
        buf((WIDTH, NU)),
        buf((4, 4, 64, NO)),
        buf((4, 4, 64, ND)),
        buf((16, 8, 128), F32),
        buf((1, WIDTH), F32),
        buf((1, WIDTH), F32),
        buf((1, 4), jnp.int32),
        buf((GROUP, 1), jnp.int32),
        buf(table, F32),
        buf(table, F32),
        buf(group),
        buf(group),
        buf(group),
        buf((GROUP, 1), F32),
        buf((GROUP, 384), F32),
        buf((2 * GROUP, HEAD)),
        buf(table),
        buf(table),
        buf((GROUP, 256)),
        buf((GROUP, 512)),
        buf((GROUP, GROUP)),
        *landing,
        buf(block, F32),
        buf(group),
        buf((GROUP, 384), F32),
        buf((GROUP, 384)),
        buf((GROUP, 768)),
        *landing,
        *landing,
        buf(group),
        buf(block, F32),
        *landing[1:],
        *weight_landing(NU),
        buf((8, 128, 256)),
        *weight_landing(256)[1:],
        *weight_landing_y(NO),
        *weight_landing_y(NO),
        *weight_landing_y(ND),
        buf(block),
        buf(block),
        buf(gains, F32),
        buf((8, *gains), F32),
        buf(gains, F32),
        buf((4, *gains), F32),
        buf(gains, F32),
        buf((4, *gains), F32),
        pltpu.SemaphoreType.DMA((N_SENDS,)),
        pltpu.SemaphoreType.DMA((N_RECVS,)),
    ]
    return pl.pallas_call(
        layer_kernel,
        out_shape=(
            sds(block, BF),
            sds(block, BF),
            sds((64, 256), F32),
            sds((64, 256), F32),
            sds((64, NO), F32),
            sds((64, NU), F32),
            sds((64, ND), F32),
            sds(gains, F32),
        ),
        in_specs=[vmem] * len(args),
        out_specs=(vmem,) * 8,
        scratch_shapes=scratch,
        name="layer",
        compiler_params=pltpu.CompilerParams(
            collective_id=0, has_side_effects=True, vmem_limit_bytes=63 * 2**20
        ),
    )(*args)


def results_kernel(
    out_in,
    in_grad_in,
    gq,
    gk,
    go,
    gu,
    gd,
    gains,
    out,
    in_grad,
    attn_gain,
    query,
    key,
    value,
    query_gain,
    key_gain,
    w_out,
    mlp_gain,
    gate,
    up,
    down,
):
    d = lax.axis_index("dp")
    out[...] = out_in[...]
    in_grad[...] = in_grad_in[...]
    query[...] = gq[...]
    key[...] = gk[:, 0:128]
    value[...] = gk[:, 128:256]
    w_out[...] = go[...]
    gate[...] = gu[:, 0:384]
    up[...] = gu[:, 384:768]
    down[...] = gd[...]
    query_gain[...] = gains[16:17]
    key_gain[...] = gains[17:18]
    for first, ref in ((0, attn_gain), (8, mlp_gain)):
        row = gains[pl.ds(first + d // 2, 1)]
        ref[...] = jnp.where(d % 2 == 1, pltpu.roll(row, 64, 1), row)[:, 0:64]


def write_results(*args):
    vmem = pl.BlockSpec(memory_space=pltpu.VMEM)
    shapes = [
        ((TOK, WIDTH), BF),
        ((TOK, WIDTH), BF),
        ((1, 64), F32),
        ((64, 256), F32),
        ((64, 128), F32),
        ((64, 128), F32),
        ((1, 128), F32),
        ((1, 128), F32),
        ((64, 256), F32),
        ((1, 64), F32),
        ((64, 384), F32),
        ((64, 384), F32),
        ((64, 384), F32),
    ]
    return pl.pallas_call(
        results_kernel,
        out_shape=tuple(jax.ShapeDtypeStruct(shape, kind) for shape, kind in shapes),
        in_specs=[vmem] * len(args),
        out_specs=(vmem,) * len(shapes),
        name="results",
    )(*args)


def per_device(
    layer_input,
    seq_lengths,
    attn_gain,
    w_query,
    key_projection,
    value_projection,
    query_gain,
    key_gain,
    w_out,
    mlp_gain,
    w_gate,
    w_up,
    w_down,
    out_grad,
):
    frequency = ROPE_BASE ** (-(np.arange(HEAD // 2) * 2.0 / HEAD)).astype(np.float32)
    parts = run_layer(
        w_query,
        key_projection,
        value_projection,
        w_out.T,
        w_gate,
        w_up,
        w_down.T,
        attn_gain[None],
        mlp_gain[None],
        layer_input,
        out_grad,
        query_gain[None],
        key_gain[None],
        seq_lengths,
        np.concatenate([frequency, frequency]).astype(np.float32)[None],
    )
    results = list(write_results(*parts))
    for k in (2, 6, 7, 9):
        results[k] = results[k].reshape(-1)
    results[8], results[12] = results[8].T, results[12].T
    return tuple(results)


def solution(mesh):
    both = P(("dp", "tensor"), None)
    split = P("dp", "tensor")
    turned = P("tensor", "dp")
    in_specs = (
        both,
        P("dp", None),
        P("dp"),
        split,
        split,
        split,
        P(),
        P(),
        turned,
        P("dp"),
        split,
        split,
        turned,
        both,
    )
    out_specs = (both, both, P("dp"), split, split, split, P(), P(), turned, P("dp"), split, split, turned)
    return jax.shard_map(
        per_device, mesh=mesh, in_specs=in_specs, out_specs=out_specs, check_vma=False
    )
```
